32 devices in a mesh: grp: 2 (over y), lon: 4 (over z), lat: 2 (over x), dir: 2 (over core).
Axes of the slice: x: 2, y: 2, z: 4, core: 2. Of those that a mesh axis runs over, the one named last changes fastest.
Arguments:
- perturb: float32 [6, 16, 64, 512], P('grp', 'dir', 'lat', 'lon'), parts along dimension 0, may hold values from -6 to 6
- background: float32 [6, 64, 512], P('grp', 'lat', 'lon'), parts along dimension 0, may hold values from -0.3 to 0.3
- land_mask: int32 [64, 512], P('lat', 'lon'), may hold values 0 or 1
- levels: int32 [64, 512], P('lat', 'lon'), may hold values from 1 to 90
- fold_partner: int32 [512], replicated, may hold values from 0 to 511, as said below
Outputs:
- evolved: float32 [6, 16, 64, 512], P('grp', 'dir', 'lat', 'lon'), parts along dimension 0
The draws below stay inside these ranges and needn't reach their ends.
There are 2 independent parts, one for each index of `grp`. The reference program is written for one: setup_inputs(seed, part) draws one part's arguments, and reference() takes and returns one part's arrays. A program takes and returns all parts, laid end to end along the dimension named above; an argument that names none is the same for every part. Nothing has to cross between parts.
Inputs may be any that keep to these rules, and one draw needn't show every extreme that they name: fold_partner[i] = (P - i) mod 512 for one odd P of the draw.
All inputs are finite; a program needn't handle non-finite values. No bound on the sum of `land_mask` on one device may be relied on, other than what follows from the above.
Results may differ from the reference program's by a relative error of at most 0.00002.
Values sent between devices are 32-bit elements; how exact they have to be, the bound alone decides.
No kernel may reach another device: no remote copies, remote signals or barrier semaphores. Data moves between devices by JAX's collectives and lax.ppermute only.
A program may use at most 64 MiB of HBM per device.

```python
import jax
import jax.numpy as jnp

DIRS = 16
SUBCYCLES = 5
NLEV = 90
NLAT = 64
NLON = 512


def draw_fold_partner(key, part):
    key = jax.random.fold_in(key, 7)
    pivot = 2 * jax.random.randint(key, (), 0, NLON // 2) + 1
    return ((pivot - jnp.arange(NLON, dtype=jnp.int32)) % NLON).astype(jnp.int32)


def set_ends(values, rng, least, largest):
    dims = values.shape
    index_at = [jax.random.randint(jax.random.fold_in(rng, axis), (), 0, dims[axis]) for axis in range(len(dims))]
    values = values.at[tuple(index_at)].set(least)
    longest = dims.index(max(dims))
    index_at[longest] = (index_at[longest] + 1) % dims[longest]
    return values.at[tuple(index_at)].set(largest)


def shard_levels(own_key, dims, cuts, smallest, top_value):
    def one(axis_at, shards_of):
        heights = jax.random.uniform(jax.random.fold_in(jax.random.fold_in(own_key, 6), axis_at), (shards_of,), jnp.float32, smallest / len(cuts), top_value / len(cuts))
        return jnp.repeat(jnp.exp(heights), dims[axis_at] // shards_of).reshape((-1,) + (1,) * (len(dims) - axis_at - 1))

    level = one(*cuts[0])
    for cut in cuts[1:]:
        level = level * one(*cut)
    return level


def scatter_about(own_key, extent, width, bound, pieces=(), held_as=jnp.bfloat16):
    drawn = jax.random.normal(own_key, extent, jnp.float32) * width
    if len(pieces) > 0:
        drawn = shard_levels(own_key, extent, pieces, -0.22, 0.18) * drawn
    return jnp.clip(drawn, min=-bound, max=bound).astype(held_as)


def setup_inputs(seed: int = 0, part: int = 0) -> dict:
    key_list = jax.random.split(jax.random.key(seed), 6)
    part_splits = jax.random.split(jax.random.fold_in(key_list[5], part), 6)
    perturb = scatter_about(part_splits[0], (3, DIRS, NLAT, NLON), 1.0, 6.0, ((1, 2), (2, 2), (3, 4)), jnp.float32)
    background = jnp.clip(jax.random.uniform(part_splits[1], (3, NLAT, NLON), jnp.float32, -0.3, 0.3) * shard_levels(part_splits[1], (3, NLAT, NLON), ((1, 2), (2, 4)), -0.4, 0.0), -0.3, 0.3)
    land_mask = set_ends((jax.random.randint(key_list[2], (NLAT, NLON), 0, 5) < 4).astype(jnp.int32), jax.random.fold_in(key_list[2], 1), 0, 1)
    levels = set_ends(jax.random.randint(key_list[3], (NLAT, NLON), 1, NLEV + 1), jax.random.fold_in(key_list[3], 1), 1, NLEV).astype(jnp.int32)
    fold_partner = draw_fold_partner(jax.random.fold_in(key_list[5], 71), part)
    return dict(perturb=perturb, background=background, land_mask=land_mask, levels=levels, fold_partner=fold_partner)


TIME_STEP = 0.35


def extend(fields, signs, partner):
    height = fields.shape[2]
    mirror = jnp.take(fields[:, :, height - 1:, :], partner, axis=3) * signs
    south = jnp.zeros_like(fields[:, :, :1, :])
    grown = jnp.concatenate([south, fields, mirror], axis=2)
    return jnp.concatenate([grown[:, :, :, -1:], grown, grown[:, :, :, :1]], axis=3)


def reference(perturb, background, land_mask, levels, fold_partner):
    wet_cells = land_mask.astype(jnp.float32)
    depth = 0.5 + 1.5 * ((levels - 1).astype(jnp.float32) / (NLEV - 1)) ** 2
    thickness = wet_cells * (depth + background[0])
    coef_signs = jnp.array([1.0, -1.0, -1.0, 1.0], jnp.float32).reshape(4, 1, 1, 1)
    state_signs = jnp.array([1.0, -1.0, -1.0], jnp.float32).reshape(3, 1, 1, 1)
    elev_sign = jnp.ones((1, 1, 1, 1), jnp.float32)
    coeffs = jnp.stack([thickness, background[1], background[2], wet_cells])[:, None]
    wide = extend(coeffs, coef_signs, fold_partner)
    grid_rows = jnp.arange(NLAT, dtype=jnp.float32)
    coriolis = (0.3 + 0.2 * grid_rows / NLAT)[:, None]
    elevation, zonal, meridional = perturb[0], perturb[1], perturb[2]
    for subcycle in range(SUBCYCLES):
        grown = extend(jnp.stack([elevation, zonal, meridional]), state_signs, fold_partner)
        flux_east = wide[0] * grown[1] + grown[0] * wide[1]
        flux_north = wide[0] * grown[2] + grown[0] * wide[2]
        divergence = 0.5 * (flux_east[:, 1:-1, 2:] - flux_east[:, 1:-1, :-2]) + 0.5 * (flux_north[:, 2:, 1:-1] - flux_north[:, :-2, 1:-1])
        elevation = wet_cells * (elevation - TIME_STEP * divergence)
        ext_elev = extend(elevation[None], elev_sign, fold_partner)[0]
        slope_east = 0.5 * (ext_elev[:, 1:-1, 2:] - ext_elev[:, 1:-1, :-2])
        slope_north = 0.5 * (ext_elev[:, 2:, 1:-1] - ext_elev[:, :-2, 1:-1])
        zonal = wet_cells * (zonal + TIME_STEP * (coriolis * meridional - slope_east))
        meridional = wet_cells * (meridional - TIME_STEP * (coriolis * zonal + slope_north))
    return jnp.stack([elevation, zonal, meridional])
```

```python
import functools
from collections import deque

import jax
import jax.numpy as jnp
from jax import lax
from jax.experimental import pallas as pl
from jax.experimental.pallas import tpu as pltpu
from jax.sharding import PartitionSpec as P

SUBCYCLES = 5
NLEV = 90
TIME_STEP = 0.35
HALF_STEP = 0.5 * TIME_STEP

LANES = 128
SUBLANES = 8
HALF = LANES // 2
HALO = 2 * SUBCYCLES
PAIRS = HALO // 2
FIELDS = 4
STATE = 3
COEF = 3
STRIP_SLOTS = HALF // HALO
CORNER_SLOTS = LANES // (2 * HALO)
F32 = jnp.float32


def ceil_div(a, b):
    return -(-a // b)


class Shapes:
    def __init__(self, height):
        self.height = height
        self.ext = height + 2 * HALO
        self.mid = self.ext // 2
        self.fold_first = height
        self.blocks = FIELDS * PAIRS
        self.strip_rows = height // 2
        self.strips = ceil_div(self.strip_rows * FIELDS, STRIP_SLOTS)
        self.side = self.blocks + self.strips
        self.main = STATE * HALO + PAIRS
        self.corners = ceil_div(FIELDS * HALO, CORNER_SLOTS)
        self.band = self.main + self.corners

    def strip(self, k, f):
        slot = (k - HALO) * FIELDS + f
        return self.blocks + slot // STRIP_SLOTS, HALO * (slot % STRIP_SLOTS)

    def corner(self, i, f):
        slot = f * HALO + i
        return self.main + slot // CORNER_SLOTS, 2 * HALO * (slot % CORNER_SLOTS)


def roll(x, shift, axis=1):
    shift = shift % x.shape[axis]
    return x if shift == 0 else pltpu.roll(x, shift, axis)


def lane_ids():
    return lax.broadcasted_iota(jnp.int32, (SUBLANES, LANES), 1)


def sublane_ids():
    return lax.broadcasted_iota(jnp.int32, (SUBLANES, LANES), 0)


def run_staged(tasks, window):
    waiting = deque()

    def advance(task):
        try:
            next(task)
        except StopIteration:
            return
        waiting.append(task)

    for task in tasks:
        advance(task)
        while len(waiting) >= window:
            advance(waiting.popleft())
    while waiting:
        advance(waiting.popleft())


def own_row(x_ref, c_ref, height, f, row):
    if f == COEF:
        return c_ref[row]
    return x_ref[f, pl.ds(row, SUBLANES, stride=height), :]


def pick_pair(even, first, second):
    return jnp.where(even, first, second)


def fold_place(fold_ref, lon_size):
    pivot = fold_ref[0]
    block = pivot // LANES
    rest = pivot - block * LANES
    low = rest < HALF
    place = jnp.where(low, rest + LANES, rest)
    branch = jnp.where(low, block - 1 + lon_size, block)
    return lax.rem(branch, lon_size), place


def sides_kernel(sh, sizes, x_ref, b_ref, m_ref, l_ref, p_ref, a_out, b_out, c_out, q_out):
    lat_size, lon_size = sizes
    height = sh.height
    q_out[0], _ = fold_place(p_ref, lon_size)

    wet = m_ref[...].astype(F32)
    depth = 0.5 + 1.5 * ((l_ref[...] - 1).astype(F32) / (NLEV - 1)) ** 2
    row0 = lax.axis_index("lat") * height
    rows = (row0 + lax.broadcasted_iota(jnp.int32, (height, LANES), 0)).astype(F32)
    coriolis = 0.3 + 0.2 * rows / (height * lat_size)
    planes = (
        HALF_STEP * (wet * (depth + b_ref[0])),
        HALF_STEP * b_ref[1],
        HALF_STEP * b_ref[2],
        wet * (TIME_STEP * coriolis),
    )
    c_out[...] = jnp.zeros_like(c_out)
    for c, plane in enumerate(planes):
        for r in range(height):
            c_out[r, c : c + 1, :] = plane[r : r + 1, :]

    even = jnp.full((SUBLANES, LANES), lax.rem(lax.axis_index("lon"), 2), jnp.int32) == 0
    lane = lane_ids()
    low = lane < HALF
    own = functools.partial(own_row, x_ref, c_out, height)
    top = height - HALO

    def block(f, i):
        a, b = own(f, top + i), own(f, top + i + PAIRS)
        a_up, b_up = roll(a, HALF), roll(b, HALF)
        yield
        east = jnp.where(low, a_up, b)
        west = jnp.where(low, a, b_up)
        v = f * PAIRS + i
        a_out[v] = jnp.where(even, east, west)
        b_out[v] = jnp.where(even, west, east)

    slots = {}
    for k in range(HALO, sh.mid):
        for f in range(FIELDS):
            v, at = sh.strip(k, f)
            slots.setdefault(v, []).append((k, f, at))

    def strips(v):
        parts = []
        for k, f, at in slots[v]:
            a, b = own(f, k - HALO), own(f, sh.ext - 1 - k - HALO)
            beyond = HALF if sh.ext - 1 - k >= sh.fold_first else 0
            parts.append(
                (
                    at,
                    roll(a, at - (LANES - HALO)),
                    roll(b, HALF + at - (LANES - HALO) + beyond),
                    roll(a, at),
                    roll(b, HALF + at - beyond),
                )
            )
        yield
        east = west = jnp.zeros((SUBLANES, LANES), F32)
        for at, ea, eb, wa, wb in parts:
            here = (lane >= at) & (lane < at + HALO)
            there = (lane >= HALF + at) & (lane < HALF + at + HALO)
            east = jnp.where(here, ea, jnp.where(there, eb, east))
            west = jnp.where(here, wa, jnp.where(there, wb, west))
        a_out[v] = jnp.where(even, east, west)
        b_out[v] = jnp.where(even, west, east)

    run_staged([block(f, i) for f in range(FIELDS) for i in range(PAIRS)], 10)
    run_staged([strips(v) for v in sorted(slots)], 2)


def bands_kernel(sh, sizes, x_ref, c_ref, ra_ref, rb_ref, p_ref, *outs):
    lat_size, lon_size = sizes
    height = sh.height
    fold_out, lat_outs = outs[0], outs[1:]
    even = jnp.full((SUBLANES, LANES), lax.rem(lax.axis_index("lon"), 2), jnp.int32) == 0
    lane, sub = lane_ids(), sublane_ids()
    low = lane < HALF
    own = functools.partial(own_row, x_ref, c_ref, height)
    top = height - HALO

    def from_east(v):
        return jnp.where(even, ra_ref[v], rb_ref[v])

    def from_west(v):
        return jnp.where(even, rb_ref[v], ra_ref[v])

    def pair_coefs(a, b):
        return jnp.where(sub < SUBLANES // 2, a, roll(b, SUBLANES // 2, 0))

    corner_items = {}
    for f in range(FIELDS):
        for i in range(HALO):
            v, at = sh.corner(i, f)
            corner_items.setdefault(v, []).append((i, f, at))

    def band(out, first, is_top):
        def main():
            for f in range(STATE):
                for i in range(HALO):
                    out[f * HALO + i] = own(f, first + i)
            for i in range(PAIRS):
                out[STATE * HALO + i] = pair_coefs(
                    own(COEF, first + i), own(COEF, first + i + PAIRS)
                )

        def corners(v):
            parts = []
            for i, f, at in corner_items[v]:
                if is_top:
                    src, h = f * PAIRS + i % PAIRS, HALF * (i // PAIRS)
                    w_at, e_at = h + HALF - HALO, h
                else:
                    src, w_at = sh.strip(HALO + i, f)
                    e_at = w_at
                parts.append(
                    (at, roll(from_west(src), at - w_at), roll(from_east(src), at + HALO - e_at))
                )
            yield
            total = jnp.zeros((SUBLANES, LANES), F32)
            for at, w, e in parts:
                total = jnp.where((lane >= at) & (lane < at + HALO), w, total)
                total = jnp.where((lane >= at + HALO) & (lane < at + 2 * HALO), e, total)
            out[v] = total

        main()
        run_staged([corners(v) for v in sorted(corner_items)], 3)

    lat_even = lax.rem(lax.axis_index("lat"), 2) == 0

    @pl.when(lat_even)
    def _():
        band(lat_outs[0], top, True)
        if lat_size > 2:
            band(lat_outs[1], 0, False)

    @pl.when(jnp.logical_not(lat_even))
    def _():
        band(lat_outs[0], 0, False)
        if lat_size > 2:
            band(lat_outs[1], top, True)

    @pl.when(lax.axis_index("lat") == lat_size - 1)
    def _():
        _, place = fold_place(p_ref, lon_size)
        where_to = jnp.full((SUBLANES, LANES), place, jnp.int32)
        rest = where_to & (LANES - 1)
        eastern = where_to >= LANES
        backwards = (where_to - lane) & (LANES - 1)
        main_own = (eastern & (lane >= rest + 1)) | (jnp.logical_not(eastern) & (lane <= rest))
        upper = (lane >= rest + 1) & (lane <= rest + HALO)
        lower = (lane >= rest + 1 - HALO) & (lane <= rest)
        side_own = (eastern & lower) | (jnp.logical_not(eastern) & upper)
        side_far = (eastern & upper & (lane >= HALF)) | (
            jnp.logical_not(eastern) & lower & (lane < HALF)
        )
        coef_signs = jnp.where((sub == 1) | (sub == 2), -1.0, 1.0).astype(F32)

        def reversed_row(f, i):
            v, h = f * PAIRS + i % PAIRS, i // PAIRS
            w, e = from_west(v), from_east(v)
            if h == 0:
                w = roll(w, HALF)
            else:
                e = roll(e, HALF)
            v, at = sh.strip(sh.ext - 1 - sh.fold_first - i, f)
            far_w = roll(from_west(v), HALF - HALO - HALF - at)
            far_e = roll(from_east(v), -at)
            yield
            both = jnp.where(low, e, w)
            mine = own(f, top + i)
            main = jnp.where(main_own, mine, both)
            side = jnp.where(
                side_own, mine, jnp.where(side_far, jnp.where(low, far_w, far_e), both)
            )
            if f == COEF:
                main, side = main * coef_signs, side * coef_signs
            elif f > 0:
                main, side = -main, -side
            main = jnp.take_along_axis(main, backwards, axis=1)
            side = jnp.take_along_axis(side, backwards, axis=1)
            yield
            j = HALO - 1 - i
            v, at = sh.corner(j, f)
            side = roll(side, at - (LANES - HALO))
            if f < STATE:
                fold_out[f * HALO + j] = main
            elif j < PAIRS:
                v2 = STATE * HALO + j
                fold_out[v2] = jnp.where(sub < SUBLANES // 2, main, fold_out[v2])
            else:
                fold_out[STATE * HALO + j - PAIRS] = roll(main, SUBLANES // 2, 0)
            yield
            here = (lane >= at) & (lane < at + 2 * HALO)
            fold_out[v] = jnp.where(here, side, fold_out[v])

        for v in range(STATE * HALO, sh.band):
            fold_out[v] = jnp.zeros((SUBLANES, LANES), F32)
        run_staged([reversed_row(f, i) for f in range(FIELDS) for i in range(HALO)], 8)


def steps_kernel(sh, sizes, has_second, *refs):
    lat_size, lon_size = sizes
    x_ref, c_ref, ra_ref, rb_ref, fold_ref, lat_a = refs[:6]
    lat_b = refs[6] if has_second else None
    out_ref, main, main_c, edge, edge_c = refs[7 if has_second else 6 :]
    height, ext, mid = sh.height, sh.ext, sh.mid
    even = jnp.full((SUBLANES, LANES), lax.rem(lax.axis_index("lon"), 2), jnp.int32) == 0
    lane, sub = lane_ids(), sublane_ids()
    low = lane < HALF
    own = functools.partial(own_row, x_ref, c_ref, height)

    def from_east(v):
        return jnp.where(even, ra_ref[v], rb_ref[v])

    def from_west(v):
        return jnp.where(even, rb_ref[v], ra_ref[v])

    def put_main(f, r, value):
        if f == COEF:
            main_c[r] = value
        else:
            main[f, r] = value

    def get_main(f, r):
        return main_c[r] if f == COEF else main[f, r]

    def add_edge(f, k, value, mask):
        if f == COEF:
            edge_c[k] = jnp.where(mask, value, edge_c[k])
        else:
            edge[f, k] = jnp.where(mask, value, edge[f, k])

    east0 = HALF // 2
    half_lane = lane & (HALF - 1)
    west_halo = half_lane < HALO
    west_own = (half_lane >= HALO) & (half_lane < 3 * HALO)
    east_own = (half_lane >= east0) & (half_lane < east0 + 2 * HALO)
    east_halo = (half_lane >= east0 + 2 * HALO) & (half_lane < east0 + 3 * HALO)

    def take_band(ref, north):
        def rows(f, i):
            r = (sh.ext - HALO + i) if north else i
            if f < STATE:
                put_main(f, r, ref[f * HALO + i])
            else:
                v = ref[STATE * HALO + i % PAIRS]
                put_main(f, r, v if i < PAIRS else roll(v, SUBLANES // 2, 0))
            v, at = sh.corner(i, f)
            base = HALF if north else 0
            w = roll(ref[v], base - at)
            e = roll(ref[v], base + east0 + HALO - at)
            yield
            k = sh.ext - 1 - r if north else r
            value = jnp.where(half_lane < HALO, w, e)
            if f == COEF:
                edge_c[k, :, base : base + HALF] = value[:, base : base + HALF]
            else:
                edge[f, k, :, base : base + HALF] = value[:, base : base + HALF]

        run_staged([rows(f, i) for f in range(FIELDS) for i in range(HALO)], 10)

    def no_band():
        zero = jnp.zeros((SUBLANES, LANES), F32)
        for f in range(FIELDS):
            for i in range(HALO):
                put_main(f, i, zero)
                if f == COEF:
                    edge_c[i, :, :HALF] = zero[:, :HALF]
                else:
                    edge[f, i, :, :HALF] = zero[:, :HALF]

    lat = lax.axis_index("lat")
    lat_even = lax.rem(lat, 2) == 0
    at_top = lat == lat_size - 1

    @pl.when(at_top)
    def _():
        take_band(fold_ref, True)

    @pl.when(jnp.logical_not(at_top) & lat_even)
    def _():
        take_band(lat_a, True)

    @pl.when(jnp.logical_not(lat_even))
    def _():
        take_band(lat_a, False)

    @pl.when(lat == 0)
    def _():
        no_band()

    if has_second:

        @pl.when(jnp.logical_not(at_top) & jnp.logical_not(lat_even))
        def _():
            take_band(lat_b, True)

        @pl.when((lat > 0) & lat_even)
        def _():
            take_band(lat_b, False)

    for f in range(FIELDS):
        for r in range(height):
            put_main(f, HALO + r, own(f, r))

    def edge_rows(f, k):
        a, b = get_main(f, k), get_main(f, ext - 1 - k)
        aw, ae = roll(a, HALO), roll(a, east0 - (LANES - 2 * HALO))
        bw, be = roll(b, HALF + HALO), roll(b, HALF + east0 - (LANES - 2 * HALO))
        if k >= HALO:
            v, at = sh.strip(k, f)
            w, e = roll(from_west(v), -at), roll(from_east(v), east0 + 2 * HALO - at)
            if ext - 1 - k >= sh.fold_first:
                i = ext - 1 - k - sh.fold_first
                v, h = f * PAIRS + i % PAIRS, HALF * (i // PAIRS)
                w2 = roll(from_west(v), HALF - (h + HALF - HALO))
                e2 = roll(from_east(v), HALF + east0 + 2 * HALO - h)
            else:
                w2 = e2 = None
        yield
        value = jnp.where(east_own, jnp.where(low, ae, be), jnp.where(low, aw, bw))
        if k >= HALO:
            if w2 is not None:
                w, e = jnp.where(low, w, w2), jnp.where(low, e, e2)
            value = jnp.where(west_halo, w, value)
            value = jnp.where(east_halo, e, value)
        else:
            mine = west_own | east_own
            halo = edge_c[k] if f == COEF else edge[f, k]
            value = jnp.where(mine, value, halo)
        if f == COEF:
            edge_c[k] = value
        else:
            edge[f, k] = value

    run_staged([edge_rows(f, k) for f in range(FIELDS) for k in range(mid)], 6)

    north_sign = jnp.where(low, 1.0, -1.0).astype(F32)
    for r in range(ext):
        main_c[r, 4:5, :] = jnp.where(main_c[r, 0:1, :] > 0, 1.0, 0.0).astype(F32)
    for k in range(mid):
        thick = edge_c[k, 0:1, :]
        edge_c[k, 4:5, :] = jnp.where(thick > 0, 1.0, 0.0).astype(F32)
        edge_c[k, 5:6, :] = thick * north_sign[0:1]
        edge_c[k, 2:3, :] = edge_c[k, 2:3, :] * north_sign[0:1]

    def coef(ref, r, c):
        return jnp.broadcast_to(ref[r, c : c + 1, :], (SUBLANES, LANES))

    class Sweep:
        def __init__(self, step, state, coefs, count, mirrored, final):
            self.state, self.coefs, self.count = state, coefs, count
            self.mirrored, self.final = mirrored, final
            self.lo = 2 * step - 1
            self.hi = count if mirrored else count - self.lo
            self.flux_n, self.rolled, self.elev, self.slopes = {}, {}, {}, {}
            self.step_n = HALF_STEP * north_sign if mirrored else HALF_STEP

        def flux(self, r):
            s, c = self.state, self.coefs
            eta, zonal, merid = s[0, r], s[1, r], s[2, r]
            thick = coef(c, r, 0)
            thick_n = coef(c, r, 5) if self.mirrored else thick
            self.flux_n[r] = thick_n * merid + coef(c, r, 2) * eta
            if self.lo <= r < self.hi:
                east = thick * zonal + coef(c, r, 1) * eta
                self.rolled[r] = (roll(east, -1), roll(east, 1))
            if self.mirrored and r == self.count - 1:
                self.flux_n[r + 1] = -roll(self.flux_n[r], HALF)

        def elevation(self, r):
            if not self.lo <= r < self.hi:
                return
            plus, minus = self.rolled.pop(r)
            change = (plus - minus) + (self.flux_n[r + 1] - self.flux_n[r - 1])
            eta = coef(self.coefs, r, 4) * (self.state[0, r] - change)
            self.elev[r] = eta
            if self.velocity_row(r):
                if not self.final:
                    self.state[0, r] = eta
                self.slopes[r] = (roll(eta, -1), roll(eta, 1))
            if self.mirrored and r == self.count - 1:
                self.elev[r + 1] = roll(eta, HALF)

        def velocity_row(self, r):
            return self.lo < r < (self.hi if self.mirrored else self.hi - 1)

        def velocity(self, r):
            if not self.velocity_row(r):
                return
            plus, minus = self.slopes.pop(r)
            wet, turn = coef(self.coefs, r, 4), coef(self.coefs, r, 3)
            zonal, merid = self.state[1, r], self.state[2, r]
            zonal = wet * (zonal - HALF_STEP * (plus - minus)) + turn * merid
            slope = self.step_n * (self.elev[r + 1] - self.elev[r - 1])
            merid = wet * (merid - slope) - turn * zonal
            if self.final:
                self.final(r, (self.elev[r], zonal, merid))
            else:
                self.state[1, r] = zonal
                self.state[2, r] = merid
            self.elev.pop(r - 1)

        def advance(self, t, lag):
            if self.lo - 1 <= t < (self.hi if self.mirrored else self.hi + 1):
                self.flux(t)
            self.elevation(t - lag)
            self.velocity(t - 2 * lag)

    def keep_edge(k, values):
        for f in range(STATE):
            edge[f, k] = values[f]

    pending = deque()

    def emit(limit):
        while len(pending) > limit:
            r, values, moved = pending.popleft()
            for f in range(STATE):
                w, e = moved[f]
                value = jnp.where(lane < HALO, w, jnp.where(lane >= LANES - HALO, e, values[f]))
                out_ref[f, pl.ds(r - HALO, SUBLANES, stride=height), :] = value

    def write_row(r, values):
        k, h = (r, 0) if r < mid else (ext - 1 - r, HALF)
        moved = []
        for f in range(STATE):
            v = edge[f, k]
            moved.append(
                (
                    roll(v, -(h + HALO)),
                    roll(v, LANES - HALO - (h + east0 + HALO)),
                )
            )
        pending.append((r, values, moved))
        emit(3)

    lag = 5
    for step in range(1, SUBCYCLES + 1):
        last = step == SUBCYCLES
        edges = Sweep(step, edge, edge_c, mid, True, keep_edge if last else None)
        rows = Sweep(step, main, main_c, ext, False, write_row if last else None)
        if last:
            for t in range(mid + 2 * lag):
                edges.advance(t, lag)
            for t in range(ext + 2 * lag):
                rows.advance(t, lag)
            emit(0)
        else:
            for t in range(ext + 2 * lag):
                rows.advance(t, lag)
                if t % 2 == 0:
                    edges.advance(t // 2, lag)
            for t in range((ext + 2 * lag + 1) // 2, mid + 2 * lag):
                edges.advance(t, lag)


def pair_swaps(size, wrap):
    first = [(i, i ^ 1) for i in range(size)]
    second = []
    for i in range(size):
        j = i + 1 if i % 2 else i - 1
        if wrap or 0 <= j < size:
            second.append((i, j % size))
    return first, second


def vmem(n):
    return [pl.BlockSpec(memory_space=pltpu.VMEM)] * n


def smem():
    return pl.BlockSpec(memory_space=pltpu.SMEM)


def on_device(mesh_sizes, perturb, background, land_mask, levels, fold_partner):
    lat_size, lon_size = mesh_sizes
    height = perturb.shape[2]
    sh = Shapes(height)
    sizes = (lat_size, lon_size)
    flat = perturb.reshape(STATE, SUBLANES * height, LANES)
    tile = (SUBLANES, LANES)

    def shape(n):
        return jax.ShapeDtypeStruct((n,) + tile, F32)

    params = pltpu.CompilerParams(vmem_limit_bytes=32 * 1024 * 1024)
    side_a, side_b, coefs, branch = pl.pallas_call(
        functools.partial(sides_kernel, sh, sizes),
        out_shape=(
            shape(sh.side),
            shape(sh.side),
            shape(height),
            jax.ShapeDtypeStruct((1,), jnp.int32),
        ),
        in_specs=vmem(4) + [smem()],
        out_specs=tuple(vmem(3)) + (smem(),),
        compiler_params=params,
        name="sides",
    )(flat, background, land_mask, levels, fold_partner)

    lon_first, lon_second = pair_swaps(lon_size, True)
    got_a = lax.ppermute(side_a, "lon", lon_first)
    got_b = lax.ppermute(side_b, "lon", lon_second)

    n_lat = 1 if lat_size == 2 else 2
    bands = pl.pallas_call(
        functools.partial(bands_kernel, sh, sizes),
        out_shape=tuple(shape(sh.band) for _ in range(1 + n_lat)),
        in_specs=vmem(4) + [smem()],
        out_specs=tuple(vmem(1 + n_lat)),
        compiler_params=params,
        name="bands",
    )(flat, coefs, got_a, got_b, fold_partner)

    lat_swaps = pair_swaps(lat_size, False)[:n_lat]
    top = lat_size - 1

    def exchange(q, bands):
        across = []
        for m in range(lon_size):
            j = (q - m) % lon_size
            across.append((m * lat_size + top, j * lat_size + top))
        got = [lax.ppermute(band, "lat", pairs) for band, pairs in zip(bands[1:], lat_swaps)]
        got.insert(0, lax.ppermute(bands[0], ("lon", "lat"), across))
        return tuple(got)

    got = lax.switch(
        branch[0], [functools.partial(exchange, q) for q in range(lon_size)], bands
    )

    out = pl.pallas_call(
        functools.partial(steps_kernel, sh, sizes, n_lat == 2),
        out_shape=jax.ShapeDtypeStruct(flat.shape, F32),
        in_specs=vmem(5 + n_lat),
        out_specs=vmem(1)[0],
        scratch_shapes=[
            pltpu.VMEM((STATE, sh.ext) + tile, F32),
            pltpu.VMEM((sh.ext,) + tile, F32),
            pltpu.VMEM((STATE, sh.mid) + tile, F32),
            pltpu.VMEM((sh.mid,) + tile, F32),
        ],
        compiler_params=params,
        name="subcycles",
    )(flat, coefs, got_a, got_b, *got)
    return out.reshape(perturb.shape)


def solution(mesh):
    placed = (
        P("grp", "dir", "lat", "lon"),
        P("grp", "lat", "lon"),
        P("lat", "lon"),
        P("lat", "lon"),
        P(),
    )
    sizes = (mesh.shape["lat"], mesh.shape["lon"])
    return jax.shard_map(
        functools.partial(on_device, sizes),
        mesh=mesh,
        in_specs=placed,
        out_specs=P("grp", "dir", "lat", "lon"),
        check_vma=False,
    )
```

```python
import functools
from collections import deque

import jax
import jax.numpy as jnp
from jax import lax
from jax.experimental import pallas as pl
from jax.experimental.pallas import tpu as pltpu
from jax.sharding import PartitionSpec as P

SUBCYCLES = 5
NLEV = 90
TIME_STEP = 0.35
HALF_STEP = 0.5 * TIME_STEP

LANES = 128
SUBLANES = 8
HALF = LANES // 2
HALO = 2 * SUBCYCLES
PAIRS = HALO // 2
FIELDS = 4
STATE = 3
COEF = 3
STRIP_SLOTS = HALF // HALO
CORNER_SLOTS = LANES // (2 * HALO)
F32 = jnp.float32


def ceil_div(a, b):
    return -(-a // b)


class Shapes:
    def __init__(self, height):
        self.height = height
        self.ext = height + 2 * HALO
        self.mid = self.ext // 2
        self.fold_first = height
        self.blocks = FIELDS * PAIRS
        self.strip_rows = height // 2
        self.strips = ceil_div(self.strip_rows * FIELDS, STRIP_SLOTS)
        self.side = self.blocks + self.strips
        self.main = STATE * HALO + PAIRS
        self.corners = ceil_div(FIELDS * HALO, CORNER_SLOTS)
        self.band = self.main + self.corners

    def strip(self, k, f):
        slot = (k - HALO) * FIELDS + f
        return self.blocks + slot // STRIP_SLOTS, HALO * (slot % STRIP_SLOTS)

    def corner(self, i, f):
        slot = f * HALO + i
        return self.main + slot // CORNER_SLOTS, 2 * HALO * (slot % CORNER_SLOTS)


def roll(x, shift, axis=1):
    shift = shift % x.shape[axis]
    return x if shift == 0 else pltpu.roll(x, shift, axis)


def lane_ids():
    return lax.broadcasted_iota(jnp.int32, (SUBLANES, LANES), 1)


def sublane_ids():
    return lax.broadcasted_iota(jnp.int32, (SUBLANES, LANES), 0)


def run_staged(tasks, window):
    waiting = deque()

    def advance(task):
        try:
            next(task)
        except StopIteration:
            return
        waiting.append(task)

    for task in tasks:
        advance(task)
        while len(waiting) >= window:
            advance(waiting.popleft())
    while waiting:
        advance(waiting.popleft())


def row(ref, f, r):
    return ref[f, SUBLANES * r : SUBLANES * (r + 1), :]


def put_row(ref, f, r, value):
    ref[f, SUBLANES * r : SUBLANES * (r + 1), :] = value


def coef(ref, r, c):
    return jnp.broadcast_to(ref[SUBLANES * r + c : SUBLANES * r + c + 1, :], (SUBLANES, LANES))


def even_lon():
    return jnp.full((SUBLANES, LANES), lax.rem(lax.axis_index("lon"), 2), jnp.int32) == 0


def fold_place(fold_ref, lon_size):
    pivot = fold_ref[0]
    block = pivot // LANES
    rest = pivot - block * LANES
    low = rest < HALF
    place = jnp.where(low, rest + LANES, rest)
    branch = jnp.where(low, block - 1 + lon_size, block)
    return lax.rem(branch, lon_size), place


def sides_kernel(sh, sizes, x_hbm, b_hbm, m_hbm, l_hbm, p_hbm, *rest):
    a_out, b_out, own_ref, place_out, q_out = rest[:5]
    x_ref, b_ref, m_ref, l_ref, p_ref, sems = rest[5:]
    lat_size, lon_size = sizes
    height = sh.height
    copies = [
        pltpu.make_async_copy(src, dst, sems.at[n])
        for n, (src, dst) in enumerate(
            [(b_hbm, b_ref), (m_hbm, m_ref), (l_hbm, l_ref), (p_hbm, p_ref)]
            + [(x_hbm.at[f], x_ref.at[f]) for f in range(STATE)]
        )
    ]
    for copy in copies:
        copy.start()
    for copy in copies[:4]:
        copy.wait()
    q_out[0], place = fold_place(p_ref, lon_size)
    place_out[...] = jnp.full((SUBLANES, LANES), place, jnp.int32)

    wet = m_ref[...].astype(F32)
    depth = 0.5 + 1.5 * ((l_ref[...] - 1).astype(F32) / (NLEV - 1)) ** 2
    row0 = lax.axis_index("lat") * height
    rows = (row0 + lax.broadcasted_iota(jnp.int32, (height, LANES), 0)).astype(F32)
    coriolis = 0.3 + 0.2 * rows / (height * lat_size)
    planes = [
        HALF_STEP * (wet * (depth + b_ref[0])),
        HALF_STEP * b_ref[1],
        HALF_STEP * b_ref[2],
        wet * (TIME_STEP * coriolis),
        wet,
    ]
    planes += [jnp.zeros_like(wet)] * (SUBLANES - len(planes))
    for c, plane in enumerate(planes):
        for r in range(0, height, SUBLANES):
            own_ref[COEF, pl.ds(SUBLANES * r + c, SUBLANES, stride=SUBLANES), :] = plane[
                r : r + SUBLANES
            ]
    for copy in copies[4:]:
        copy.wait()
    for f in range(STATE):
        for r in range(height):
            put_row(own_ref, f, r, x_ref[f, pl.ds(r, SUBLANES, stride=height), :])

    even = even_lon()
    lane = lane_ids()
    low = lane < HALF
    own = functools.partial(row, own_ref)
    top = height - HALO

    def block(f, i):
        a, b = own(f, top + i), own(f, top + i + PAIRS)
        a_up, b_up = roll(a, HALF), roll(b, HALF)
        yield
        east = jnp.where(low, a_up, b)
        west = jnp.where(low, a, b_up)
        v = f * PAIRS + i
        a_out[v] = jnp.where(even, east, west)
        b_out[v] = jnp.where(even, west, east)

    slots = {}
    for k in range(HALO, sh.mid):
        for f in range(FIELDS):
            v, at = sh.strip(k, f)
            slots.setdefault(v, []).append((k, f, at))

    def strips(v):
        parts = []
        for k, f, at in slots[v]:
            a, b = own(f, k - HALO), own(f, sh.ext - 1 - k - HALO)
            beyond = HALF if sh.ext - 1 - k >= sh.fold_first else 0
            parts.append(
                (
                    at,
                    roll(a, at - (LANES - HALO)),
                    roll(b, HALF + at - (LANES - HALO) + beyond),
                    roll(a, at),
                    roll(b, HALF + at - beyond),
                )
            )
        yield
        east = west = jnp.zeros((SUBLANES, LANES), F32)
        for at, ea, eb, wa, wb in parts:
            here = (lane >= at) & (lane < at + HALO)
            there = (lane >= HALF + at) & (lane < HALF + at + HALO)
            east = jnp.where(here, ea, jnp.where(there, eb, east))
            west = jnp.where(here, wa, jnp.where(there, wb, west))
        a_out[v] = jnp.where(even, east, west)
        b_out[v] = jnp.where(even, west, east)

    run_staged([block(f, i) for f in range(FIELDS) for i in range(PAIRS)], 10)
    run_staged([strips(v) for v in sorted(slots)], 2)


def bands_kernel(sh, sizes, own_ref, ra_ref, rb_ref, place_ref, *outs):
    lat_size, _ = sizes
    height = sh.height
    fold_out, lat_outs = outs[0], outs[1:]
    even = even_lon()
    lane, sub = lane_ids(), sublane_ids()
    low = lane < HALF
    own = functools.partial(row, own_ref)
    top = height - HALO

    def from_east(v):
        return jnp.where(even, ra_ref[v], rb_ref[v])

    def from_west(v):
        return jnp.where(even, rb_ref[v], ra_ref[v])

    def pair_coefs(a, b):
        return jnp.where(sub < SUBLANES // 2, a, roll(b, SUBLANES // 2, 0))

    corner_items = {}
    for f in range(FIELDS):
        for i in range(HALO):
            v, at = sh.corner(i, f)
            corner_items.setdefault(v, []).append((i, f, at))

    def band(out, first, is_top):
        def main():
            for f in range(STATE):
                for i in range(HALO):
                    out[f * HALO + i] = own(f, first + i)
            for i in range(PAIRS):
                out[STATE * HALO + i] = pair_coefs(
                    own(COEF, first + i), own(COEF, first + i + PAIRS)
                )

        def corners(v):
            parts = []
            for i, f, at in corner_items[v]:
                if is_top:
                    src, h = f * PAIRS + i % PAIRS, HALF * (i // PAIRS)
                    w_at, e_at = h + HALF - HALO, h
                else:
                    src, w_at = sh.strip(HALO + i, f)
                    e_at = w_at
                parts.append(
                    (at, roll(from_west(src), at - w_at), roll(from_east(src), at + HALO - e_at))
                )
            yield
            total = jnp.zeros((SUBLANES, LANES), F32)
            for at, w, e in parts:
                total = jnp.where((lane >= at) & (lane < at + HALO), w, total)
                total = jnp.where((lane >= at + HALO) & (lane < at + 2 * HALO), e, total)
            out[v] = total

        main()
        run_staged([corners(v) for v in sorted(corner_items)], 3)

    lat_even = lax.rem(lax.axis_index("lat"), 2) == 0

    @pl.when(lat_even)
    def _():
        band(lat_outs[0], top, True)
        if lat_size > 2:
            band(lat_outs[1], 0, False)

    @pl.when(jnp.logical_not(lat_even))
    def _():
        band(lat_outs[0], 0, False)
        if lat_size > 2:
            band(lat_outs[1], top, True)

    @pl.when(lax.axis_index("lat") == lat_size - 1)
    def _():
        where_to = place_ref[...]
        rest = where_to & (LANES - 1)
        eastern = where_to >= LANES
        backwards = (where_to - lane) & (LANES - 1)
        main_own = (eastern & (lane >= rest + 1)) | (jnp.logical_not(eastern) & (lane <= rest))
        upper = (lane >= rest + 1) & (lane <= rest + HALO)
        lower = (lane >= rest + 1 - HALO) & (lane <= rest)
        side_own = (eastern & lower) | (jnp.logical_not(eastern) & upper)
        side_far = (eastern & upper & (lane >= HALF)) | (
            jnp.logical_not(eastern) & lower & (lane < HALF)
        )
        coef_signs = jnp.where((sub == 1) | (sub == 2), -1.0, 1.0).astype(F32)

        def reversed_row(f, i):
            v, h = f * PAIRS + i % PAIRS, i // PAIRS
            w, e = from_west(v), from_east(v)
            if h == 0:
                w = roll(w, HALF)
            else:
                e = roll(e, HALF)
            v, at = sh.strip(sh.ext - 1 - sh.fold_first - i, f)
            far_w = roll(from_west(v), HALF - HALO - HALF - at)
            far_e = roll(from_east(v), -at)
            yield
            both = jnp.where(low, e, w)
            mine = own(f, top + i)
            main = jnp.where(main_own, mine, both)
            side = jnp.where(
                side_own, mine, jnp.where(side_far, jnp.where(low, far_w, far_e), both)
            )
            if f == COEF:
                main, side = main * coef_signs, side * coef_signs
            elif f > 0:
                main, side = -main, -side
            main = jnp.take_along_axis(main, backwards, axis=1)
            side = jnp.take_along_axis(side, backwards, axis=1)
            yield
            j = HALO - 1 - i
            v, at = sh.corner(j, f)
            side = roll(side, at - (LANES - HALO))
            if f < STATE:
                fold_out[f * HALO + j] = main
            elif j < PAIRS:
                v2 = STATE * HALO + j
                fold_out[v2] = jnp.where(sub < SUBLANES // 2, main, fold_out[v2])
            else:
                fold_out[STATE * HALO + j - PAIRS] = roll(main, SUBLANES // 2, 0)
            yield
            here = (lane >= at) & (lane < at + 2 * HALO)
            fold_out[v] = jnp.where(here, side, fold_out[v])

        for v in range(STATE * HALO, sh.band):
            fold_out[v] = jnp.zeros((SUBLANES, LANES), F32)
        run_staged([reversed_row(f, i) for f in range(FIELDS) for i in range(HALO)], 8)


EAST0 = HALF // 2
LAG = 4
WET, NORTH_THICK = 4, 5


def north_sign():
    return jnp.where(lane_ids() < HALF, 1.0, -1.0).astype(F32)


class Sweep:
    def __init__(self, elev, vel, old, coef, put, known=None, mirror=None):
        self.elev_rows, self.vel_rows = elev, vel
        self.old, self.coef, self.put, self.known, self.mirror = old, coef, put, known, mirror
        self.flux_n, self.rolled, self.new, self.slopes = {}, {}, {}, {}
        self.sign = HALF_STEP * north_sign() if mirror is not None else HALF_STEP
        self.first = min(elev[0] - 1, vel[0])
        self.last = (max(elev[1] + 1, vel[1]) if mirror is None else mirror) + 2 * LAG

    def flux(self, r):
        lo, hi = self.elev_rows
        if not lo - 1 <= r <= hi or r == self.mirror:
            return
        eta, merid = self.old(0, r), self.old(2, r)
        thick = self.coef(r, 0)
        thick_n = thick if self.mirror is None else self.coef(r, NORTH_THICK)
        self.flux_n[r] = thick_n * merid + self.coef(r, 2) * eta
        if lo <= r < hi:
            east = thick * self.old(1, r) + self.coef(r, 1) * eta
            self.rolled[r] = (roll(east, -1), roll(east, 1))
        if self.mirror is not None and r == self.mirror - 1:
            self.flux_n[r + 1] = -roll(self.flux_n[r], HALF)

    def elevation(self, r):
        lo, hi = self.elev_rows
        if not lo <= r < hi:
            return
        plus, minus = self.rolled.pop(r)
        change = (plus - minus) + (self.flux_n[r + 1] - self.flux_n[r - 1])
        eta = self.coef(r, WET) * (self.old(0, r) - change)
        self.new[r] = eta
        self.put(0, r, eta)
        if self.mirror is not None and r == self.mirror - 1:
            self.new[r + 1] = roll(eta, HALF)

    def get_new(self, r):
        if r not in self.new:
            self.new[r] = self.known(r)
            if self.vel_rows[0] <= r < self.vel_rows[1]:
                self.put(0, r, self.new[r])
        return self.new[r]

    def slope(self, r):
        if self.vel_rows[0] <= r < self.vel_rows[1]:
            eta = self.get_new(r)
            self.slopes[r] = (roll(eta, -1), roll(eta, 1))

    def velocity(self, r):
        if not self.vel_rows[0] <= r < self.vel_rows[1]:
            return
        plus, minus = self.slopes.pop(r)
        wet, turn = self.coef(r, WET), self.coef(r, 3)
        zonal, merid = self.old(1, r), self.old(2, r)
        zonal = wet * (zonal - HALF_STEP * (plus - minus)) + turn * merid
        slope = self.sign * (self.get_new(r + 1) - self.get_new(r - 1))
        merid = wet * (merid - slope) - turn * zonal
        self.put(1, r, zonal)
        self.put(2, r, merid)

    def advance(self, t):
        self.flux(t)
        self.elevation(t - LAG)
        self.slope(t - LAG)
        self.velocity(t - 2 * LAG)


def run_sweeps(sweeps):
    for t in range(max(s.last - s.first for s in sweeps) + 1):
        for s in sweeps:
            s.advance(s.first + t)


def middle_kernel(sh, own_ref, hist_ref):
    for step in range(1, SUBCYCLES + 1):
        before, after = hist_ref.at[max(step - 2, 0)], hist_ref.at[step - 1]
        source = own_ref if step == 1 else before

        def put(f, r, value, after=after):
            put_row(after, f, r, value)

        run_sweeps(
            [
                Sweep(
                    (2 * step - 1, sh.height - 2 * step + 1),
                    (2 * step, sh.height - 2 * step),
                    functools.partial(row, source),
                    functools.partial(coef, own_ref.at[COEF]),
                    put,
                )
            ]
        )


def edges_kernel(sh, own_ref, ra_ref, rb_ref, start_ref, coef_ref, hist_ref):
    even = even_lon()
    lane = lane_ids()
    low = lane < HALF
    half_lane = lane & (HALF - 1)
    west_halo = half_lane < HALO
    east_own = (half_lane >= EAST0) & (half_lane < EAST0 + 2 * HALO)
    east_halo = (half_lane >= EAST0 + 2 * HALO) & (half_lane < EAST0 + 3 * HALO)
    sign = north_sign()

    def from_east(v):
        return jnp.where(even, ra_ref[v], rb_ref[v])

    def from_west(v):
        return jnp.where(even, rb_ref[v], ra_ref[v])

    def edge_row(f, k):
        own = own_columns(row(own_ref, f, k - HALO), row(own_ref, f, sh.ext - 1 - k - HALO))
        v, at = sh.strip(k, f)
        w, e = roll(from_west(v), -at), roll(from_east(v), EAST0 + 2 * HALO - at)
        i = sh.ext - 1 - k - sh.fold_first
        if i >= 0:
            v, h = f * PAIRS + i % PAIRS, HALF * (i // PAIRS)
            w2 = roll(from_west(v), HALF - (h + HALF - HALO))
            e2 = roll(from_east(v), HALF + EAST0 + 2 * HALO - h)
        yield
        value = merge_own(own, low, east_own)
        if i >= 0:
            w, e = jnp.where(low, w, w2), jnp.where(low, e, e2)
        value = jnp.where(west_halo, w, jnp.where(east_halo, e, value))
        if f == COEF:
            put_edge_coefs(coef_ref, k - HALO, value, sign)
        else:
            put_row(start_ref, f, k - HALO, value)

    run_staged([edge_row(f, k) for k in range(HALO, sh.mid) for f in range(FIELDS)], 4)

    rows = sh.mid - HALO
    for step in range(1, SUBCYCLES + 1):
        source = start_ref if step == 1 else hist_ref.at[step - 2]
        after = hist_ref.at[step - 1]

        def put(f, r, value, after=after):
            put_row(after, f, r, value)

        run_sweeps(
            [
                Sweep(
                    (2 * step - 1, rows),
                    (2 * step, rows),
                    functools.partial(row, source),
                    functools.partial(coef, coef_ref),
                    put,
                    mirror=rows,
                )
            ]
        )


def own_columns(a, b):
    east = EAST0 - (LANES - 2 * HALO)
    return roll(a, HALO), roll(a, east), roll(b, HALF + HALO), roll(b, HALF + east)


def merge_own(parts, low, east_own):
    aw, ae, bw, be = parts
    return jnp.where(east_own, jnp.where(low, ae, be), jnp.where(low, aw, bw))


def put_edge_coefs(ref, k, value, sign):
    at = SUBLANES * k
    thick = value[0:1]
    ref[at : at + 2, :] = value[0:2]
    ref[at + 2 : at + 3, :] = value[2:3] * sign[0:1]
    ref[at + 3 : at + 4, :] = value[3:4]
    ref[at + WET : at + WET + 1, :] = jnp.where(thick > 0, 1.0, 0.0).astype(F32)
    ref[at + NORTH_THICK : at + NORTH_THICK + 1, :] = thick * sign[0:1]


def last_kernel(sh, sizes, n_lat, *refs):
    lat_size, _ = sizes
    own_ref, hist_ref, start_ref, ecoef_ref, ehist_ref, fold_ref = refs[:6]
    lat_refs = refs[6 : 6 + n_lat]
    out_ref, main, main_c, edge, edge_c = refs[6 + n_lat :]
    height, ext, mid = sh.height, sh.ext, sh.mid
    lane = lane_ids()
    low = lane < HALF
    half_lane = lane & (HALF - 1)
    east_own = (half_lane >= EAST0) & (half_lane < EAST0 + 2 * HALO)
    halo = (half_lane < HALO) | (
        (half_lane >= EAST0 + 2 * HALO) & (half_lane < EAST0 + 3 * HALO)
    )
    sign = north_sign()
    span = 2 * HALO

    def south_or_north(r):
        return r if r < span else r - (ext - span) + span

    def take_band(ref, north):
        def band_row(f, i):
            r = ext - HALO + i if north else i
            k = ext - 1 - r if north else r
            base = HALF if north else 0
            if f < STATE:
                put_row(main, f, south_or_north(r), ref[f * HALO + i])
            else:
                v = ref[STATE * HALO + i % PAIRS]
                v = v if i < PAIRS else roll(v, SUBLANES // 2, 0)
                at = SUBLANES * south_or_north(r)
                main_c[at : at + SUBLANES, :] = v
                main_c[at + WET : at + WET + 1, :] = jnp.where(v[0:1] > 0, 1.0, 0.0).astype(F32)
            v, at = sh.corner(i, f)
            w = roll(ref[v], base - at)
            e = roll(ref[v], base + EAST0 + HALO - at)
            yield
            value = jnp.where(half_lane < HALO, w, e)
            edge[f, SUBLANES * k : SUBLANES * (k + 1), base : base + HALF] = value[
                :, base : base + HALF
            ]

        run_staged([band_row(f, i) for f in range(FIELDS) for i in range(HALO)], 10)

    def no_band():
        zero = jnp.zeros((SUBLANES, LANES), F32)
        for i in range(HALO):
            for f in range(FIELDS):
                edge[f, SUBLANES * i : SUBLANES * (i + 1), :HALF] = zero[:, :HALF]
                if f < STATE:
                    put_row(main, f, i, zero)
            main_c[SUBLANES * i : SUBLANES * (i + 1), :] = zero

    lat = lax.axis_index("lat")
    lat_even = lax.rem(lat, 2) == 0
    at_top = lat == lat_size - 1

    @pl.when(at_top)
    def _():
        take_band(fold_ref, True)

    @pl.when(jnp.logical_not(at_top) & lat_even)
    def _():
        take_band(lat_refs[0], True)

    @pl.when(jnp.logical_not(lat_even))
    def _():
        take_band(lat_refs[0], False)

    @pl.when(lat == 0)
    def _():
        no_band()

    if n_lat == 2:

        @pl.when(jnp.logical_not(at_top) & jnp.logical_not(lat_even))
        def _():
            take_band(lat_refs[1], True)

        @pl.when((lat > 0) & lat_even)
        def _():
            take_band(lat_refs[1], False)

    def main_row(f, r):
        if f == COEF:
            at = SUBLANES * south_or_north(r)
            return main_c[at : at + SUBLANES, :]
        return row(main, f, south_or_north(r))

    def edge_row(f, k):
        own = own_columns(main_row(f, k), main_row(f, ext - 1 - k))
        yield
        value = jnp.where(halo, row(edge, f, k), merge_own(own, low, east_own))
        if f == COEF:
            put_edge_coefs(edge_c, k, value, sign)
        else:
            put_row(edge, f, k, value)

    run_staged([edge_row(f, k) for k in range(HALO) for f in range(FIELDS)], 8)

    def put_edge(f, k, value):
        put_row(edge, f, k, value)

    def edge_coef(k, c):
        return coef(edge_c, k, c) if k < HALO else coef(ecoef_ref, k - HALO, c)

    def main_coef(r, c):
        if HALO <= r < ext - HALO:
            return coef(own_ref.at[COEF], r - HALO, c)
        return coef(main_c, south_or_north(r), c)

    def put_main(f, r, value):
        put_row(main, f, south_or_north(r), value)

    for step in range(1, SUBCYCLES + 1):
        source = own_ref if step == 1 else hist_ref.at[step - 2]
        e_source = start_ref if step == 1 else ehist_ref.at[step - 2]
        first, ready = 2 * step - 2, 2 * step + HALO - 2

        def old_main(f, r, source=source, ready=ready):
            if ready <= r < ext - ready:
                return row(source, f, r - HALO)
            return main_row(f, r)

        def old_edge(f, k, e_source=e_source, ready=ready):
            return row(e_source, f, k - HALO) if k >= ready else row(edge, f, k)

        after, e_after = hist_ref.at[step - 1], ehist_ref.at[step - 1]

        def known_main(r, after=after):
            return row(after, 0, r - HALO)

        def known_edge(k, e_after=e_after):
            return row(e_after, 0, k - HALO)

        elev, vel = (first + 1, ready + 1), (first + 2, ready + 2)

        def flip(rows):
            return ext - rows[1], ext - rows[0]

        run_sweeps(
            [
                Sweep(elev, vel, old_edge, edge_coef, put_edge, known_edge, mirror=mid),
                Sweep(elev, vel, old_main, main_coef, put_main, known_main),
                Sweep(flip(elev), flip(vel), old_main, main_coef, put_main, known_main),
            ]
        )

    ready = 2 * HALO
    final, e_final = hist_ref.at[SUBCYCLES - 1], ehist_ref.at[SUBCYCLES - 1]

    def output_row(f, r):
        k, h = (r, 0) if r < mid else (ext - 1 - r, HALF)
        v = row(edge, f, k) if k < ready else row(e_final, f, k - HALO)
        w, e = roll(v, -(h + HALO)), roll(v, LANES - HALO - (h + EAST0 + HALO))
        yield
        inner = ready <= r < ext - ready
        v = row(final, f, r - HALO) if inner else main_row(f, r)
        v = jnp.where(lane < HALO, w, jnp.where(lane >= LANES - HALO, e, v))
        out_ref[f, pl.ds(r - HALO, SUBLANES, stride=height), :] = v

    run_staged([output_row(f, r) for f in range(STATE) for r in range(HALO, ext - HALO)], 10)


def pair_swaps(size, wrap):
    first = [(i, i ^ 1) for i in range(size)]
    second = []
    for i in range(size):
        j = i + 1 if i % 2 else i - 1
        if wrap or 0 <= j < size:
            second.append((i, j % size))
    return first, second


def vmem(n):
    return [pl.BlockSpec(memory_space=pltpu.VMEM)] * n


def in_hbm(x):
    return pltpu.with_memory_space_constraint(x, pltpu.HBM)


def smem():
    return pl.BlockSpec(memory_space=pltpu.SMEM)


def on_device(mesh_sizes, perturb, background, land_mask, levels, fold_partner):
    lat_size, lon_size = mesh_sizes
    height = perturb.shape[2]
    sh = Shapes(height)
    sizes = (lat_size, lon_size)
    flat = perturb.reshape(STATE, SUBLANES * height, LANES)
    tile = (SUBLANES, LANES)

    def shape(n):
        return jax.ShapeDtypeStruct((n,) + tile, F32)

    params = pltpu.CompilerParams(vmem_limit_bytes=16 * 1024 * 1024)
    rows = SUBLANES * height
    side_a, side_b, own, place, branch = pl.pallas_call(
        functools.partial(sides_kernel, sh, sizes),
        out_shape=(
            shape(sh.side),
            shape(sh.side),
            jax.ShapeDtypeStruct((FIELDS, rows, LANES), F32),
            jax.ShapeDtypeStruct(tile, jnp.int32),
            jax.ShapeDtypeStruct((1,), jnp.int32),
        ),
        in_specs=[pl.BlockSpec(memory_space=pltpu.HBM)] * 5,
        out_specs=tuple(vmem(4)) + (smem(),),
        scratch_shapes=[
            pltpu.VMEM(flat.shape, F32),
            pltpu.VMEM(background.shape, F32),
            pltpu.VMEM(land_mask.shape, jnp.int32),
            pltpu.VMEM(levels.shape, jnp.int32),
            pltpu.SMEM(fold_partner.shape, jnp.int32),
            pltpu.SemaphoreType.DMA((4 + STATE,)),
        ],
        compiler_params=params,
        name="sides",
    )(*[in_hbm(v) for v in (flat, background, land_mask, levels, fold_partner)])

    lon_first, lon_second = pair_swaps(lon_size, True)
    got_a = lax.ppermute(side_a, "lon", lon_first)
    got_b = lax.ppermute(side_b, "lon", lon_second)
    hist = pl.pallas_call(
        functools.partial(middle_kernel, sh),
        out_shape=jax.ShapeDtypeStruct((SUBCYCLES, STATE, rows, LANES), F32),
        in_specs=vmem(1),
        out_specs=vmem(1)[0],
        compiler_params=params,
        name="middle",
    )(own)

    n_lat = 1 if lat_size == 2 else 2
    bands = pl.pallas_call(
        functools.partial(bands_kernel, sh, sizes),
        out_shape=tuple(shape(sh.band) for _ in range(1 + n_lat)),
        in_specs=vmem(4),
        out_specs=tuple(vmem(1 + n_lat)),
        compiler_params=params,
        name="bands",
    )(own, got_a, got_b, place)

    lat_swaps = pair_swaps(lat_size, False)[:n_lat]
    top = lat_size - 1
    edge_rows = SUBLANES * (sh.mid - HALO)

    def exchange(q, own, got_a, got_b, bands):
        across = []
        for m in range(lon_size):
            j = (q - m) % lon_size
            across.append((m * lat_size + top, j * lat_size + top))
        got = [lax.ppermute(band, "lat", pairs) for band, pairs in zip(bands[1:], lat_swaps)]
        got.insert(0, lax.ppermute(bands[0], ("lon", "lat"), across))
        edges = pl.pallas_call(
            functools.partial(edges_kernel, sh),
            out_shape=(
                jax.ShapeDtypeStruct((STATE, edge_rows, LANES), F32),
                jax.ShapeDtypeStruct((edge_rows, LANES), F32),
                jax.ShapeDtypeStruct((SUBCYCLES, STATE, edge_rows, LANES), F32),
            ),
            in_specs=vmem(3),
            out_specs=tuple(vmem(3)),
            compiler_params=params,
            name="edges",
        )(own, got_a, got_b)
        return tuple(edges) + tuple(got)

    got = lax.switch(
        branch[0],
        [functools.partial(exchange, q) for q in range(lon_size)],
        own,
        got_a,
        got_b,
        bands,
    )

    out = pl.pallas_call(
        functools.partial(last_kernel, sh, sizes, n_lat),
        out_shape=jax.ShapeDtypeStruct(flat.shape, F32),
        in_specs=vmem(6 + n_lat),
        out_specs=vmem(1)[0],
        scratch_shapes=[
            pltpu.VMEM((STATE, 4 * HALO * SUBLANES, LANES), F32),
            pltpu.VMEM((4 * HALO * SUBLANES, LANES), F32),
            pltpu.VMEM((FIELDS, SUBLANES * sh.mid, LANES), F32),
            pltpu.VMEM((SUBLANES * HALO, LANES), F32),
        ],
        compiler_params=params,
        name="last",
    )(own, hist, *got)
    return out.reshape(perturb.shape)


def solution(mesh):
    placed = (
        P("grp", "dir", "lat", "lon"),
        P("grp", "lat", "lon"),
        P("lat", "lon"),
        P("lat", "lon"),
        P(),
    )
    sizes = (mesh.shape["lat"], mesh.shape["lon"])
    return jax.shard_map(
        functools.partial(on_device, sizes),
        mesh=mesh,
        in_specs=placed,
        out_specs=P("grp", "dir", "lat", "lon"),
        check_vma=False,
    )
```

```python
import functools
from collections import deque

import jax
import jax.numpy as jnp
from jax import lax
from jax.experimental import pallas as pl
from jax.experimental.pallas import tpu as pltpu
from jax.sharding import PartitionSpec as P

SUBCYCLES = 5
NLEV = 90
TIME_STEP = 0.35
HALF_STEP = 0.5 * TIME_STEP

LANES = 128
SUBLANES = 8
HALF = LANES // 2
HALO = 2 * SUBCYCLES
PAIRS = HALO // 2
FIELDS = 4
STATE = 3
COEF = 3
STRIP_SLOTS = HALF // HALO
CORNER_SLOTS = LANES // (2 * HALO)
F32 = jnp.float32


def ceil_div(a, b):
    return -(-a // b)


class Shapes:
    def __init__(self, height):
        self.height = height
        self.ext = height + 2 * HALO
        self.mid = self.ext // 2
        self.fold_first = height
        self.blocks = FIELDS * PAIRS
        self.strip_rows = height // 2
        self.strips = ceil_div(self.strip_rows * FIELDS, STRIP_SLOTS)
        self.side = self.blocks + self.strips
        self.main = STATE * HALO + PAIRS
        self.corners = ceil_div(FIELDS * HALO, CORNER_SLOTS)
        self.band = self.main + self.corners

    def strip(self, k, f):
        slot = (k - HALO) * FIELDS + f
        return self.blocks + slot // STRIP_SLOTS, HALO * (slot % STRIP_SLOTS)

    def corner(self, i, f):
        slot = f * HALO + i
        return self.main + slot // CORNER_SLOTS, 2 * HALO * (slot % CORNER_SLOTS)


def by_register(items, where):
    groups = {}
    for i, f in items:
        v, at = where(i, f)
        groups.setdefault(v, []).append((i, f, at))
    return groups


def roll(x, shift, axis=1):
    shift = shift % x.shape[axis]
    return x if shift == 0 else pltpu.roll(x, shift, axis)


def lane_ids():
    return lax.broadcasted_iota(jnp.int32, (SUBLANES, LANES), 1)


def sublane_ids():
    return lax.broadcasted_iota(jnp.int32, (SUBLANES, LANES), 0)


def run_staged(tasks, window):
    waiting = deque()

    def advance(task):
        try:
            next(task)
        except StopIteration:
            return
        waiting.append(task)

    for task in tasks:
        advance(task)
        while len(waiting) >= window:
            advance(waiting.popleft())
    while waiting:
        advance(waiting.popleft())


def row(ref, f, r):
    return ref[f, SUBLANES * r : SUBLANES * (r + 1), :]


def put_row(ref, f, r, value):
    ref[f, SUBLANES * r : SUBLANES * (r + 1), :] = value


def coef(ref, r, c):
    return jnp.broadcast_to(ref[SUBLANES * r + c : SUBLANES * r + c + 1, :], (SUBLANES, LANES))


def even_lon():
    return jnp.full((SUBLANES, LANES), lax.rem(lax.axis_index("lon"), 2), jnp.int32) == 0


def fold_place(fold_ref, lon_size):
    pivot = fold_ref[0]
    block = pivot // LANES
    rest = pivot - block * LANES
    low = rest < HALF
    place = jnp.where(low, rest + LANES, rest)
    branch = jnp.where(low, block - 1 + lon_size, block)
    return lax.rem(branch, lon_size), place


def pair_coefs(a, b):
    return jnp.where(sublane_ids() < SUBLANES // 2, a, roll(b, SUBLANES // 2, 0))


def sides_kernel(sh, sizes, x_hbm, b_hbm, m_hbm, l_hbm, p_hbm, *rest):
    a_out, b_out, own_ref, place_out, q_out = rest[:5]
    lat_outs, (x_ref, b_ref, m_ref, l_ref, p_ref, sems) = rest[5:-6], rest[-6:]
    lat_size, lon_size = sizes
    height = sh.height
    copies = [
        pltpu.make_async_copy(src, dst, sems.at[n])
        for n, (src, dst) in enumerate(
            [(b_hbm, b_ref), (m_hbm, m_ref), (l_hbm, l_ref), (p_hbm, p_ref)]
            + [(x_hbm.at[f], x_ref.at[f]) for f in range(STATE)]
        )
    ]
    for copy in copies:
        copy.start()
    for copy in copies[:4]:
        copy.wait()
    q_out[0], place = fold_place(p_ref, lon_size)
    place_out[...] = jnp.full((SUBLANES, LANES), place, jnp.int32)

    wet = m_ref[...].astype(F32)
    depth = 0.5 + 1.5 * ((l_ref[...] - 1).astype(F32) / (NLEV - 1)) ** 2
    row0 = lax.axis_index("lat") * height
    rows = (row0 + lax.broadcasted_iota(jnp.int32, (height, LANES), 0)).astype(F32)
    coriolis = 0.3 + 0.2 * rows / (height * lat_size)
    planes = [
        HALF_STEP * (wet * (depth + b_ref[0])),
        HALF_STEP * b_ref[1],
        HALF_STEP * b_ref[2],
        wet * (TIME_STEP * coriolis),
        wet,
    ]
    planes += [jnp.zeros_like(wet)] * (SUBLANES - len(planes))
    for c, plane in enumerate(planes):
        for r in range(0, height, SUBLANES):
            own_ref[COEF, pl.ds(SUBLANES * r + c, SUBLANES, stride=SUBLANES), :] = plane[
                r : r + SUBLANES
            ]
    for copy in copies[4:]:
        copy.wait()
    for f in range(STATE):
        for r in range(height):
            put_row(own_ref, f, r, x_ref[f, pl.ds(r, SUBLANES, stride=height), :])

    even = even_lon()
    lane = lane_ids()
    low = lane < HALF
    own = functools.partial(row, own_ref)
    top = height - HALO

    def block(f, i):
        a, b = own(f, top + i), own(f, top + i + PAIRS)
        a_up, b_up = roll(a, HALF), roll(b, HALF)
        yield
        east = jnp.where(low, a_up, b)
        west = jnp.where(low, a, b_up)
        v = f * PAIRS + i
        a_out[v] = jnp.where(even, east, west)
        b_out[v] = jnp.where(even, west, east)

    slots = {}
    for k in range(HALO, sh.mid):
        for f in range(FIELDS):
            v, at = sh.strip(k, f)
            slots.setdefault(v, []).append((k, f, at))

    def strips(v):
        parts = []
        for k, f, at in slots[v]:
            a, b = own(f, k - HALO), own(f, sh.ext - 1 - k - HALO)
            beyond = HALF if sh.ext - 1 - k >= sh.fold_first else 0
            parts.append(
                (
                    at,
                    roll(a, at - (LANES - HALO)),
                    roll(b, HALF + at - (LANES - HALO) + beyond),
                    roll(a, at),
                    roll(b, HALF + at - beyond),
                )
            )
        yield
        east = west = jnp.zeros((SUBLANES, LANES), F32)
        for at, ea, eb, wa, wb in parts:
            here = (lane >= at) & (lane < at + HALO)
            there = (lane >= HALF + at) & (lane < HALF + at + HALO)
            east = jnp.where(here, ea, jnp.where(there, eb, east))
            west = jnp.where(here, wa, jnp.where(there, wb, west))
        a_out[v] = jnp.where(even, east, west)
        b_out[v] = jnp.where(even, west, east)

    run_staged([block(f, i) for f in range(FIELDS) for i in range(PAIRS)], 10)
    run_staged([strips(v) for v in sorted(slots)], 2)

    def raw_rows(out, first):
        for f in range(STATE):
            for i in range(HALO):
                out[f * HALO + i] = own(f, first + i)
        for i in range(PAIRS):
            out[STATE * HALO + i] = pair_coefs(
                own(COEF, first + i), own(COEF, first + i + PAIRS)
            )

    lat_even = lax.rem(lax.axis_index("lat"), 2) == 0

    @pl.when(lat_even)
    def _():
        raw_rows(lat_outs[0], top)
        if len(lat_outs) > 1:
            raw_rows(lat_outs[1], 0)

    @pl.when(jnp.logical_not(lat_even))
    def _():
        raw_rows(lat_outs[0], 0)
        if len(lat_outs) > 1:
            raw_rows(lat_outs[1], top)


def bands_kernel(sh, sizes, own_ref, ra_ref, rb_ref, place_ref, fold_out, *lat_outs):
    lat_size, _ = sizes
    even = even_lon()
    lane, sub = lane_ids(), sublane_ids()
    low = lane < HALF
    own = functools.partial(row, own_ref)
    top = sh.height - HALO

    def from_east(v):
        return jnp.where(even, ra_ref[v], rb_ref[v])

    def from_west(v):
        return jnp.where(even, rb_ref[v], ra_ref[v])

    def corners(out, is_top):
        def register(v, items):
            parts = []
            for i, f, at in items:
                if is_top:
                    src, h = f * PAIRS + i % PAIRS, HALF * (i // PAIRS)
                    w_at, e_at = h + HALF - HALO, h
                else:
                    src, w_at = sh.strip(HALO + i, f)
                    e_at = w_at
                parts.append(
                    (at, roll(from_west(src), at - w_at), roll(from_east(src), at + HALO - e_at))
                )
            yield
            total = jnp.zeros((SUBLANES, LANES), F32)
            for at, w, e in parts:
                total = jnp.where((lane >= at) & (lane < at + HALO), w, total)
                total = jnp.where((lane >= at + HALO) & (lane < at + 2 * HALO), e, total)
            out[v - sh.main] = total

        groups = by_register([(i, f) for f in range(FIELDS) for i in range(HALO)], sh.corner)
        run_staged([register(v, items) for v, items in groups.items()], 3)

    lat_even = lax.rem(lax.axis_index("lat"), 2) == 0

    @pl.when(lat_even)
    def _():
        corners(lat_outs[0], True)
        if len(lat_outs) > 1:
            corners(lat_outs[1], False)

    @pl.when(jnp.logical_not(lat_even))
    def _():
        corners(lat_outs[0], False)
        if len(lat_outs) > 1:
            corners(lat_outs[1], True)

    @pl.when(lax.axis_index("lat") == lat_size - 1)
    def _():
        where_to = place_ref[...]
        rest = where_to & (LANES - 1)
        eastern = where_to >= LANES
        backwards = (where_to - lane) & (LANES - 1)
        main_own = (eastern & (lane >= rest + 1)) | (jnp.logical_not(eastern) & (lane <= rest))
        upper = (lane >= rest + 1) & (lane <= rest + HALO)
        lower = (lane >= rest + 1 - HALO) & (lane <= rest)
        side_own = (eastern & lower) | (jnp.logical_not(eastern) & upper)
        side_far = (eastern & upper & (lane >= HALF)) | (
            jnp.logical_not(eastern) & lower & (lane < HALF)
        )
        coef_signs = jnp.where((sub == 1) | (sub == 2), -1.0, 1.0).astype(F32)

        def reversed_row(f, i):
            v, h = f * PAIRS + i % PAIRS, i // PAIRS
            w, e = from_west(v), from_east(v)
            if h == 0:
                w = roll(w, HALF)
            else:
                e = roll(e, HALF)
            v, at = sh.strip(sh.ext - 1 - sh.fold_first - i, f)
            far_w = roll(from_west(v), HALF - HALO - HALF - at)
            far_e = roll(from_east(v), -at)
            yield
            both = jnp.where(low, e, w)
            mine = own(f, top + i)
            main = jnp.where(main_own, mine, both)
            side = jnp.where(
                side_own, mine, jnp.where(side_far, jnp.where(low, far_w, far_e), both)
            )
            if f == COEF:
                main, side = main * coef_signs, side * coef_signs
            elif f > 0:
                main, side = -main, -side
            main = jnp.take_along_axis(main, backwards, axis=1)
            side = jnp.take_along_axis(side, backwards, axis=1)
            yield
            j = HALO - 1 - i
            v, at = sh.corner(j, f)
            side = roll(side, at - (LANES - HALO))
            if f < STATE:
                fold_out[f * HALO + j] = main
            elif j < PAIRS:
                v2 = STATE * HALO + j
                fold_out[v2] = jnp.where(sub < SUBLANES // 2, main, fold_out[v2])
            else:
                fold_out[STATE * HALO + j - PAIRS] = roll(main, SUBLANES // 2, 0)
            yield
            here = (lane >= at) & (lane < at + 2 * HALO)
            fold_out[v] = jnp.where(here, side, fold_out[v])

        for v in range(STATE * HALO, sh.band):
            fold_out[v] = jnp.zeros((SUBLANES, LANES), F32)
        run_staged([reversed_row(f, i) for f in range(FIELDS) for i in range(HALO)], 8)


EAST0 = HALF // 2
LAG = 4
WET, NORTH_THICK = 4, 5


def north_sign():
    return jnp.where(lane_ids() < HALF, 1.0, -1.0).astype(F32)


class Sweep:
    def __init__(self, elev, vel, old, coef, put, known=None, mirror=None):
        self.elev_rows, self.vel_rows = elev, vel
        self.old, self.coef, self.put, self.known, self.mirror = old, coef, put, known, mirror
        self.flux_n, self.rolled, self.new, self.slopes = {}, {}, {}, {}
        self.sign = HALF_STEP * north_sign() if mirror is not None else HALF_STEP
        self.first = min(elev[0] - 1, vel[0])
        self.last = (max(elev[1] + 1, vel[1]) if mirror is None else mirror) + 2 * LAG

    def flux(self, r):
        lo, hi = self.elev_rows
        if not lo - 1 <= r <= hi or r == self.mirror:
            return
        eta, merid = self.old(0, r), self.old(2, r)
        thick = self.coef(r, 0)
        thick_n = thick if self.mirror is None else self.coef(r, NORTH_THICK)
        self.flux_n[r] = thick_n * merid + self.coef(r, 2) * eta
        if lo <= r < hi:
            east = thick * self.old(1, r) + self.coef(r, 1) * eta
            self.rolled[r] = (roll(east, -1), roll(east, 1))
        if self.mirror is not None and r == self.mirror - 1:
            self.flux_n[r + 1] = -roll(self.flux_n[r], HALF)

    def elevation(self, r):
        lo, hi = self.elev_rows
        if not lo <= r < hi:
            return
        plus, minus = self.rolled.pop(r)
        change = (plus - minus) + (self.flux_n[r + 1] - self.flux_n[r - 1])
        eta = self.coef(r, WET) * (self.old(0, r) - change)
        self.new[r] = eta
        self.put(0, r, eta)
        if self.mirror is not None and r == self.mirror - 1:
            self.new[r + 1] = roll(eta, HALF)

    def get_new(self, r):
        if r not in self.new:
            self.new[r] = self.known(r)
            if self.vel_rows[0] <= r < self.vel_rows[1]:
                self.put(0, r, self.new[r])
        return self.new[r]

    def slope(self, r):
        if self.vel_rows[0] <= r < self.vel_rows[1]:
            eta = self.get_new(r)
            self.slopes[r] = (roll(eta, -1), roll(eta, 1))

    def velocity(self, r):
        if not self.vel_rows[0] <= r < self.vel_rows[1]:
            return
        plus, minus = self.slopes.pop(r)
        wet, turn = self.coef(r, WET), self.coef(r, 3)
        zonal, merid = self.old(1, r), self.old(2, r)
        zonal = wet * (zonal - HALF_STEP * (plus - minus)) + turn * merid
        slope = self.sign * (self.get_new(r + 1) - self.get_new(r - 1))
        merid = wet * (merid - slope) - turn * zonal
        self.put(1, r, zonal)
        self.put(2, r, merid)

    def advance(self, t):
        self.flux(t)
        self.elevation(t - LAG)
        self.slope(t - LAG)
        self.velocity(t - 2 * LAG)


def run_sweeps(sweeps):
    for t in range(max(s.last - s.first for s in sweeps) + 1):
        for s in sweeps:
            s.advance(s.first + t)


def middle_kernel(sh, own_ref, hist_ref):
    for step in range(1, SUBCYCLES + 1):
        before, after = hist_ref.at[max(step - 2, 0)], hist_ref.at[step - 1]
        source = own_ref if step == 1 else before

        def put(f, r, value, after=after):
            put_row(after, f, r, value)

        run_sweeps(
            [
                Sweep(
                    (2 * step - 1, sh.height - 2 * step + 1),
                    (2 * step, sh.height - 2 * step),
                    functools.partial(row, source),
                    functools.partial(coef, own_ref.at[COEF]),
                    put,
                )
            ]
        )


def edges_kernel(sh, own_ref, ra_ref, rb_ref, start_ref, coef_ref, hist_ref):
    even = even_lon()
    lane = lane_ids()
    low = lane < HALF
    half_lane = lane & (HALF - 1)
    west_halo = half_lane < HALO
    east_own = (half_lane >= EAST0) & (half_lane < EAST0 + 2 * HALO)
    east_halo = (half_lane >= EAST0 + 2 * HALO) & (half_lane < EAST0 + 3 * HALO)
    sign = north_sign()

    def from_east(v):
        return jnp.where(even, ra_ref[v], rb_ref[v])

    def from_west(v):
        return jnp.where(even, rb_ref[v], ra_ref[v])

    def edge_row(f, k):
        own = own_columns(row(own_ref, f, k - HALO), row(own_ref, f, sh.ext - 1 - k - HALO))
        v, at = sh.strip(k, f)
        w, e = roll(from_west(v), -at), roll(from_east(v), EAST0 + 2 * HALO - at)
        i = sh.ext - 1 - k - sh.fold_first
        if i >= 0:
            v, h = f * PAIRS + i % PAIRS, HALF * (i // PAIRS)
            w2 = roll(from_west(v), HALF - (h + HALF - HALO))
            e2 = roll(from_east(v), HALF + EAST0 + 2 * HALO - h)
        yield
        value = merge_own(own, low, east_own)
        if i >= 0:
            w, e = jnp.where(low, w, w2), jnp.where(low, e, e2)
        value = jnp.where(west_halo, w, jnp.where(east_halo, e, value))
        if f == COEF:
            put_edge_coefs(coef_ref, k - HALO, value, sign)
        else:
            put_row(start_ref, f, k - HALO, value)

    run_staged([edge_row(f, k) for k in range(HALO, sh.mid) for f in range(FIELDS)], 4)

    rows = sh.mid - HALO
    for step in range(1, SUBCYCLES + 1):
        source = start_ref if step == 1 else hist_ref.at[step - 2]
        after = hist_ref.at[step - 1]

        def put(f, r, value, after=after):
            put_row(after, f, r, value)

        run_sweeps(
            [
                Sweep(
                    (2 * step - 1, rows),
                    (2 * step, rows),
                    functools.partial(row, source),
                    functools.partial(coef, coef_ref),
                    put,
                    mirror=rows,
                )
            ]
        )


def own_columns(a, b):
    east = EAST0 - (LANES - 2 * HALO)
    return roll(a, HALO), roll(a, east), roll(b, HALF + HALO), roll(b, HALF + east)


def merge_own(parts, low, east_own):
    aw, ae, bw, be = parts
    return jnp.where(east_own, jnp.where(low, ae, be), jnp.where(low, aw, bw))


def put_edge_coefs(ref, k, value, sign):
    at = SUBLANES * k
    thick = value[0:1]
    ref[at : at + 2, :] = value[0:2]
    ref[at + 2 : at + 3, :] = value[2:3] * sign[0:1]
    ref[at + 3 : at + 4, :] = value[3:4]
    ref[at + WET : at + WET + 1, :] = jnp.where(thick > 0, 1.0, 0.0).astype(F32)
    ref[at + NORTH_THICK : at + NORTH_THICK + 1, :] = thick * sign[0:1]


class Wedges:
    def __init__(self, sh, own_ref, hist_ref, start_ref, ecoef_ref, ehist_ref, buffers):
        self.sh, self.own, self.hist = sh, own_ref, hist_ref
        self.start, self.ecoef, self.ehist = start_ref, ecoef_ref, ehist_ref
        self.main, self.main_c, self.edge, self.edge_c = buffers
        lane = lane_ids()
        self.low = lane < HALF
        self.half_lane = half = lane & (HALF - 1)
        self.east_own = (half >= EAST0) & (half < EAST0 + 2 * HALO)
        self.halo = (half < HALO) | ((half >= EAST0 + 2 * HALO) & (half < EAST0 + 3 * HALO))
        self.sign = north_sign()

    SHAPES = (
        (STATE, 4 * HALO * SUBLANES, LANES),
        (4 * HALO * SUBLANES, LANES),
        (FIELDS, 2 * HALO * SUBLANES, LANES),
        (HALO * SUBLANES, LANES),
    )

    def at(self, r):
        span = 2 * HALO
        return r if r < span else r - (self.sh.ext - span) + span

    def main_row(self, f, r):
        if f == COEF:
            at = SUBLANES * self.at(r)
            return self.main_c[at : at + SUBLANES, :]
        return row(self.main, f, self.at(r))

    def put_main(self, f, r, value):
        if f < STATE:
            put_row(self.main, f, self.at(r), value)
            return
        at = SUBLANES * self.at(r)
        self.main_c[at : at + SUBLANES, :] = value
        self.main_c[at + WET : at + WET + 1, :] = jnp.where(value[0:1] > 0, 1.0, 0.0).astype(F32)

    def put_halo(self, f, r, value):
        north = r >= self.sh.mid
        k, base = (self.sh.ext - 1 - r, HALF) if north else (r, 0)
        self.edge[f, SUBLANES * k : SUBLANES * (k + 1), base : base + HALF] = value[
            :, base : base + HALF
        ]

    def take_band(self, ref, corners, north):
        base = HALF if north else 0

        def band_row(f, i):
            r = self.sh.ext - HALO + i if north else i
            if f < STATE:
                value = ref[f * HALO + i]
            else:
                value = ref[STATE * HALO + i % PAIRS]
                value = value if i < PAIRS else roll(value, SUBLANES // 2, 0)
            v, at = self.sh.corner(i, f)
            v = corners[v - self.sh.main]
            w, e = roll(v, base - at), roll(v, base + EAST0 + HALO - at)
            yield
            self.put_main(f, r, value)
            self.put_halo(f, r, jnp.where(self.half_lane < HALO, w, e))

        run_staged([band_row(f, i) for f in range(FIELDS) for i in range(HALO)], 10)

    def no_band(self, north):
        zero = jnp.zeros((SUBLANES, LANES), F32)
        for f in range(FIELDS):
            for i in range(HALO):
                r = self.sh.ext - HALO + i if north else i
                self.put_main(f, r, zero)
                self.put_halo(f, r, zero)

    def edge_rows(self, north_only=False):
        def edge_row(f, k):
            b = self.main_row(f, self.sh.ext - 1 - k)
            parts = own_columns(b if north_only else self.main_row(f, k), b)
            yield
            value = jnp.where(
                self.halo, row(self.edge, f, k), merge_own(parts, self.low, self.east_own)
            )
            if f == COEF:
                put_edge_coefs(self.edge_c, k, value, self.sign)
            else:
                put_row(self.edge, f, k, value)

        run_staged([edge_row(f, k) for k in range(HALO) for f in range(FIELDS)], 8)

    def steps(self, sides):
        ext = self.sh.ext

        def put_edge(f, k, value):
            put_row(self.edge, f, k, value)

        def edge_coef(k, c):
            return coef(self.edge_c, k, c) if k < HALO else coef(self.ecoef, k - HALO, c)

        def main_coef(r, c):
            if HALO <= r < ext - HALO:
                return coef(self.own.at[COEF], r - HALO, c)
            return coef(self.main_c, self.at(r), c)

        for step in range(1, SUBCYCLES + 1):
            source = self.own if step == 1 else self.hist.at[step - 2]
            e_source = self.start if step == 1 else self.ehist.at[step - 2]
            after, e_after = self.hist.at[step - 1], self.ehist.at[step - 1]
            first, ready = 2 * step - 2, 2 * step + HALO - 2

            def old_main(f, r, source=source, ready=ready):
                if ready <= r < ext - ready:
                    return row(source, f, r - HALO)
                return self.main_row(f, r)

            def old_edge(f, k, e_source=e_source, ready=ready):
                return row(e_source, f, k - HALO) if k >= ready else row(self.edge, f, k)

            def known_main(r, after=after):
                return row(after, 0, r - HALO)

            def known_edge(k, e_after=e_after):
                return row(e_after, 0, k - HALO)

            elev, vel = (first + 1, ready + 1), (first + 2, ready + 2)
            sweeps = [
                Sweep(elev, vel, old_edge, edge_coef, put_edge, known_edge, mirror=self.sh.mid)
            ]
            if "south" in sides:
                sweeps.append(Sweep(elev, vel, old_main, main_coef, self.put_main, known_main))
            if "north" in sides:
                elev, vel = [(ext - rows[1], ext - rows[0]) for rows in (elev, vel)]
                sweeps.append(Sweep(elev, vel, old_main, main_coef, self.put_main, known_main))
            run_sweeps(sweeps)

    def output(self, first, last, put):
        ext, mid, ready = self.sh.ext, self.sh.mid, 2 * HALO
        final, e_final = self.hist.at[SUBCYCLES - 1], self.ehist.at[SUBCYCLES - 1]
        lane = lane_ids()

        def output_row(f, r):
            k, h = (r, 0) if r < mid else (ext - 1 - r, HALF)
            v = row(self.edge, f, k) if k < ready else row(e_final, f, k - HALO)
            w, e = roll(v, -(h + HALO)), roll(v, LANES - HALO - (h + EAST0 + HALO))
            yield
            inner = ready <= r < ext - ready
            v = row(final, f, r - HALO) if inner else self.main_row(f, r)
            v = jnp.where(lane < HALO, w, jnp.where(lane >= LANES - HALO, e, v))
            put(f, r - HALO, v)

        run_staged([output_row(f, r) for f in range(STATE) for r in range(first, last)], 10)


def wedge_kernel(sh, sizes, n_lat, *refs):
    lat_size, _ = sizes
    bands, refs = [(refs[n], refs[n_lat + n]) for n in range(n_lat)], refs[2 * n_lat :]
    state, (out_ref, order_out), kept, buffers = refs[:5], refs[5:7], refs[7:10], refs[10:]
    wedges = Wedges(sh, *state, buffers)
    order_out[...] = jnp.zeros((SUBLANES, LANES), F32)
    for source, target in zip(state[2:], kept):
        target[...] = source[...]

    def take(band, north):
        wedges.take_band(*band, north)

    lat = lax.axis_index("lat")
    lat_even = lax.rem(lat, 2) == 0
    lat_odd = jnp.logical_not(lat_even)
    at_top = lat == lat_size - 1

    @pl.when(at_top)
    def _():
        wedges.no_band(True)

    @pl.when(lat == 0)
    def _():
        wedges.no_band(False)

    @pl.when(lat_even)
    def _():
        take(bands[0], True)

    @pl.when(lat_odd)
    def _():
        take(bands[0], False)

    if n_lat == 2:

        @pl.when(lat_odd & jnp.logical_not(at_top))
        def _():
            take(bands[1], True)

        @pl.when(lat_even & (lat > 0))
        def _():
            take(bands[1], False)

    wedges.edge_rows()
    wedges.steps(("south", "north"))

    def put(f, r, value):
        out_ref[f, pl.ds(r, SUBLANES, stride=sh.height), :] = value

    wedges.output(HALO, sh.ext - HALO, put)


def north_kernel(sh, sizes, fold_ref, order_ref, *buffers):
    @pl.when(lax.axis_index("lat") == sizes[0] - 1)
    def _():
        wedges = Wedges(sh, None, None, None, None, None, buffers)
        wedges.no_band(False)
        wedges.take_band(fold_ref, fold_ref.at[sh.main :], True)
        wedges.edge_rows(north_only=True)


def last_kernel(sh, sizes, *refs):
    lat_size, _ = sizes
    done_ref, state, begin = refs[0], refs[1:6], refs[6:10]
    out_hbm, late_ref, sems, main, edge = refs[10:]
    height, ext = sh.height, sh.ext
    split = (height - HALO) // SUBLANES * SUBLANES
    at_top = lax.axis_index("lat") == lat_size - 1
    lines = [
        [pl.ds(d * height + start, size) for d in range(SUBLANES)]
        for start, size in ((0, split), (split, height - split))
    ]

    def copies(source, part):
        return [
            pltpu.make_async_copy(
                source.at[f, line], out_hbm.at[f, line], sems.at[part, f, d]
            )
            for f in range(STATE)
            for d, line in enumerate(lines[part])
        ]

    early = copies(done_ref, 0)
    for copy in early:
        copy.start()

    @pl.when(jnp.logical_not(at_top))
    def _():
        rest = copies(done_ref, 1)
        for copy in rest:
            copy.start()
        for copy in rest:
            copy.wait()

    @pl.when(at_top)
    def _():
        wedges = Wedges(sh, *state, (main, begin[1], edge, begin[3]))
        for f in range(STATE):
            for k in range(HALO):
                put_row(edge, f, k, row(begin[2], f, k))
                at = wedges.at(ext - 1 - k)
                put_row(main, f, at, row(begin[0], f, at))
        wedges.steps(("north",))

        def put(f, r, value):
            late_ref[f, pl.ds(r, SUBLANES, stride=height), :] = value

        for f in range(STATE):
            for r in range(split, height - HALO):
                put(f, r, done_ref[f, pl.ds(r, SUBLANES, stride=height), :])
        wedges.output(ext - 2 * HALO, ext - HALO, put)
        rest = copies(late_ref, 1)
        for copy in rest:
            copy.start()
        for copy in rest:
            copy.wait()

    for copy in early:
        copy.wait()


def pair_swaps(size, wrap):
    first = [(i, i ^ 1) for i in range(size)]
    second = []
    for i in range(size):
        j = i + 1 if i % 2 else i - 1
        if wrap or 0 <= j < size:
            second.append((i, j % size))
    return first, second


def vmem(n):
    return [pl.BlockSpec(memory_space=pltpu.VMEM)] * n


def in_hbm(x):
    return pltpu.with_memory_space_constraint(x, pltpu.HBM)


def smem():
    return pl.BlockSpec(memory_space=pltpu.SMEM)


def on_device(mesh_sizes, perturb, background, land_mask, levels, fold_partner):
    lat_size, lon_size = mesh_sizes
    height = perturb.shape[2]
    sh = Shapes(height)
    sizes = (lat_size, lon_size)
    flat = perturb.reshape(STATE, SUBLANES * height, LANES)
    tile = (SUBLANES, LANES)

    def shape(n):
        return pltpu.VMEM((n,) + tile, F32)

    params = pltpu.CompilerParams(vmem_limit_bytes=16 * 1024 * 1024)
    rows = SUBLANES * height
    n_lat = 1 if lat_size == 2 else 2
    side_a, side_b, own, place, branch, *lat_rows = pl.pallas_call(
        functools.partial(sides_kernel, sh, sizes),
        out_shape=(
            shape(sh.side),
            shape(sh.side),
            pltpu.VMEM((FIELDS, rows, LANES), F32),
            pltpu.VMEM(tile, jnp.int32),
            jax.ShapeDtypeStruct((1,), jnp.int32),
        )
        + (shape(sh.main),) * n_lat,
        in_specs=[pl.BlockSpec(memory_space=pltpu.HBM)] * 5,
        out_specs=tuple(vmem(4)) + (smem(),) + tuple(vmem(n_lat)),
        scratch_shapes=[
            pltpu.VMEM(flat.shape, F32),
            pltpu.VMEM(background.shape, F32),
            pltpu.VMEM(land_mask.shape, jnp.int32),
            pltpu.VMEM(levels.shape, jnp.int32),
            pltpu.SMEM(fold_partner.shape, jnp.int32),
            pltpu.SemaphoreType.DMA((4 + STATE,)),
        ],
        compiler_params=params,
        name="sides",
    )(*[in_hbm(v) for v in (flat, background, land_mask, levels, fold_partner)])

    got_a, got_b = [
        lax.ppermute(x, "lon", swap)
        for x, swap in zip((side_a, side_b), pair_swaps(lon_size, True))
    ]
    lat_swaps = pair_swaps(lat_size, False)[:n_lat]
    got_lat = [lax.ppermute(x, "lat", swap) for x, swap in zip(lat_rows, lat_swaps)]
    hist = pl.pallas_call(
        functools.partial(middle_kernel, sh),
        out_shape=pltpu.VMEM((SUBCYCLES, STATE, rows, LANES), F32),
        in_specs=vmem(1),
        out_specs=vmem(1)[0],
        compiler_params=params,
        name="middle",
    )(own)
    fold_band, *lat_corners = pl.pallas_call(
        functools.partial(bands_kernel, sh, sizes),
        out_shape=(shape(sh.band),) + (shape(sh.corners),) * n_lat,
        in_specs=vmem(4),
        out_specs=tuple(vmem(1 + n_lat)),
        compiler_params=params,
        name="bands",
    )(own, got_a, got_b, place)

    edge_rows = SUBLANES * (sh.mid - HALO)
    edge_shapes = (
        pltpu.VMEM((STATE, edge_rows, LANES), F32),
        pltpu.VMEM((edge_rows, LANES), F32),
        pltpu.VMEM((SUBCYCLES, STATE, edge_rows, LANES), F32),
    )
    step_edges = jax.jit(
        pl.pallas_call(
            functools.partial(edges_kernel, sh),
            out_shape=edge_shapes,
            in_specs=vmem(3),
            out_specs=tuple(vmem(3)),
            compiler_params=params,
            name="edges",
        )
    )
    step_wedges = jax.jit(
        pl.pallas_call(
            functools.partial(wedge_kernel, sh, sizes, n_lat),
            out_shape=(pltpu.VMEM(flat.shape, F32), pltpu.VMEM(tile, F32)) + edge_shapes,
            in_specs=vmem(2 * n_lat + 5),
            out_specs=tuple(vmem(5)),
            scratch_shapes=[pltpu.VMEM(x, F32) for x in Wedges.SHAPES],
            compiler_params=params,
            name="wedges",
        )
    )
    take_north = jax.jit(
        pl.pallas_call(
            functools.partial(north_kernel, sh, sizes),
            out_shape=tuple(pltpu.VMEM(x, F32) for x in Wedges.SHAPES),
            in_specs=vmem(2),
            out_specs=tuple(vmem(4)),
            compiler_params=params,
            name="north",
        )
    )
    top = lat_size - 1

    def rest(q, fold_band, lat_corners, got_lat, own, hist, got_a, got_b):
        across = []
        for m in range(lon_size):
            j = (q - m) % lon_size
            across.append((m * lat_size + top, j * lat_size + top))
        got_fold = lax.ppermute(fold_band, ("lon", "lat"), across)
        got_corners = [lax.ppermute(x, "lat", swap) for x, swap in zip(lat_corners, lat_swaps)]
        edges = step_edges(own, got_a, got_b)
        done, order, *kept = step_wedges(*got_lat, *got_corners, own, hist, *edges)
        return kept, done, take_north(got_fold, order)

    edges, done, beyond = lax.switch(
        branch[0],
        [functools.partial(rest, q) for q in range(lon_size)],
        fold_band,
        lat_corners,
        got_lat,
        own,
        hist,
        got_a,
        got_b,
    )
    out = pl.pallas_call(
        functools.partial(last_kernel, sh, sizes),
        out_shape=jax.ShapeDtypeStruct(flat.shape, F32),
        in_specs=vmem(10),
        out_specs=pl.BlockSpec(memory_space=pltpu.HBM),
        scratch_shapes=[
            pltpu.VMEM(flat.shape, F32),
            pltpu.SemaphoreType.DMA((2, STATE, SUBLANES)),
            pltpu.VMEM(Wedges.SHAPES[0], F32),
            pltpu.VMEM(Wedges.SHAPES[2], F32),
        ],
        compiler_params=params,
        name="last",
    )(done, own, hist, *edges, *beyond)
    return out.reshape(perturb.shape)


def solution(mesh):
    placed = (
        P("grp", "dir", "lat", "lon"),
        P("grp", "lat", "lon"),
        P("lat", "lon"),
        P("lat", "lon"),
        P(),
    )
    sizes = (mesh.shape["lat"], mesh.shape["lon"])
    return jax.shard_map(
        functools.partial(on_device, sizes),
        mesh=mesh,
        in_specs=placed,
        out_specs=P("grp", "dir", "lat", "lon"),
        check_vma=False,
    )
```

```python
import functools
from collections import deque

import jax
import jax.numpy as jnp
from jax import lax
from jax.experimental import pallas as pl
from jax.experimental.pallas import tpu as pltpu
from jax.sharding import PartitionSpec as P

SUBCYCLES = 5
NLEV = 90
TIME_STEP = 0.35
HALF_STEP = 0.5 * TIME_STEP

LANES = 128
SUBLANES = 8
HALF = LANES // 2
HALO = 2 * SUBCYCLES
PAIRS = HALO // 2
FIELDS = 4
STATE = 3
COEF = 3
STRIP_SLOTS = HALF // HALO
CORNER_SLOTS = LANES // (2 * HALO)
F32 = jnp.float32


def ceil_div(a, b):
    return -(-a // b)


class Shapes:
    def __init__(self, height):
        self.height = height
        self.ext = height + 2 * HALO
        self.mid = self.ext // 2
        self.fold_first = height
        self.blocks = STATE * PAIRS + ceil_div(PAIRS, 2)
        self.strip_rows = self.mid - HALO
        self.strip_pairs = self.strip_rows // 2
        slots = self.strip_rows * STATE + self.strip_pairs
        self.side = self.blocks + ceil_div(slots, STRIP_SLOTS)
        self.main = STATE * HALO + PAIRS
        self.corners = ceil_div(FIELDS * HALO, CORNER_SLOTS)
        self.band = self.main + self.corners

    def block(self, i, f):
        upper = i // PAIRS
        if f < STATE:
            return f * PAIRS + i % PAIRS, upper, False
        return STATE * PAIRS + i % PAIRS // 2, i % PAIRS % 2, upper == 1

    def strip(self, k, f):
        slot, upper = (k - HALO) * STATE + f, False
        if f == COEF:
            upper = k - HALO >= self.strip_pairs
            slot = self.strip_rows * STATE + (k - HALO) % self.strip_pairs
        return self.blocks + slot // STRIP_SLOTS, HALO * (slot % STRIP_SLOTS), upper

    def corner(self, i, f):
        slot = f * HALO + i
        return self.main + slot // CORNER_SLOTS, 2 * HALO * (slot % CORNER_SLOTS)


def by_register(items, where):
    groups = {}
    for i, f in items:
        v, at = where(i, f)
        groups.setdefault(v, []).append((i, f, at))
    return groups


def roll(x, shift, axis=1):
    shift = shift % x.shape[axis]
    return x if shift == 0 else pltpu.roll(x, shift, axis)


def lane_ids():
    return lax.broadcasted_iota(jnp.int32, (SUBLANES, LANES), 1)


def sublane_ids():
    return lax.broadcasted_iota(jnp.int32, (SUBLANES, LANES), 0)


def run_staged(tasks, window):
    waiting = deque()

    def advance(task):
        try:
            next(task)
        except StopIteration:
            return
        waiting.append(task)

    for task in tasks:
        advance(task)
        while len(waiting) >= window:
            advance(waiting.popleft())
    while waiting:
        advance(waiting.popleft())


def row(ref, f, r):
    return ref[f, SUBLANES * r : SUBLANES * (r + 1), :]


def put_row(ref, f, r, value):
    ref[f, SUBLANES * r : SUBLANES * (r + 1), :] = value


def flat_rows(ref):
    return ref.reshape(ref.shape[0], ref.shape[1] * ref.shape[2], ref.shape[3])


def coef(ref, r, c):
    return jnp.broadcast_to(ref[SUBLANES * r + c : SUBLANES * r + c + 1, :], (SUBLANES, LANES))


def even_lon():
    return jnp.full((SUBLANES, LANES), lax.rem(lax.axis_index("lon"), 2), jnp.int32) == 0


def fold_place(fold_ref, lon_size):
    pivot = fold_ref[0]
    block = pivot // LANES
    rest = pivot - block * LANES
    low = rest < HALF
    place = jnp.where(low, rest + LANES, rest)
    branch = jnp.where(low, block - 1 + lon_size, block)
    return lax.rem(branch, lon_size), place


def pair_coefs(a, b):
    return jnp.where(sublane_ids() < SUBLANES // 2, a, roll(b, SUBLANES // 2, 0))


def lat_rows(sh, own_ref, outs):
    own = functools.partial(row, own_ref)

    def raw_rows(out, first):
        for f in range(STATE):
            for i in range(HALO):
                out[f * HALO + i] = own(f, first + i)
        for i in range(PAIRS):
            out[STATE * HALO + i] = pair_coefs(
                own(COEF, first + i), own(COEF, first + i + PAIRS)
            )

    top = sh.height - HALO
    lat_even = lax.rem(lax.axis_index("lat"), 2) == 0

    @pl.when(lat_even)
    def _():
        raw_rows(outs[0], top)
        if len(outs) > 1:
            raw_rows(outs[1], 0)

    @pl.when(jnp.logical_not(lat_even))
    def _():
        raw_rows(outs[0], 0)
        if len(outs) > 1:
            raw_rows(outs[1], top)


def sides_kernel(sh, sizes, x_hbm, b_hbm, m_hbm, l_hbm, p_hbm, *rest):
    a_out, b_out, own_ref, place_out, q_out = rest[:5]
    lat_outs, (x_ref, b_ref, m_ref, l_ref, p_ref, sems) = rest[5:-6], rest[-6:]
    lat_size, lon_size = sizes
    height = sh.height
    copies = [
        pltpu.make_async_copy(src, dst, sems.at[n])
        for n, (src, dst) in enumerate(
            [(b_hbm, b_ref), (m_hbm, m_ref), (l_hbm, l_ref), (p_hbm, p_ref)]
            + [(x_hbm.at[f], x_ref.at[f]) for f in range(STATE)]
        )
    ]
    for copy in copies:
        copy.start()
    for copy in copies[:4]:
        copy.wait()
    q_out[0], place = fold_place(p_ref, lon_size)
    place_out[...] = jnp.full((SUBLANES, LANES), place, jnp.int32)

    wet = m_ref[...].astype(F32)
    depth = 0.5 + 1.5 * ((l_ref[...] - 1).astype(F32) / (NLEV - 1)) ** 2
    row0 = lax.axis_index("lat") * height
    rows = (row0 + lax.broadcasted_iota(jnp.int32, (height, LANES), 0)).astype(F32)
    coriolis = 0.3 + 0.2 * rows / (height * lat_size)
    planes = [
        HALF_STEP * (wet * (depth + b_ref[0])),
        HALF_STEP * b_ref[1],
        HALF_STEP * b_ref[2],
        wet * (TIME_STEP * coriolis),
        wet,
    ]
    planes += [jnp.zeros_like(wet)] * (SUBLANES - len(planes))
    for c, plane in enumerate(planes):
        for r in range(0, height, SUBLANES):
            own_ref[COEF, pl.ds(SUBLANES * r + c, SUBLANES, stride=SUBLANES), :] = plane[
                r : r + SUBLANES
            ]
    for copy in copies[4:]:
        copy.wait()
    for f in range(STATE):
        for r in range(height):
            put_row(own_ref, f, r, x_ref[f, pl.ds(r, SUBLANES, stride=height), :])

    even = even_lon()
    lane, sub = lane_ids(), sublane_ids()
    low = lane < HALF
    own = functools.partial(row, own_ref)
    top = height - HALO

    def rows_of(f, r):
        return pair_coefs(own(f, r), own(f, r + PAIRS)) if f == COEF else own(f, r)

    def strip_rows_of(f, r, other):
        return pair_coefs(own(f, r), own(f, other)) if f == COEF else own(f, r)

    def block(v, a, b):
        a_up, b_up = roll(a, HALF), roll(b, HALF)
        yield
        east = jnp.where(low, a_up, b)
        west = jnp.where(low, a, b_up)
        a_out[v] = jnp.where(even, east, west)
        b_out[v] = jnp.where(even, west, east)

    def blocks():
        for f in range(STATE):
            for i in range(PAIRS):
                yield block(f * PAIRS + i, own(f, top + i), own(f, top + i + PAIRS))
        for i in range(0, PAIRS, 2):
            v, _, _ = sh.block(i, COEF)
            yield block(v, rows_of(COEF, top + i), rows_of(COEF, top + min(i + 1, PAIRS - 1)))

    slots = {}
    for k in range(HALO, sh.mid):
        for f in range(FIELDS):
            v, at, upper = sh.strip(k, f)
            if not upper:
                slots.setdefault(v, []).append((k, f, at))

    def strips(v):
        parts = []
        for k, f, at in slots[v]:
            ahead = sh.strip_pairs
            r = sh.ext - 1 - k - HALO
            a, b = strip_rows_of(f, k - HALO, k - HALO + ahead), strip_rows_of(f, r, r - ahead)
            end = at - (LANES - HALO)
            a_east, a_west = roll(a, end), roll(a, at)
            near = sh.ext - 1 - k < sh.fold_first
            near_other = sh.ext - 1 - k - ahead < sh.fold_first
            b_east, b_west = roll(b, HALF + end), roll(b, HALF + at)
            if not near:
                b_east, b_west = roll(b, end), roll(b, at)
                if f == COEF and near_other:
                    lower_half = sub < SUBLANES // 2
                    b_east = jnp.where(lower_half, b_east, roll(b, HALF + end))
                    b_west = jnp.where(lower_half, b_west, roll(b, HALF + at))
            parts.append((at, a_east, b_east, a_west, b_west))
        yield
        east = west = jnp.zeros((SUBLANES, LANES), F32)
        for at, ea, eb, wa, wb in parts:
            here = (lane >= at) & (lane < at + HALO)
            there = (lane >= HALF + at) & (lane < HALF + at + HALO)
            east = jnp.where(here, ea, jnp.where(there, eb, east))
            west = jnp.where(here, wa, jnp.where(there, wb, west))
        a_out[v] = jnp.where(even, east, west)
        b_out[v] = jnp.where(even, west, east)

    run_staged(blocks(), 10)
    run_staged([strips(v) for v in sorted(slots)], 2)
    lat_rows(sh, own_ref, lat_outs)


def bands_kernel(sh, sizes, own_ref, ra_ref, rb_ref, place_ref, fold_out, *lat_outs):
    lat_size, _ = sizes
    even = even_lon()
    lane, sub = lane_ids(), sublane_ids()
    low = lane < HALF
    own = functools.partial(row, own_ref)
    top = sh.height - HALO

    def got(v, upper):
        a, b = ra_ref[v], rb_ref[v]
        w, e = jnp.where(even, b, a), jnp.where(even, a, b)
        if upper:
            w, e = roll(w, SUBLANES // 2, 0), roll(e, SUBLANES // 2, 0)
        return w, e

    def corners(out, is_top):
        def register(v, items):
            parts = []
            for i, f, at in items:
                if is_top:
                    src, h, upper = sh.block(i, f)
                    w_at, e_at = HALF * h + HALF - HALO, HALF * h
                else:
                    src, w_at, upper = sh.strip(HALO + i, f)
                    e_at = w_at
                w, e = got(src, upper)
                parts.append((at, roll(w, at - w_at), roll(e, at + HALO - e_at)))
            yield
            total = jnp.zeros((SUBLANES, LANES), F32)
            for at, w, e in parts:
                total = jnp.where((lane >= at) & (lane < at + HALO), w, total)
                total = jnp.where((lane >= at + HALO) & (lane < at + 2 * HALO), e, total)
            out[v - sh.main] = total

        groups = by_register([(i, f) for f in range(FIELDS) for i in range(HALO)], sh.corner)
        run_staged([register(v, items) for v, items in groups.items()], 3)

    lat_even = lax.rem(lax.axis_index("lat"), 2) == 0

    @pl.when(lat_even)
    def _():
        corners(lat_outs[0], True)
        if len(lat_outs) > 1:
            corners(lat_outs[1], False)

    @pl.when(jnp.logical_not(lat_even))
    def _():
        corners(lat_outs[0], False)
        if len(lat_outs) > 1:
            corners(lat_outs[1], True)

    @pl.when(lax.axis_index("lat") == lat_size - 1)
    def _():
        where_to = place_ref[...]
        rest = where_to & (LANES - 1)
        eastern = where_to >= LANES
        backwards = (where_to - lane) & (LANES - 1)
        main_own = (eastern & (lane >= rest + 1)) | (jnp.logical_not(eastern) & (lane <= rest))
        upper = (lane >= rest + 1) & (lane <= rest + HALO)
        lower = (lane >= rest + 1 - HALO) & (lane <= rest)
        side_own = (eastern & lower) | (jnp.logical_not(eastern) & upper)
        side_far = (eastern & upper & (lane >= HALF)) | (
            jnp.logical_not(eastern) & lower & (lane < HALF)
        )
        coef_signs = jnp.where((sub == 1) | (sub == 2), -1.0, 1.0).astype(F32)

        def reversed_row(f, i):
            v, h, upper = sh.block(i, f)
            w, e = got(v, upper)
            if h == 0:
                w = roll(w, HALF)
            else:
                e = roll(e, HALF)
            v, at, upper = sh.strip(sh.ext - 1 - sh.fold_first - i, f)
            far_w, far_e = got(v, upper)
            far_w, far_e = roll(far_w, -HALO - at), roll(far_e, -at)
            yield
            both = jnp.where(low, e, w)
            mine = own(f, top + i)
            main = jnp.where(main_own, mine, both)
            side = jnp.where(
                side_own, mine, jnp.where(side_far, jnp.where(low, far_w, far_e), both)
            )
            if f == COEF:
                main, side = main * coef_signs, side * coef_signs
            elif f > 0:
                main, side = -main, -side
            main = jnp.take_along_axis(main, backwards, axis=1)
            side = jnp.take_along_axis(side, backwards, axis=1)
            yield
            j = HALO - 1 - i
            v, at = sh.corner(j, f)
            side = roll(side, at - (LANES - HALO))
            if f < STATE:
                fold_out[f * HALO + j] = main
            elif j < PAIRS:
                v2 = STATE * HALO + j
                fold_out[v2] = jnp.where(sub < SUBLANES // 2, main, fold_out[v2])
            else:
                fold_out[STATE * HALO + j - PAIRS] = roll(main, SUBLANES // 2, 0)
            yield
            here = (lane >= at) & (lane < at + 2 * HALO)
            fold_out[v] = jnp.where(here, side, fold_out[v])

        for v in range(STATE * HALO, sh.band):
            fold_out[v] = jnp.zeros((SUBLANES, LANES), F32)
        run_staged([reversed_row(f, i) for f in range(FIELDS) for i in range(HALO)], 8)


EAST0 = HALF // 2
LAG = 4
WET, NORTH_THICK = 4, 5


def north_sign():
    return jnp.where(lane_ids() < HALF, 1.0, -1.0).astype(F32)


class Sweep:
    def __init__(self, elev, vel, old, coef, put, known=None, mirror=None):
        self.elev_rows, self.vel_rows = elev, vel
        self.old, self.coef, self.put, self.known, self.mirror = old, coef, put, known, mirror
        self.flux_n, self.rolled, self.new, self.slopes = {}, {}, {}, {}
        self.sign = HALF_STEP * north_sign() if mirror is not None else HALF_STEP
        self.first = min(elev[0] - 1, vel[0])
        self.last = (max(elev[1] + 1, vel[1]) if mirror is None else mirror) + 2 * LAG

    def flux(self, r):
        lo, hi = self.elev_rows
        if not lo - 1 <= r <= hi or r == self.mirror:
            return
        eta, merid = self.old(0, r), self.old(2, r)
        thick = self.coef(r, 0)
        thick_n = thick if self.mirror is None else self.coef(r, NORTH_THICK)
        self.flux_n[r] = thick_n * merid + self.coef(r, 2) * eta
        if lo <= r < hi:
            east = thick * self.old(1, r) + self.coef(r, 1) * eta
            self.rolled[r] = (roll(east, -1), roll(east, 1))
        if self.mirror is not None and r == self.mirror - 1:
            self.flux_n[r + 1] = -roll(self.flux_n[r], HALF)

    def elevation(self, r):
        lo, hi = self.elev_rows
        if not lo <= r < hi:
            return
        plus, minus = self.rolled.pop(r)
        change = (plus - minus) + (self.flux_n[r + 1] - self.flux_n[r - 1])
        eta = self.coef(r, WET) * (self.old(0, r) - change)
        self.new[r] = eta
        self.put(0, r, eta)
        if self.mirror is not None and r == self.mirror - 1:
            self.new[r + 1] = roll(eta, HALF)

    def get_new(self, r):
        if r not in self.new:
            self.new[r] = self.known(r)
            if self.vel_rows[0] <= r < self.vel_rows[1]:
                self.put(0, r, self.new[r])
        return self.new[r]

    def slope(self, r):
        if self.vel_rows[0] <= r < self.vel_rows[1]:
            eta = self.get_new(r)
            self.slopes[r] = (roll(eta, -1), roll(eta, 1))

    def velocity(self, r):
        if not self.vel_rows[0] <= r < self.vel_rows[1]:
            return
        plus, minus = self.slopes.pop(r)
        wet, turn = self.coef(r, WET), self.coef(r, 3)
        zonal, merid = self.old(1, r), self.old(2, r)
        zonal = wet * (zonal - HALF_STEP * (plus - minus)) + turn * merid
        slope = self.sign * (self.get_new(r + 1) - self.get_new(r - 1))
        merid = wet * (merid - slope) - turn * zonal
        self.put(1, r, zonal)
        self.put(2, r, merid)

    def advance(self, t):
        self.flux(t)
        self.elevation(t - LAG)
        self.slope(t - LAG)
        self.velocity(t - 2 * LAG)


def run_sweeps(sweeps):
    for t in range(max(s.last - s.first for s in sweeps) + 1):
        for s in sweeps:
            s.advance(s.first + t)


def middle_kernel(sh, own_ref, hist_ref):
    for step in range(1, SUBCYCLES + 1):
        before, after = hist_ref.at[max(step - 2, 0)], hist_ref.at[step - 1]
        source = own_ref if step == 1 else before

        def put(f, r, value, after=after):
            put_row(after, f, r, value)

        run_sweeps(
            [
                Sweep(
                    (2 * step - 1, sh.height - 2 * step + 1),
                    (2 * step, sh.height - 2 * step),
                    functools.partial(row, source),
                    functools.partial(coef, own_ref.at[COEF]),
                    put,
                )
            ]
        )


def edges_kernel(sh, own_ref, ra_ref, rb_ref, start_ref, coef_ref, hist_ref):
    even = even_lon()
    lane = lane_ids()
    low = lane < HALF
    half_lane = lane & (HALF - 1)
    west_halo = half_lane < HALO
    east_own = (half_lane >= EAST0) & (half_lane < EAST0 + 2 * HALO)
    east_halo = (half_lane >= EAST0 + 2 * HALO) & (half_lane < EAST0 + 3 * HALO)
    sign = north_sign()

    def got(v, upper):
        a, b = ra_ref[v], rb_ref[v]
        w, e = jnp.where(even, b, a), jnp.where(even, a, b)
        if upper:
            w, e = roll(w, SUBLANES // 2, 0), roll(e, SUBLANES // 2, 0)
        return w, e

    def edge_row(f, k):
        own = own_columns(row(own_ref, f, k - HALO), row(own_ref, f, sh.ext - 1 - k - HALO))
        v, at, upper = sh.strip(k, f)
        w, e = got(v, upper)
        w, e = roll(w, -at), roll(e, EAST0 + 2 * HALO - at)
        i = sh.ext - 1 - k - sh.fold_first
        if i >= 0:
            v, h, upper = sh.block(i, f)
            w2, e2 = got(v, upper)
            w2 = roll(w2, HALF - (HALF * h + HALF - HALO))
            e2 = roll(e2, HALF + EAST0 + 2 * HALO - HALF * h)
        yield
        value = merge_own(own, low, east_own)
        if i >= 0:
            w, e = jnp.where(low, w, w2), jnp.where(low, e, e2)
        value = jnp.where(west_halo, w, jnp.where(east_halo, e, value))
        if f == COEF:
            put_edge_coefs(coef_ref, k - HALO, value, sign)
        else:
            put_row(start_ref, f, k - HALO, value)

    run_staged([edge_row(f, k) for k in range(HALO, sh.mid) for f in range(FIELDS)], 4)

    rows = sh.mid - HALO
    for step in range(1, SUBCYCLES + 1):
        source = start_ref if step == 1 else hist_ref.at[step - 2]
        after = hist_ref.at[step - 1]

        def put(f, r, value, after=after):
            put_row(after, f, r, value)

        run_sweeps(
            [
                Sweep(
                    (2 * step - 1, rows),
                    (2 * step, rows),
                    functools.partial(row, source),
                    functools.partial(coef, coef_ref),
                    put,
                    mirror=rows,
                )
            ]
        )


def own_columns(a, b):
    east = EAST0 - (LANES - 2 * HALO)
    return roll(a, HALO), roll(a, east), roll(b, HALF + HALO), roll(b, HALF + east)


def merge_own(parts, low, east_own):
    aw, ae, bw, be = parts
    return jnp.where(east_own, jnp.where(low, ae, be), jnp.where(low, aw, bw))


def put_edge_coefs(ref, k, value, sign):
    at = SUBLANES * k
    thick = value[0:1]
    ref[at : at + 2, :] = value[0:2]
    ref[at + 2 : at + 3, :] = value[2:3] * sign[0:1]
    ref[at + 3 : at + 4, :] = value[3:4]
    ref[at + WET : at + WET + 1, :] = jnp.where(thick > 0, 1.0, 0.0).astype(F32)
    ref[at + NORTH_THICK : at + NORTH_THICK + 1, :] = thick * sign[0:1]


class Wedges:
    def __init__(self, sh, own_ref, hist_ref, start_ref, ecoef_ref, ehist_ref, buffers):
        self.sh, self.own, self.hist = sh, own_ref, hist_ref
        self.start, self.ecoef, self.ehist = start_ref, ecoef_ref, ehist_ref
        self.main, self.main_c, self.edge, self.edge_c = buffers
        lane = lane_ids()
        self.low = lane < HALF
        self.half_lane = half = lane & (HALF - 1)
        self.east_own = (half >= EAST0) & (half < EAST0 + 2 * HALO)
        self.halo = (half < HALO) | ((half >= EAST0 + 2 * HALO) & (half < EAST0 + 3 * HALO))
        self.sign = north_sign()

    SHAPES = (
        (STATE, 4 * HALO * SUBLANES, LANES),
        (4 * HALO * SUBLANES, LANES),
        (FIELDS, 2 * HALO * SUBLANES, LANES),
        (HALO * SUBLANES, LANES),
    )

    def at(self, r):
        span = 2 * HALO
        return r if r < span else r - (self.sh.ext - span) + span

    def main_row(self, f, r):
        if f == COEF:
            at = SUBLANES * self.at(r)
            return self.main_c[at : at + SUBLANES, :]
        return row(self.main, f, self.at(r))

    def put_main(self, f, r, value):
        if f < STATE:
            put_row(self.main, f, self.at(r), value)
            return
        at = SUBLANES * self.at(r)
        self.main_c[at : at + SUBLANES, :] = value
        self.main_c[at + WET : at + WET + 1, :] = jnp.where(value[0:1] > 0, 1.0, 0.0).astype(F32)

    def put_halo(self, f, r, value):
        north = r >= self.sh.mid
        k, base = (self.sh.ext - 1 - r, HALF) if north else (r, 0)
        self.edge[f, SUBLANES * k : SUBLANES * (k + 1), base : base + HALF] = value[
            :, base : base + HALF
        ]

    def take_band(self, ref, halos, north):
        def band_row(f, i):
            r = self.sh.ext - HALO + i if north else i
            if f < STATE:
                value = ref[f * HALO + i]
            else:
                value = ref[STATE * HALO + i % PAIRS]
                value = value if i < PAIRS else roll(value, SUBLANES // 2, 0)
            w, e = halos(f, i, HALF if north else 0)
            yield
            self.put_main(f, r, value)
            self.put_halo(f, r, jnp.where(self.half_lane < HALO, w, e))

        run_staged([band_row(f, i) for f in range(FIELDS) for i in range(HALO)], 10)

    def no_band(self, north):
        zero = jnp.zeros((SUBLANES, LANES), F32)
        for f in range(FIELDS):
            for i in range(HALO):
                r = self.sh.ext - HALO + i if north else i
                self.put_main(f, r, zero)
                self.put_halo(f, r, zero)

    def edge_rows(self, north_only=False):
        def edge_row(f, k):
            b = self.main_row(f, self.sh.ext - 1 - k)
            parts = own_columns(b if north_only else self.main_row(f, k), b)
            yield
            value = jnp.where(
                self.halo, row(self.edge, f, k), merge_own(parts, self.low, self.east_own)
            )
            if f == COEF:
                put_edge_coefs(self.edge_c, k, value, self.sign)
            else:
                put_row(self.edge, f, k, value)

        run_staged([edge_row(f, k) for k in range(HALO) for f in range(FIELDS)], 8)

    def steps(self, sides):
        ext = self.sh.ext

        def put_edge(f, k, value):
            put_row(self.edge, f, k, value)

        def edge_coef(k, c):
            return coef(self.edge_c, k, c) if k < HALO else coef(self.ecoef, k - HALO, c)

        def main_coef(r, c):
            if HALO <= r < ext - HALO:
                return coef(self.own.at[COEF], r - HALO, c)
            return coef(self.main_c, self.at(r), c)

        for step in range(1, SUBCYCLES + 1):
            source = self.own if step == 1 else self.hist.at[step - 2]
            e_source = self.start if step == 1 else self.ehist.at[step - 2]
            after, e_after = self.hist.at[step - 1], self.ehist.at[step - 1]
            first, ready = 2 * step - 2, 2 * step + HALO - 2

            def old_main(f, r, source=source, ready=ready):
                if ready <= r < ext - ready:
                    return row(source, f, r - HALO)
                return self.main_row(f, r)

            def old_edge(f, k, e_source=e_source, ready=ready):
                return row(e_source, f, k - HALO) if k >= ready else row(self.edge, f, k)

            def known_main(r, after=after):
                return row(after, 0, r - HALO)

            def known_edge(k, e_after=e_after):
                return row(e_after, 0, k - HALO)

            elev, vel = (first + 1, ready + 1), (first + 2, ready + 2)
            sweeps = [
                Sweep(elev, vel, old_edge, edge_coef, put_edge, known_edge, mirror=self.sh.mid)
            ]
            if "south" in sides:
                sweeps.append(Sweep(elev, vel, old_main, main_coef, self.put_main, known_main))
            if "north" in sides:
                elev, vel = [(ext - rows[1], ext - rows[0]) for rows in (elev, vel)]
                sweeps.append(Sweep(elev, vel, old_main, main_coef, self.put_main, known_main))
            run_sweeps(sweeps)

    def output(self, first, last, put):
        ext, mid, ready = self.sh.ext, self.sh.mid, 2 * HALO
        final, e_final = self.hist.at[SUBCYCLES - 1], self.ehist.at[SUBCYCLES - 1]
        lane = lane_ids()

        def output_row(f, r):
            k, h = (r, 0) if r < mid else (ext - 1 - r, HALF)
            v = row(self.edge, f, k) if k < ready else row(e_final, f, k - HALO)
            w, e = roll(v, -(h + HALO)), roll(v, LANES - HALO - (h + EAST0 + HALO))
            yield
            inner = ready <= r < ext - ready
            v = row(final, f, r - HALO) if inner else self.main_row(f, r)
            v = jnp.where(lane < HALO, w, jnp.where(lane >= LANES - HALO, e, v))
            put(f, r - HALO, v)

        run_staged([output_row(f, r) for f in range(STATE) for r in range(first, last)], 10)


def wedge_kernel(sh, sizes, n_lat, *refs):
    lat_size, _ = sizes
    bands, refs = [(refs[n], refs[n_lat + n]) for n in range(n_lat)], refs[2 * n_lat :]
    state, (out_ref, order_out), kept, buffers = refs[:5], refs[5:7], refs[7:10], refs[10:]
    wedges = Wedges(sh, *state, buffers)
    order_out[...] = jnp.zeros((SUBLANES, LANES), F32)
    for source, target in zip(state[2:], kept):
        target[...] = source[...]

    def take(band, north):
        ref, corners = band

        def halos(f, i, base):
            v, at = sh.corner(i, f)
            v = corners[v - sh.main]
            return roll(v, base - at), roll(v, base + EAST0 + HALO - at)

        wedges.take_band(ref, halos, north)

    lat = lax.axis_index("lat")
    lat_even = lax.rem(lat, 2) == 0
    lat_odd = jnp.logical_not(lat_even)
    at_top = lat == lat_size - 1

    @pl.when(at_top)
    def _():
        wedges.no_band(True)

    @pl.when(lat == 0)
    def _():
        wedges.no_band(False)

    @pl.when(lat_even)
    def _():
        take(bands[0], True)

    @pl.when(lat_odd)
    def _():
        take(bands[0], False)

    if n_lat == 2:

        @pl.when(lat_odd & jnp.logical_not(at_top))
        def _():
            take(bands[1], True)

        @pl.when(lat_even & (lat > 0))
        def _():
            take(bands[1], False)

    wedges.edge_rows()
    wedges.steps(("south", "north"))

    out_flat = flat_rows(out_ref)

    def put(f, r, value):
        out_flat[f, pl.ds(r, SUBLANES, stride=sh.height), :] = value

    wedges.output(HALO, sh.ext - HALO, put)


def north_kernel(sh, sizes, fold_ref, order_ref, *buffers):
    @pl.when(lax.axis_index("lat") == sizes[0] - 1)
    def _():
        wedges = Wedges(sh, None, None, None, None, None, buffers)
        wedges.no_band(False)

        def halos(f, i, base):
            v, at = sh.corner(i, f)
            return roll(fold_ref[v], base - at), roll(fold_ref[v], base + EAST0 + HALO - at)

        wedges.take_band(fold_ref, halos, True)
        wedges.edge_rows(north_only=True)


def last_kernel(sh, sizes, *refs):
    lat_size, _ = sizes
    done_ref, state, begin = refs[0], refs[1:6], refs[6:10]
    out_hbm, late_ref, sems, main, edge = refs[10:]
    height, ext = sh.height, sh.ext
    split = (height - HALO) // SUBLANES * SUBLANES
    at_top = lax.axis_index("lat") == lat_size - 1
    lines = (pl.ds(0, split), pl.ds(split, height - split))

    def copies(source, part):
        return [
            pltpu.make_async_copy(
                source.at[f, :, lines[part]], out_hbm.at[f, :, lines[part]], sems.at[part, f]
            )
            for f in range(STATE)
        ]

    early = copies(done_ref, 0)
    for copy in early:
        copy.start()

    @pl.when(jnp.logical_not(at_top))
    def _():
        rest = copies(done_ref, 1)
        for copy in rest:
            copy.start()
        for copy in rest:
            copy.wait()

    @pl.when(at_top)
    def _():
        wedges = Wedges(sh, *state, (main, begin[1], edge, begin[3]))
        for f in range(STATE):
            for k in range(HALO):
                put_row(edge, f, k, row(begin[2], f, k))
                at = wedges.at(ext - 1 - k)
                put_row(main, f, at, row(begin[0], f, at))
        wedges.steps(("north",))

        late_flat, done_flat = flat_rows(late_ref), flat_rows(done_ref)

        def put(f, r, value):
            late_flat[f, pl.ds(r, SUBLANES, stride=height), :] = value

        for f in range(STATE):
            for r in range(split, height - HALO):
                put(f, r, done_flat[f, pl.ds(r, SUBLANES, stride=height), :])
        wedges.output(ext - 2 * HALO, ext - HALO, put)
        rest = copies(late_ref, 1)
        for copy in rest:
            copy.start()
        for copy in rest:
            copy.wait()

    for copy in early:
        copy.wait()


def pair_swaps(size, wrap):
    first = [(i, i ^ 1) for i in range(size)]
    second = []
    for i in range(size):
        j = i + 1 if i % 2 else i - 1
        if wrap or 0 <= j < size:
            second.append((i, j % size))
    return first, second


def vmem(n):
    return [pl.BlockSpec(memory_space=pltpu.VMEM)] * n


def in_hbm(x):
    return pltpu.with_memory_space_constraint(x, pltpu.HBM)


def smem():
    return pl.BlockSpec(memory_space=pltpu.SMEM)


def on_device(mesh_sizes, perturb, background, land_mask, levels, fold_partner):
    lat_size, lon_size = mesh_sizes
    height = perturb.shape[2]
    sh = Shapes(height)
    sizes = (lat_size, lon_size)
    flat = perturb.reshape(STATE, SUBLANES * height, LANES)
    tile = (SUBLANES, LANES)

    def shape(n):
        return pltpu.VMEM((n,) + tile, F32)

    params = pltpu.CompilerParams(vmem_limit_bytes=16 * 1024 * 1024)
    rows = SUBLANES * height
    n_lat = 1 if lat_size == 2 else 2
    side_a, side_b, own, place, branch, *lat_out = pl.pallas_call(
        functools.partial(sides_kernel, sh, sizes),
        out_shape=(
            shape(sh.side),
            shape(sh.side),
            pltpu.VMEM((FIELDS, rows, LANES), F32),
            pltpu.VMEM(tile, jnp.int32),
            jax.ShapeDtypeStruct((1,), jnp.int32),
        )
        + (shape(sh.main),) * n_lat,
        in_specs=[pl.BlockSpec(memory_space=pltpu.HBM)] * 5,
        out_specs=tuple(vmem(4)) + (smem(),) + tuple(vmem(n_lat)),
        scratch_shapes=[
            pltpu.VMEM(flat.shape, F32),
            pltpu.VMEM(background.shape, F32),
            pltpu.VMEM(land_mask.shape, jnp.int32),
            pltpu.VMEM(levels.shape, jnp.int32),
            pltpu.SMEM(fold_partner.shape, jnp.int32),
            pltpu.SemaphoreType.DMA((4 + STATE,)),
        ],
        compiler_params=params,
        name="sides",
    )(*[in_hbm(v) for v in (flat, background, land_mask, levels, fold_partner)])

    lon_swaps = pair_swaps(lon_size, True)
    got_a, got_b = [lax.ppermute(x, "lon", swap) for x, swap in zip((side_a, side_b), lon_swaps)]

    hist = pl.pallas_call(
        functools.partial(middle_kernel, sh),
        out_shape=pltpu.VMEM((SUBCYCLES, STATE, rows, LANES), F32),
        in_specs=vmem(1),
        out_specs=vmem(1)[0],
        compiler_params=params,
        name="middle",
    )(own)
    lat_swaps = pair_swaps(lat_size, False)[:n_lat]
    got_lat = [lax.ppermute(x, "lat", swap) for x, swap in zip(lat_out, lat_swaps)]
    fold_band, *lat_corners = pl.pallas_call(
        functools.partial(bands_kernel, sh, sizes),
        out_shape=(shape(sh.band),) + (shape(sh.corners),) * n_lat,
        in_specs=vmem(4),
        out_specs=tuple(vmem(1 + n_lat)),
        compiler_params=params,
        name="bands",
    )(own, got_a, got_b, place)

    edge_rows = SUBLANES * (sh.mid - HALO)
    edge_shapes = (
        pltpu.VMEM((STATE, edge_rows, LANES), F32),
        pltpu.VMEM((edge_rows, LANES), F32),
        pltpu.VMEM((SUBCYCLES, STATE, edge_rows, LANES), F32),
    )
    step_edges = jax.jit(
        pl.pallas_call(
            functools.partial(edges_kernel, sh),
            out_shape=edge_shapes,
            in_specs=vmem(3),
            out_specs=tuple(vmem(3)),
            compiler_params=params,
            name="edges",
        )
    )
    step_wedges = jax.jit(
        pl.pallas_call(
            functools.partial(wedge_kernel, sh, sizes, n_lat),
            out_shape=(pltpu.VMEM(perturb.shape, F32), pltpu.VMEM(tile, F32)) + edge_shapes,
            in_specs=vmem(2 * n_lat + 5),
            out_specs=tuple(vmem(5)),
            scratch_shapes=[pltpu.VMEM(x, F32) for x in Wedges.SHAPES],
            compiler_params=params,
            name="wedges",
        )
    )
    take_north = jax.jit(
        pl.pallas_call(
            functools.partial(north_kernel, sh, sizes),
            out_shape=tuple(pltpu.VMEM(x, F32) for x in Wedges.SHAPES),
            in_specs=vmem(2),
            out_specs=tuple(vmem(4)),
            compiler_params=params,
            name="north",
        )
    )
    top = lat_size - 1

    def rest(q, fold_band, lat_corners, got_lat, own, hist, got_a, got_b):
        across = []
        for m in range(lon_size):
            j = (q - m) % lon_size
            across.append((m * lat_size + top, j * lat_size + top))
        got_fold = lax.ppermute(fold_band, ("lon", "lat"), across)
        got_corners = [lax.ppermute(x, "lat", swap) for x, swap in zip(lat_corners, lat_swaps)]
        edges = step_edges(own, got_a, got_b)
        done, order, *kept = step_wedges(*got_lat, *got_corners, own, hist, *edges)
        return kept, done, take_north(got_fold, order)

    edges, done, beyond = lax.switch(
        branch[0],
        [functools.partial(rest, q) for q in range(lon_size)],
        fold_band,
        lat_corners,
        got_lat,
        own,
        hist,
        got_a,
        got_b,
    )
    return pl.pallas_call(
        functools.partial(last_kernel, sh, sizes),
        out_shape=jax.ShapeDtypeStruct(perturb.shape, F32),
        in_specs=vmem(10),
        out_specs=pl.BlockSpec(memory_space=pltpu.HBM),
        scratch_shapes=[
            pltpu.VMEM(perturb.shape, F32),
            pltpu.SemaphoreType.DMA((2, STATE)),
            pltpu.VMEM(Wedges.SHAPES[0], F32),
            pltpu.VMEM(Wedges.SHAPES[2], F32),
        ],
        compiler_params=params,
        name="last",
    )(done, own, hist, *edges, *beyond)


def solution(mesh):
    placed = (
        P("grp", "dir", "lat", "lon"),
        P("grp", "lat", "lon"),
        P("lat", "lon"),
        P("lat", "lon"),
        P(),
    )
    sizes = (mesh.shape["lat"], mesh.shape["lon"])
    return jax.shard_map(
        functools.partial(on_device, sizes),
        mesh=mesh,
        in_specs=placed,
        out_specs=P("grp", "dir", "lat", "lon"),
        check_vma=False,
    )
```

```python
import functools
from collections import deque

import jax
import jax.numpy as jnp
from jax import lax
from jax.experimental import pallas as pl
from jax.experimental.pallas import tpu as pltpu
from jax.sharding import PartitionSpec as P

SUBCYCLES = 5
NLEV = 90
TIME_STEP = 0.35
HALF_STEP = 0.5 * TIME_STEP

LANES = 128
SUBLANES = 8
HALF = LANES // 2
HALO = 2 * SUBCYCLES
PAIRS = HALO // 2
FIELDS = 4
STATE = 3
COEF = 3
STRIP_SLOTS = HALF // HALO
CORNER_SLOTS = LANES // (2 * HALO)
F32 = jnp.float32


def ceil_div(a, b):
    return -(-a // b)


class Shapes:
    def __init__(self, height):
        self.height = height
        self.ext = height + 2 * HALO
        self.mid = self.ext // 2
        self.fold_first = height
        self.blocks = STATE * PAIRS + ceil_div(PAIRS, 2)
        self.strip_rows = self.mid - HALO
        self.strip_pairs = self.strip_rows // 2
        slots = self.strip_rows * STATE + self.strip_pairs
        self.side = self.blocks + ceil_div(slots, STRIP_SLOTS)
        self.main = STATE * HALO + PAIRS
        self.corners = ceil_div(FIELDS * HALO, CORNER_SLOTS)
        self.band = self.main + self.corners

    def block(self, i, f):
        upper = i // PAIRS
        if f < STATE:
            return f * PAIRS + i % PAIRS, upper, False
        return STATE * PAIRS + i % PAIRS // 2, i % PAIRS % 2, upper == 1

    def strip(self, k, f):
        slot, upper = (k - HALO) * STATE + f, False
        if f == COEF:
            upper = k - HALO >= self.strip_pairs
            slot = self.strip_rows * STATE + (k - HALO) % self.strip_pairs
        return self.blocks + slot // STRIP_SLOTS, HALO * (slot % STRIP_SLOTS), upper

    def corner(self, i, f):
        slot = f * HALO + i
        return self.main + slot // CORNER_SLOTS, 2 * HALO * (slot % CORNER_SLOTS)


def by_register(items, where):
    groups = {}
    for i, f in items:
        v, at = where(i, f)
        groups.setdefault(v, []).append((i, f, at))
    return groups


def roll(x, shift, axis=1):
    shift = shift % x.shape[axis]
    return x if shift == 0 else pltpu.roll(x, shift, axis)


def lane_ids():
    return lax.broadcasted_iota(jnp.int32, (SUBLANES, LANES), 1)


def sublane_ids():
    return lax.broadcasted_iota(jnp.int32, (SUBLANES, LANES), 0)


def run_staged(tasks, window):
    waiting = deque()

    def advance(task):
        try:
            next(task)
        except StopIteration:
            return
        waiting.append(task)

    for task in tasks:
        advance(task)
        while len(waiting) >= window:
            advance(waiting.popleft())
    while waiting:
        advance(waiting.popleft())


def row(ref, f, r):
    return ref[f, SUBLANES * r : SUBLANES * (r + 1), :]


def put_row(ref, f, r, value):
    ref[f, SUBLANES * r : SUBLANES * (r + 1), :] = value


def flat_rows(ref):
    return ref.reshape(ref.shape[0], ref.shape[1] * ref.shape[2], ref.shape[3])


def coef(ref, r, c):
    return jnp.broadcast_to(ref[SUBLANES * r + c : SUBLANES * r + c + 1, :], (SUBLANES, LANES))


def even_lon():
    return jnp.full((SUBLANES, LANES), lax.rem(lax.axis_index("lon"), 2), jnp.int32) == 0


def fold_place(fold_ref, lon_size):
    pivot = fold_ref[0]
    block = pivot // LANES
    rest = pivot - block * LANES
    low = rest < HALF
    place = jnp.where(low, rest + LANES, rest)
    branch = jnp.where(low, block - 1 + lon_size, block)
    return lax.rem(branch, lon_size), place


def pair_coefs(a, b):
    return jnp.where(sublane_ids() < SUBLANES // 2, a, roll(b, SUBLANES // 2, 0))


def lat_rows(sh, own_ref, outs):
    own = functools.partial(row, own_ref)

    def raw_rows(out, first):
        for f in range(STATE):
            for i in range(HALO):
                out[f * HALO + i] = own(f, first + i)
        for i in range(PAIRS):
            out[STATE * HALO + i] = pair_coefs(
                own(COEF, first + i), own(COEF, first + i + PAIRS)
            )

    top = sh.height - HALO
    lat_even = lax.rem(lax.axis_index("lat"), 2) == 0

    @pl.when(lat_even)
    def _():
        raw_rows(outs[0], top)
        if len(outs) > 1:
            raw_rows(outs[1], 0)

    @pl.when(jnp.logical_not(lat_even))
    def _():
        raw_rows(outs[0], 0)
        if len(outs) > 1:
            raw_rows(outs[1], top)


def sides_kernel(sh, sizes, x_hbm, b_hbm, m_hbm, l_hbm, *rest):
    a_out, b_out, own_ref = rest[:3]
    lat_outs, (x_ref, b_ref, m_ref, l_ref, sems) = rest[3:-5], rest[-5:]
    lat_size, _ = sizes
    height = sh.height
    copies = [
        pltpu.make_async_copy(src, dst, sems.at[n])
        for n, (src, dst) in enumerate(
            [(b_hbm, b_ref), (m_hbm, m_ref), (l_hbm, l_ref)]
            + [(x_hbm.at[f], x_ref.at[f]) for f in range(STATE)]
        )
    ]
    for copy in copies:
        copy.start()
    for copy in copies[:3]:
        copy.wait()

    wet = m_ref[...].astype(F32)
    depth = 0.5 + 1.5 * ((l_ref[...] - 1).astype(F32) / (NLEV - 1)) ** 2
    row0 = lax.axis_index("lat") * height
    rows = (row0 + lax.broadcasted_iota(jnp.int32, (height, LANES), 0)).astype(F32)
    coriolis = 0.3 + 0.2 * rows / (height * lat_size)
    planes = [
        HALF_STEP * (wet * (depth + b_ref[0])),
        HALF_STEP * b_ref[1],
        HALF_STEP * b_ref[2],
        wet * (TIME_STEP * coriolis),
        wet,
    ]
    planes += [jnp.zeros_like(wet)] * (SUBLANES - len(planes))
    for c, plane in enumerate(planes):
        for r in range(0, height, SUBLANES):
            own_ref[COEF, pl.ds(SUBLANES * r + c, SUBLANES, stride=SUBLANES), :] = plane[
                r : r + SUBLANES
            ]
    for copy in copies[3:]:
        copy.wait()
    for f in range(STATE):
        for r in range(height):
            put_row(own_ref, f, r, x_ref[f, pl.ds(r, SUBLANES, stride=height), :])

    even = even_lon()
    lane, sub = lane_ids(), sublane_ids()
    low = lane < HALF
    own = functools.partial(row, own_ref)
    top = height - HALO

    def rows_of(f, r):
        return pair_coefs(own(f, r), own(f, r + PAIRS)) if f == COEF else own(f, r)

    def strip_rows_of(f, r, other):
        return pair_coefs(own(f, r), own(f, other)) if f == COEF else own(f, r)

    def block(v, a, b):
        a_up, b_up = roll(a, HALF), roll(b, HALF)
        yield
        east = jnp.where(low, a_up, b)
        west = jnp.where(low, a, b_up)
        a_out[v] = jnp.where(even, east, west)
        b_out[v] = jnp.where(even, west, east)

    def blocks():
        for f in range(STATE):
            for i in range(PAIRS):
                yield block(f * PAIRS + i, own(f, top + i), own(f, top + i + PAIRS))
        for i in range(0, PAIRS, 2):
            v, _, _ = sh.block(i, COEF)
            yield block(v, rows_of(COEF, top + i), rows_of(COEF, top + min(i + 1, PAIRS - 1)))

    slots = {}
    for k in range(HALO, sh.mid):
        for f in range(FIELDS):
            v, at, upper = sh.strip(k, f)
            if not upper:
                slots.setdefault(v, []).append((k, f, at))

    def strips(v):
        parts = []
        for k, f, at in slots[v]:
            ahead = sh.strip_pairs
            r = sh.ext - 1 - k - HALO
            a, b = strip_rows_of(f, k - HALO, k - HALO + ahead), strip_rows_of(f, r, r - ahead)
            end = at - (LANES - HALO)
            a_east, a_west = roll(a, end), roll(a, at)
            near = sh.ext - 1 - k < sh.fold_first
            near_other = sh.ext - 1 - k - ahead < sh.fold_first
            b_east, b_west = roll(b, HALF + end), roll(b, HALF + at)
            if not near:
                b_east, b_west = roll(b, end), roll(b, at)
                if f == COEF and near_other:
                    lower_half = sub < SUBLANES // 2
                    b_east = jnp.where(lower_half, b_east, roll(b, HALF + end))
                    b_west = jnp.where(lower_half, b_west, roll(b, HALF + at))
            parts.append((at, a_east, b_east, a_west, b_west))
        yield
        east = west = jnp.zeros((SUBLANES, LANES), F32)
        for at, ea, eb, wa, wb in parts:
            here = (lane >= at) & (lane < at + HALO)
            there = (lane >= HALF + at) & (lane < HALF + at + HALO)
            east = jnp.where(here, ea, jnp.where(there, eb, east))
            west = jnp.where(here, wa, jnp.where(there, wb, west))
        a_out[v] = jnp.where(even, east, west)
        b_out[v] = jnp.where(even, west, east)

    run_staged(blocks(), 10)
    run_staged([strips(v) for v in sorted(slots)], 2)
    lat_rows(sh, own_ref, lat_outs)


def bands_kernel(sh, sizes, own_ref, ra_ref, rb_ref, place_ref, fold_out, *lat_outs):
    lat_size, _ = sizes
    even = even_lon()
    lane, sub = lane_ids(), sublane_ids()
    low = lane < HALF
    own = functools.partial(row, own_ref)
    top = sh.height - HALO

    def got(v, upper):
        a, b = ra_ref[v], rb_ref[v]
        w, e = jnp.where(even, b, a), jnp.where(even, a, b)
        if upper:
            w, e = roll(w, SUBLANES // 2, 0), roll(e, SUBLANES // 2, 0)
        return w, e

    def corners(out, is_top):
        def register(v, items):
            parts = []
            for i, f, at in items:
                if is_top:
                    src, h, upper = sh.block(i, f)
                    w_at, e_at = HALF * h + HALF - HALO, HALF * h
                else:
                    src, w_at, upper = sh.strip(HALO + i, f)
                    e_at = w_at
                w, e = got(src, upper)
                parts.append((at, roll(w, at - w_at), roll(e, at + HALO - e_at)))
            yield
            total = jnp.zeros((SUBLANES, LANES), F32)
            for at, w, e in parts:
                total = jnp.where((lane >= at) & (lane < at + HALO), w, total)
                total = jnp.where((lane >= at + HALO) & (lane < at + 2 * HALO), e, total)
            out[v - sh.main] = total

        groups = by_register([(i, f) for f in range(FIELDS) for i in range(HALO)], sh.corner)
        run_staged([register(v, items) for v, items in groups.items()], 3)

    lat_even = lax.rem(lax.axis_index("lat"), 2) == 0

    @pl.when(lat_even)
    def _():
        corners(lat_outs[0], True)
        if len(lat_outs) > 1:
            corners(lat_outs[1], False)

    @pl.when(jnp.logical_not(lat_even))
    def _():
        corners(lat_outs[0], False)
        if len(lat_outs) > 1:
            corners(lat_outs[1], True)

    @pl.when(lax.axis_index("lat") == lat_size - 1)
    def _():
        where_to = place_ref[...]
        rest = where_to & (LANES - 1)
        eastern = where_to >= LANES
        backwards = (where_to - lane) & (LANES - 1)
        main_own = (eastern & (lane >= rest + 1)) | (jnp.logical_not(eastern) & (lane <= rest))
        upper = (lane >= rest + 1) & (lane <= rest + HALO)
        lower = (lane >= rest + 1 - HALO) & (lane <= rest)
        side_own = (eastern & lower) | (jnp.logical_not(eastern) & upper)
        side_far = (eastern & upper & (lane >= HALF)) | (
            jnp.logical_not(eastern) & lower & (lane < HALF)
        )
        coef_signs = jnp.where((sub == 1) | (sub == 2), -1.0, 1.0).astype(F32)

        def reversed_row(f, i):
            v, h, upper = sh.block(i, f)
            w, e = got(v, upper)
            if h == 0:
                w = roll(w, HALF)
            else:
                e = roll(e, HALF)
            v, at, upper = sh.strip(sh.ext - 1 - sh.fold_first - i, f)
            far_w, far_e = got(v, upper)
            far_w, far_e = roll(far_w, -HALO - at), roll(far_e, -at)
            yield
            both = jnp.where(low, e, w)
            mine = own(f, top + i)
            main = jnp.where(main_own, mine, both)
            side = jnp.where(
                side_own, mine, jnp.where(side_far, jnp.where(low, far_w, far_e), both)
            )
            if f == COEF:
                main, side = main * coef_signs, side * coef_signs
            elif f > 0:
                main, side = -main, -side
            main = jnp.take_along_axis(main, backwards, axis=1)
            side = jnp.take_along_axis(side, backwards, axis=1)
            yield
            j = HALO - 1 - i
            v, at = sh.corner(j, f)
            side = roll(side, at - (LANES - HALO))
            if f < STATE:
                fold_out[f * HALO + j] = main
            elif j < PAIRS:
                v2 = STATE * HALO + j
                fold_out[v2] = jnp.where(sub < SUBLANES // 2, main, fold_out[v2])
            else:
                fold_out[STATE * HALO + j - PAIRS] = roll(main, SUBLANES // 2, 0)
            yield
            here = (lane >= at) & (lane < at + 2 * HALO)
            fold_out[v] = jnp.where(here, side, fold_out[v])

        for v in range(STATE * HALO, sh.band):
            fold_out[v] = jnp.zeros((SUBLANES, LANES), F32)
        run_staged([reversed_row(f, i) for f in range(FIELDS) for i in range(HALO)], 8)


EAST0 = HALF // 2
LAG = 4
WET, NORTH_THICK = 4, 5


def north_sign():
    return jnp.where(lane_ids() < HALF, 1.0, -1.0).astype(F32)


class Sweep:
    def __init__(self, elev, vel, old, coef, put, known=None, mirror=None):
        self.elev_rows, self.vel_rows = elev, vel
        self.old, self.coef, self.put, self.known, self.mirror = old, coef, put, known, mirror
        self.flux_n, self.rolled, self.new, self.slopes = {}, {}, {}, {}
        self.sign = HALF_STEP * north_sign() if mirror is not None else HALF_STEP
        self.first = min(elev[0] - 1, vel[0])
        self.last = max(elev[1], vel[1]) + 2 * LAG

    def flux(self, r):
        lo, hi = self.elev_rows
        if not lo - 1 <= r <= hi or r == self.mirror:
            return
        eta, merid = self.old(0, r), self.old(2, r)
        thick = self.coef(r, 0)
        thick_n = thick if self.mirror is None else self.coef(r, NORTH_THICK)
        self.flux_n[r] = thick_n * merid + self.coef(r, 2) * eta
        if lo <= r < hi:
            east = thick * self.old(1, r) + self.coef(r, 1) * eta
            self.rolled[r] = (roll(east, -1), roll(east, 1))
        if self.mirror is not None and r == self.mirror - 1:
            self.flux_n[r + 1] = -roll(self.flux_n[r], HALF)

    def elevation(self, r):
        lo, hi = self.elev_rows
        if not lo <= r < hi:
            return
        plus, minus = self.rolled.pop(r)
        change = (plus - minus) + (self.flux_n[r + 1] - self.flux_n[r - 1])
        eta = self.coef(r, WET) * (self.old(0, r) - change)
        self.new[r] = eta
        self.put(0, r, eta)
        if self.mirror is not None and r == self.mirror - 1:
            self.new[r + 1] = roll(eta, HALF)

    def get_new(self, r):
        if r not in self.new:
            self.new[r] = self.known(r)
            if self.vel_rows[0] <= r < self.vel_rows[1]:
                self.put(0, r, self.new[r])
        return self.new[r]

    def slope(self, r):
        if self.vel_rows[0] <= r < self.vel_rows[1]:
            eta = self.get_new(r)
            self.slopes[r] = (roll(eta, -1), roll(eta, 1))

    def velocity(self, r):
        if not self.vel_rows[0] <= r < self.vel_rows[1]:
            return
        plus, minus = self.slopes.pop(r)
        wet, turn = self.coef(r, WET), self.coef(r, 3)
        zonal, merid = self.old(1, r), self.old(2, r)
        zonal = wet * (zonal - HALF_STEP * (plus - minus)) + turn * merid
        slope = self.sign * (self.get_new(r + 1) - self.get_new(r - 1))
        merid = wet * (merid - slope) - turn * zonal
        self.put(1, r, zonal)
        self.put(2, r, merid)

    def advance(self, t):
        self.flux(t)
        self.elevation(t - LAG)
        self.slope(t - LAG)
        self.velocity(t - 2 * LAG)


def run_chains(chains):
    starts = []
    for chain in chains:
        at, ticks = 0, []
        for n, sweep in enumerate(chain):
            if n:
                at += max(2 * LAG + sweep.first - chain[n - 1].first, 0)
            ticks.append(at)
        starts.append(ticks)
    ends = [ticks[n] + s.last - s.first for c, ticks in zip(chains, starts) for n, s in enumerate(c)]
    for t in range(max(ends) + 1):
        for n in range(SUBCYCLES):
            for chain, ticks in zip(chains, starts):
                if t >= ticks[n]:
                    chain[n].advance(chain[n].first + t - ticks[n])


def middle_kernel(sh, sizes, own_ref, p_hbm, hist_ref, place_out, q_out, p_ref, sem):
    copy = pltpu.make_async_copy(p_hbm, p_ref, sem)
    copy.start()
    chain = []
    for step in range(1, SUBCYCLES + 1):
        source = own_ref if step == 1 else hist_ref.at[step - 2]
        chain.append(
            Sweep(
                (2 * step - 1, sh.height - 2 * step + 1),
                (2 * step, sh.height - 2 * step),
                functools.partial(row, source),
                functools.partial(coef, own_ref.at[COEF]),
                functools.partial(put_row, hist_ref.at[step - 1]),
            )
        )
    run_chains([chain])
    copy.wait()
    q_out[0], place = fold_place(p_ref, sizes[1])
    place_out[...] = jnp.full((SUBLANES, LANES), place, jnp.int32)


def edges_kernel(sh, own_ref, ra_ref, rb_ref, start_ref, coef_ref, hist_ref):
    even = even_lon()
    lane = lane_ids()
    low = lane < HALF
    half_lane = lane & (HALF - 1)
    west_halo = half_lane < HALO
    east_own = (half_lane >= EAST0) & (half_lane < EAST0 + 2 * HALO)
    east_halo = (half_lane >= EAST0 + 2 * HALO) & (half_lane < EAST0 + 3 * HALO)
    sign = north_sign()

    def got(v, upper):
        a, b = ra_ref[v], rb_ref[v]
        w, e = jnp.where(even, b, a), jnp.where(even, a, b)
        if upper:
            w, e = roll(w, SUBLANES // 2, 0), roll(e, SUBLANES // 2, 0)
        return w, e

    def edge_row(f, k):
        own = own_columns(row(own_ref, f, k - HALO), row(own_ref, f, sh.ext - 1 - k - HALO))
        v, at, upper = sh.strip(k, f)
        w, e = got(v, upper)
        w, e = roll(w, -at), roll(e, EAST0 + 2 * HALO - at)
        i = sh.ext - 1 - k - sh.fold_first
        if i >= 0:
            v, h, upper = sh.block(i, f)
            w2, e2 = got(v, upper)
            w2 = roll(w2, HALF - (HALF * h + HALF - HALO))
            e2 = roll(e2, HALF + EAST0 + 2 * HALO - HALF * h)
        yield
        value = merge_own(own, low, east_own)
        if i >= 0:
            w, e = jnp.where(low, w, w2), jnp.where(low, e, e2)
        value = jnp.where(west_halo, w, jnp.where(east_halo, e, value))
        if f == COEF:
            put_edge_coefs(coef_ref, k - HALO, value, sign)
        else:
            put_row(start_ref, f, k - HALO, value)

    run_staged([edge_row(f, k) for k in range(HALO, sh.mid) for f in range(FIELDS)], 4)

    rows = sh.mid - HALO
    chain = []
    for step in range(1, SUBCYCLES + 1):
        source = start_ref if step == 1 else hist_ref.at[step - 2]
        chain.append(
            Sweep(
                (2 * step - 1, rows),
                (2 * step, rows),
                functools.partial(row, source),
                functools.partial(coef, coef_ref),
                functools.partial(put_row, hist_ref.at[step - 1]),
                mirror=rows,
            )
        )
    run_chains([chain])


def own_columns(a, b):
    east = EAST0 - (LANES - 2 * HALO)
    return roll(a, HALO), roll(a, east), roll(b, HALF + HALO), roll(b, HALF + east)


def merge_own(parts, low, east_own):
    aw, ae, bw, be = parts
    return jnp.where(east_own, jnp.where(low, ae, be), jnp.where(low, aw, bw))


def put_edge_coefs(ref, k, value, sign):
    at = SUBLANES * k
    thick = value[0:1]
    ref[at : at + 2, :] = value[0:2]
    ref[at + 2 : at + 3, :] = value[2:3] * sign[0:1]
    ref[at + 3 : at + 4, :] = value[3:4]
    ref[at + WET : at + WET + 1, :] = jnp.where(thick > 0, 1.0, 0.0).astype(F32)
    ref[at + NORTH_THICK : at + NORTH_THICK + 1, :] = thick * sign[0:1]


class Wedges:
    def __init__(self, sh, own=None, hist=None, edges=(None,) * 3, main=None, edge=None):
        self.sh, self.own, self.hist = sh, own, hist
        self.start, self.ecoef, self.ehist = edges
        self.main, self.begin, self.main_c = main
        self.edge, self.edge_c = edge or (None, None)
        lane = lane_ids()
        self.low = lane < HALF
        self.half_lane = half = lane & (HALF - 1)
        self.east_own = (half >= EAST0) & (half < EAST0 + 2 * HALO)
        halo = (half < HALO) | ((half >= EAST0 + 2 * HALO) & (half < EAST0 + 3 * HALO))
        self.halo_south, self.halo_north = halo & self.low, halo & (lane >= HALF)
        self.sign = north_sign()

    SHAPES = (
        (STATE, 4 * HALO * SUBLANES, LANES),
        (4 * HALO * SUBLANES, LANES),
        (FIELDS, 2 * HALO * SUBLANES, LANES),
        (HALO * SUBLANES, LANES),
    )

    def at(self, r):
        span = 2 * HALO
        return r if r < span else r - (self.sh.ext - span) + span

    def main_row(self, f, r):
        if f == COEF:
            at = SUBLANES * self.at(r)
            return self.main_c[at : at + SUBLANES, :]
        return row(self.main, f, self.at(r))

    def first_row(self, f, r):
        return self.main_row(f, r) if f == COEF else row(self.begin, f, self.at(r))

    def put_main(self, f, r, value):
        if f < STATE:
            put_row(self.main, f, self.at(r), value)
            return
        at = SUBLANES * self.at(r)
        self.main_c[at : at + SUBLANES, :] = value
        self.main_c[at + WET : at + WET + 1, :] = jnp.where(value[0:1] > 0, 1.0, 0.0).astype(F32)

    def put_halo(self, f, r, value):
        north = r >= self.sh.mid
        k, mask = (self.sh.ext - 1 - r, self.halo_north) if north else (r, self.halo_south)
        put_row(self.edge, f, k, jnp.where(mask, value, row(self.edge, f, k)))

    def band(self, north):
        return [self.sh.ext - HALO + i if north else i for i in range(HALO)]

    def take_rows(self, ref, north):
        for f in range(FIELDS):
            for i, r in enumerate(self.band(north)):
                if ref is None:
                    value = jnp.zeros((SUBLANES, LANES), F32)
                elif f < STATE:
                    value = ref[f * HALO + i]
                else:
                    value = ref[STATE * HALO + i % PAIRS]
                    value = value if i < PAIRS else roll(value, SUBLANES // 2, 0)
                self.put_main(f, r, value)
                if f < STATE and self.begin is not self.main:
                    put_row(self.begin, f, self.at(r), value)

    def take_halos(self, ref, first, north):
        base = HALF if north else 0
        if ref is None:
            for f in range(FIELDS):
                for r in self.band(north):
                    self.put_halo(f, r, jnp.zeros((SUBLANES, LANES), F32))
            return

        def band_row(f, i, r):
            v, at = self.sh.corner(i, f)
            v = ref[v - self.sh.main + first]
            w, e = roll(v, base - at), roll(v, base + EAST0 + HALO - at)
            yield
            self.put_halo(f, r, jnp.where(self.half_lane < HALO, w, e))

        rows = list(enumerate(self.band(north)))
        run_staged([band_row(f, i, r) for f in range(FIELDS) for i, r in rows], 16)

    def edge_own(self, out, north_only=False):
        def edge_row(f, k):
            b = self.first_row(f, self.sh.ext - 1 - k)
            parts = own_columns(b if north_only else self.first_row(f, k), b)
            yield
            put_row(out, f, k, merge_own(parts, self.low, self.east_own))

        run_staged([edge_row(f, k) for k in range(HALO) for f in range(FIELDS)], 8)

    def edge_coefs(self):
        for k in range(HALO):
            put_edge_coefs(self.edge_c, k, row(self.edge, COEF, k), self.sign)

    def steps(self, sides):
        ext = self.sh.ext

        def put_edge(f, k, value):
            put_row(self.edge, f, k, value)

        def edge_coef(k, c):
            return coef(self.edge_c, k, c) if k < HALO else coef(self.ecoef, k - HALO, c)

        def main_coef(r, c):
            if HALO <= r < ext - HALO:
                return coef(self.own.at[COEF], r - HALO, c)
            return coef(self.main_c, self.at(r), c)

        edges, south, north = [], [], []
        for step in range(1, SUBCYCLES + 1):
            first, ready = 2 * step - 2, 2 * step + HALO - 2

            def old_main(f, r, step=step, ready=ready):
                if ready <= r < ext - ready:
                    return row(self.own if step == 1 else self.hist.at[step - 2], f, r - HALO)
                return self.main_row(f, r)

            def old_edge(f, k, step=step, ready=ready):
                if k >= ready:
                    return row(self.start if step == 1 else self.ehist.at[step - 2], f, k - HALO)
                return row(self.edge, f, k)

            def known_main(r, step=step):
                return row(self.hist.at[step - 1], 0, r - HALO)

            def known_edge(k, step=step):
                return row(self.ehist.at[step - 1], 0, k - HALO)

            elev, vel = (first + 1, ready + 1), (first + 2, ready + 2)
            edges.append(
                Sweep(elev, vel, old_edge, edge_coef, put_edge, known_edge, mirror=self.sh.mid)
            )
            south.append(Sweep(elev, vel, old_main, main_coef, self.put_main, known_main))
            elev, vel = [(ext - rows[1], ext - rows[0]) for rows in (elev, vel)]
            north.append(Sweep(elev, vel, old_main, main_coef, self.put_main, known_main))
        chains = {"edges": edges, "south": south, "north": north}
        run_chains([chains[name] for name in sides])

    def output(self, first, last, put):
        ext, mid, ready = self.sh.ext, self.sh.mid, 2 * HALO
        final, e_final = self.hist.at[SUBCYCLES - 1], self.ehist.at[SUBCYCLES - 1]
        lane = lane_ids()

        def output_row(f, r):
            k, h = (r, 0) if r < mid else (ext - 1 - r, HALF)
            v = row(self.edge, f, k) if k < ready else row(e_final, f, k - HALO)
            w, e = roll(v, -(h + HALO)), roll(v, LANES - HALO - (h + EAST0 + HALO))
            yield
            inner = ready <= r < ext - ready
            v = row(final, f, r - HALO) if inner else self.main_row(f, r)
            v = jnp.where(lane < HALO, w, jnp.where(lane >= LANES - HALO, e, v))
            put(f, r - HALO, v)

        run_staged([output_row(f, r) for f in range(STATE) for r in range(first, last)], 10)


def for_bands(sizes, n_lat, take):
    lat_size, _ = sizes
    lat = lax.axis_index("lat")
    lat_even = lax.rem(lat, 2) == 0
    lat_odd = jnp.logical_not(lat_even)
    at_top = lat == lat_size - 1
    pl.when(at_top)(lambda: take(None, True))
    pl.when(lat == 0)(lambda: take(None, False))
    pl.when(lat_even)(lambda: take(0, True))
    pl.when(lat_odd)(lambda: take(0, False))
    if n_lat == 2:
        pl.when(lat_odd & jnp.logical_not(at_top))(lambda: take(1, True))
        pl.when(lat_even & (lat > 0))(lambda: take(1, False))


def wedge_rows_kernel(sh, sizes, n_lat, *refs):
    bands, edges, outs = refs[:n_lat], refs[-10:-7], refs[-7:]
    own_ref, hist_ref = refs[n_lat], refs[n_lat + 1]
    main, edge_out, kept = outs[:3], outs[3], outs[4:]
    wedges = Wedges(sh, own_ref, hist_ref, main=main)

    def take(n, north):
        wedges.take_rows(None if n is None else bands[n], north)

    for_bands(sizes, n_lat, take)
    wedges.edge_own(edge_out)
    for source, target in zip(edges, kept):
        target[...] = source[...]
    wedges.steps(("south", "north"))


def wedge_edges_kernel(sh, sizes, n_lat, *refs):
    corners, refs = refs[:n_lat], refs[n_lat:]
    hist_ref, main, edge_own, edges = refs[0], refs[1], refs[2], refs[3:6]
    out_ref, order_out, *edge = refs[6:]
    wedges = Wedges(sh, None, hist_ref, edges, (main, None, None), edge)
    order_out[...] = jnp.zeros((SUBLANES, LANES), F32)
    for f in range(FIELDS):
        for k in range(HALO):
            put_row(edge[0], f, k, row(edge_own, f, k))

    def take(n, north):
        wedges.take_halos(None if n is None else corners[n], 0, north)

    for_bands(sizes, n_lat, take)
    wedges.edge_coefs()
    wedges.steps(("edges",))
    out_flat = flat_rows(out_ref)

    def put(f, r, value):
        out_flat[f, pl.ds(r, SUBLANES, stride=sh.height), :] = value

    wedges.output(HALO, sh.ext - HALO, put)


def north_kernel(sh, sizes, fold_ref, order_ref, main, main_c, edge, edge_c):
    @pl.when(lax.axis_index("lat") == sizes[0] - 1)
    def _():
        wedges = Wedges(sh, main=(main, main, main_c), edge=(edge, edge_c))
        wedges.take_rows(fold_ref, True)
        wedges.edge_own(edge, north_only=True)
        wedges.take_halos(fold_ref, sh.main, True)
        wedges.edge_coefs()


def last_kernel(sh, sizes, *refs):
    lat_size, _ = sizes
    done_ref, state, begin = refs[0], refs[1:6], refs[6:10]
    out_hbm, late_ref, sems, main, edge = refs[10:]
    height, ext = sh.height, sh.ext
    split = (height - HALO) // SUBLANES * SUBLANES
    at_top = lax.axis_index("lat") == lat_size - 1
    lines = (pl.ds(0, split), pl.ds(split, height - split))

    def copies(source, part):
        return [
            pltpu.make_async_copy(
                source.at[f, :, lines[part]], out_hbm.at[f, :, lines[part]], sems.at[part, f]
            )
            for f in range(STATE)
        ]

    early = copies(done_ref, 0)
    for copy in early:
        copy.start()

    @pl.when(jnp.logical_not(at_top))
    def _():
        rest = copies(done_ref, 1)
        for copy in rest:
            copy.start()
        for copy in rest:
            copy.wait()

    @pl.when(at_top)
    def _():
        wedges = Wedges(
            sh, *state[:2], state[2:], (main, main, begin[1]), (edge, begin[3])
        )
        for f in range(STATE):
            for k in range(HALO):
                put_row(edge, f, k, row(begin[2], f, k))
                at = wedges.at(ext - 1 - k)
                put_row(main, f, at, row(begin[0], f, at))
        wedges.steps(("edges", "north"))

        late_flat, done_flat = flat_rows(late_ref), flat_rows(done_ref)

        def put(f, r, value):
            late_flat[f, pl.ds(r, SUBLANES, stride=height), :] = value

        for f in range(STATE):
            for r in range(split, height - HALO):
                put(f, r, done_flat[f, pl.ds(r, SUBLANES, stride=height), :])
        wedges.output(ext - 2 * HALO, ext - HALO, put)
        rest = copies(late_ref, 1)
        for copy in rest:
            copy.start()
        for copy in rest:
            copy.wait()

    for copy in early:
        copy.wait()


def pair_swaps(size, wrap):
    first = [(i, i ^ 1) for i in range(size)]
    second = []
    for i in range(size):
        j = i + 1 if i % 2 else i - 1
        if wrap or 0 <= j < size:
            second.append((i, j % size))
    return first, second


def vmem(n):
    return [pl.BlockSpec(memory_space=pltpu.VMEM)] * n


def in_hbm(x):
    return pltpu.with_memory_space_constraint(x, pltpu.HBM)


def smem():
    return pl.BlockSpec(memory_space=pltpu.SMEM)


def on_device(mesh_sizes, perturb, background, land_mask, levels, fold_partner):
    lat_size, lon_size = mesh_sizes
    height = perturb.shape[2]
    sh = Shapes(height)
    sizes = (lat_size, lon_size)
    flat = perturb.reshape(STATE, SUBLANES * height, LANES)
    tile = (SUBLANES, LANES)

    def shape(n):
        return pltpu.VMEM((n,) + tile, F32)

    params = pltpu.CompilerParams(vmem_limit_bytes=16 * 1024 * 1024)
    rows = SUBLANES * height
    n_lat = 1 if lat_size == 2 else 2
    side_a, side_b, own, *lat_out = pl.pallas_call(
        functools.partial(sides_kernel, sh, sizes),
        out_shape=(
            shape(sh.side),
            shape(sh.side),
            pltpu.VMEM((FIELDS, rows, LANES), F32),
        )
        + (shape(sh.main),) * n_lat,
        in_specs=[pl.BlockSpec(memory_space=pltpu.HBM)] * 4,
        out_specs=tuple(vmem(3 + n_lat)),
        scratch_shapes=[
            pltpu.VMEM(flat.shape, F32),
            pltpu.VMEM(background.shape, F32),
            pltpu.VMEM(land_mask.shape, jnp.int32),
            pltpu.VMEM(levels.shape, jnp.int32),
            pltpu.SemaphoreType.DMA((3 + STATE,)),
        ],
        compiler_params=params,
        name="sides",
    )(*[in_hbm(v) for v in (flat, background, land_mask, levels)])

    lon_swaps = pair_swaps(lon_size, True)
    got_a, got_b = [lax.ppermute(x, "lon", swap) for x, swap in zip((side_a, side_b), lon_swaps)]

    hist, place, branch = pl.pallas_call(
        functools.partial(middle_kernel, sh, sizes),
        out_shape=(
            pltpu.VMEM((SUBCYCLES, STATE, rows, LANES), F32),
            pltpu.VMEM(tile, jnp.int32),
            jax.ShapeDtypeStruct((1,), jnp.int32),
        ),
        in_specs=vmem(1) + [pl.BlockSpec(memory_space=pltpu.HBM)],
        out_specs=tuple(vmem(2)) + (smem(),),
        scratch_shapes=[
            pltpu.SMEM(fold_partner.shape, jnp.int32),
            pltpu.SemaphoreType.DMA,
        ],
        compiler_params=params,
        name="middle",
    )(own, in_hbm(fold_partner))
    lat_swaps = pair_swaps(lat_size, False)[:n_lat]
    got_lat = [lax.ppermute(x, "lat", swap) for x, swap in zip(lat_out, lat_swaps)]
    fold_band, *lat_corners = pl.pallas_call(
        functools.partial(bands_kernel, sh, sizes),
        out_shape=(shape(sh.band),) + (shape(sh.corners),) * n_lat,
        in_specs=vmem(4),
        out_specs=tuple(vmem(1 + n_lat)),
        compiler_params=params,
        name="bands",
    )(own, got_a, got_b, place)

    edge_rows = SUBLANES * (sh.mid - HALO)
    edge_shapes = (
        pltpu.VMEM((STATE, edge_rows, LANES), F32),
        pltpu.VMEM((edge_rows, LANES), F32),
        pltpu.VMEM((SUBCYCLES, STATE, edge_rows, LANES), F32),
    )
    step_edges = jax.jit(
        pl.pallas_call(
            functools.partial(edges_kernel, sh),
            out_shape=edge_shapes,
            in_specs=vmem(3),
            out_specs=tuple(vmem(3)),
            compiler_params=params,
            name="edges",
        )
    )
    step_wedge_rows = jax.jit(
        pl.pallas_call(
            functools.partial(wedge_rows_kernel, sh, sizes, n_lat),
            out_shape=tuple(pltpu.VMEM(Wedges.SHAPES[n], F32) for n in (0, 0, 1, 2)) + edge_shapes,
            in_specs=vmem(n_lat + 5),
            out_specs=tuple(vmem(7)),
            compiler_params=params,
            name="wedge_rows",
        )
    )
    step_wedge_edges = jax.jit(
        pl.pallas_call(
            functools.partial(wedge_edges_kernel, sh, sizes, n_lat),
            out_shape=(pltpu.VMEM(perturb.shape, F32), pltpu.VMEM(tile, F32)),
            in_specs=vmem(n_lat + 6),
            out_specs=tuple(vmem(2)),
            scratch_shapes=[pltpu.VMEM(x, F32) for x in Wedges.SHAPES[2:]],
            compiler_params=params,
            name="wedge_edges",
        )
    )
    take_north = jax.jit(
        pl.pallas_call(
            functools.partial(north_kernel, sh, sizes),
            out_shape=tuple(pltpu.VMEM(x, F32) for x in Wedges.SHAPES),
            in_specs=vmem(2),
            out_specs=tuple(vmem(4)),
            compiler_params=params,
            name="north",
        )
    )
    top = lat_size - 1

    def rest(q, fold_band, lat_corners, got_lat, own, hist, got_a, got_b):
        across = []
        for m in range(lon_size):
            j = (q - m) % lon_size
            across.append((m * lat_size + top, j * lat_size + top))
        got_fold = lax.ppermute(fold_band, ("lon", "lat"), across)
        got_corners = [lax.ppermute(x, "lat", swap) for x, swap in zip(lat_corners, lat_swaps)]
        edges = step_edges(own, got_a, got_b)
        main, _, _, edge_own, *kept = step_wedge_rows(*got_lat, own, hist, *edges)
        done, order = step_wedge_edges(*got_corners, hist, main, edge_own, *edges)
        return kept, done, take_north(got_fold, order)

    edges, done, beyond = lax.switch(
        branch[0],
        [functools.partial(rest, q) for q in range(lon_size)],
        fold_band,
        lat_corners,
        got_lat,
        own,
        hist,
        got_a,
        got_b,
    )
    return pl.pallas_call(
        functools.partial(last_kernel, sh, sizes),
        out_shape=jax.ShapeDtypeStruct(perturb.shape, F32),
        in_specs=vmem(10),
        out_specs=pl.BlockSpec(memory_space=pltpu.HBM),
        scratch_shapes=[
            pltpu.VMEM(perturb.shape, F32),
            pltpu.SemaphoreType.DMA((2, STATE)),
            pltpu.VMEM(Wedges.SHAPES[0], F32),
            pltpu.VMEM(Wedges.SHAPES[2], F32),
        ],
        compiler_params=params,
        name="last",
    )(done, own, hist, *edges, *beyond)


def solution(mesh):
    placed = (
        P("grp", "dir", "lat", "lon"),
        P("grp", "lat", "lon"),
        P("lat", "lon"),
        P("lat", "lon"),
        P(),
    )
    sizes = (mesh.shape["lat"], mesh.shape["lon"])
    return jax.shard_map(
        functools.partial(on_device, sizes),
        mesh=mesh,
        in_specs=placed,
        out_specs=P("grp", "dir", "lat", "lon"),
        check_vma=False,
    )
```

```python
import functools
from collections import deque

import jax
import jax.numpy as jnp
from jax import lax
from jax.experimental import pallas as pl
from jax.experimental.pallas import tpu as pltpu
from jax.sharding import PartitionSpec as P

SUBCYCLES = 5
NLEV = 90
TIME_STEP = 0.35
HALF_STEP = 0.5 * TIME_STEP

LANES = 128
SUBLANES = 8
HALF = LANES // 2
HALO = 2 * SUBCYCLES
PAIRS = HALO // 2
FIELDS = 4
STATE = 3
COEF = 3
STRIP_SLOTS = HALF // HALO
CORNER_SLOTS = LANES // (2 * HALO)
F32 = jnp.float32


def ceil_div(a, b):
    return -(-a // b)


class Shapes:
    def __init__(self, height):
        self.height = height
        self.ext = height + 2 * HALO
        self.mid = self.ext // 2
        self.fold_first = height
        self.blocks = STATE * PAIRS + ceil_div(PAIRS, 2)
        self.strip_rows = self.mid - HALO
        self.strip_pairs = self.strip_rows // 2
        slots = self.strip_rows * STATE + self.strip_pairs
        self.side = self.blocks + ceil_div(slots, STRIP_SLOTS)
        self.main = STATE * HALO + PAIRS
        self.corners = ceil_div(FIELDS * HALO, CORNER_SLOTS)
        self.band = self.main + self.corners

    def block(self, i, f):
        upper = i // PAIRS
        if f < STATE:
            return f * PAIRS + i % PAIRS, upper, False
        return STATE * PAIRS + i % PAIRS // 2, i % PAIRS % 2, upper == 1

    def strip(self, k, f):
        slot, upper = (k - HALO) * STATE + f, False
        if f == COEF:
            upper = k - HALO >= self.strip_pairs
            slot = self.strip_rows * STATE + (k - HALO) % self.strip_pairs
        return self.blocks + slot // STRIP_SLOTS, HALO * (slot % STRIP_SLOTS), upper

    def corner(self, i, f):
        slot = f * HALO + i
        return self.main + slot // CORNER_SLOTS, 2 * HALO * (slot % CORNER_SLOTS)


def by_register(items, where):
    groups = {}
    for i, f in items:
        v, at = where(i, f)
        groups.setdefault(v, []).append((i, f, at))
    return groups


def roll(x, shift, axis=1):
    shift = shift % x.shape[axis]
    return x if shift == 0 else pltpu.roll(x, shift, axis)


def lane_ids():
    return lax.broadcasted_iota(jnp.int32, (SUBLANES, LANES), 1)


def sublane_ids():
    return lax.broadcasted_iota(jnp.int32, (SUBLANES, LANES), 0)


def run_staged(tasks, window):
    waiting = deque()

    def advance(task):
        try:
            next(task)
        except StopIteration:
            return
        waiting.append(task)

    for task in tasks:
        advance(task)
        while len(waiting) >= window:
            advance(waiting.popleft())
    while waiting:
        advance(waiting.popleft())


def row(ref, f, r):
    return ref[f, SUBLANES * r : SUBLANES * (r + 1), :]


def put_row(ref, f, r, value):
    ref[f, SUBLANES * r : SUBLANES * (r + 1), :] = value


def flat_rows(ref):
    return ref.reshape(ref.shape[0], ref.shape[1] * ref.shape[2], ref.shape[3])


def coef(ref, r, c):
    return jnp.broadcast_to(ref[SUBLANES * r + c : SUBLANES * r + c + 1, :], (SUBLANES, LANES))


def even_lon():
    return jnp.full((SUBLANES, LANES), lax.rem(lax.axis_index("lon"), 2), jnp.int32) == 0


def fold_place(fold_ref, lon_size):
    pivot = fold_ref[0]
    block = pivot // LANES
    rest = pivot - block * LANES
    low = rest < HALF
    place = jnp.where(low, rest + LANES, rest)
    branch = jnp.where(low, block - 1 + lon_size, block)
    return lax.rem(branch, lon_size), place


def pair_coefs(a, b):
    return jnp.where(sublane_ids() < SUBLANES // 2, a, roll(b, SUBLANES // 2, 0))


def lat_rows(sh, own_ref, outs):
    own = functools.partial(row, own_ref)

    def raw_rows(out, first):
        for f in range(STATE):
            for i in range(HALO):
                out[f * HALO + i] = own(f, first + i)
        for i in range(PAIRS):
            out[STATE * HALO + i] = pair_coefs(
                own(COEF, first + i), own(COEF, first + i + PAIRS)
            )

    top = sh.height - HALO
    lat_even = lax.rem(lax.axis_index("lat"), 2) == 0

    @pl.when(lat_even)
    def _():
        raw_rows(outs[0], top)
        if len(outs) > 1:
            raw_rows(outs[1], 0)

    @pl.when(jnp.logical_not(lat_even))
    def _():
        raw_rows(outs[0], 0)
        if len(outs) > 1:
            raw_rows(outs[1], top)


def sides_kernel(sh, sizes, x_hbm, b_hbm, m_hbm, l_hbm, *rest):
    a_out, b_out, own_ref = rest[:3]
    lat_outs, (x_ref, b_ref, m_ref, l_ref, sems) = rest[3:-5], rest[-5:]
    lat_size, _ = sizes
    height = sh.height
    copies = [
        pltpu.make_async_copy(src, dst, sems.at[n])
        for n, (src, dst) in enumerate(
            [(b_hbm, b_ref), (m_hbm, m_ref), (l_hbm, l_ref)]
            + [(x_hbm.at[f], x_ref.at[f]) for f in range(STATE)]
        )
    ]
    for copy in copies:
        copy.start()
    for copy in copies[:3]:
        copy.wait()

    wet = m_ref[...].astype(F32)
    depth = 0.5 + 1.5 * ((l_ref[...] - 1).astype(F32) / (NLEV - 1)) ** 2
    row0 = lax.axis_index("lat") * height
    rows = (row0 + lax.broadcasted_iota(jnp.int32, (height, LANES), 0)).astype(F32)
    coriolis = 0.3 + 0.2 * rows / (height * lat_size)
    planes = [
        HALF_STEP * (wet * (depth + b_ref[0])),
        HALF_STEP * b_ref[1],
        HALF_STEP * b_ref[2],
        wet * (TIME_STEP * coriolis),
        wet,
    ]
    planes += [jnp.zeros_like(wet)] * (SUBLANES - len(planes))
    for c, plane in enumerate(planes):
        for r in range(0, height, SUBLANES):
            own_ref[COEF, pl.ds(SUBLANES * r + c, SUBLANES, stride=SUBLANES), :] = plane[
                r : r + SUBLANES
            ]
    for copy in copies[3:]:
        copy.wait()
    for f in range(STATE):
        for r in range(height):
            put_row(own_ref, f, r, x_ref[f, pl.ds(r, SUBLANES, stride=height), :])

    even = even_lon()
    lane, sub = lane_ids(), sublane_ids()
    low = lane < HALF
    own = functools.partial(row, own_ref)
    top = height - HALO

    def rows_of(f, r):
        return pair_coefs(own(f, r), own(f, r + PAIRS)) if f == COEF else own(f, r)

    def strip_rows_of(f, r, other):
        return pair_coefs(own(f, r), own(f, other)) if f == COEF else own(f, r)

    def block(v, a, b):
        a_up, b_up = roll(a, HALF), roll(b, HALF)
        yield
        east = jnp.where(low, a_up, b)
        west = jnp.where(low, a, b_up)
        a_out[v] = jnp.where(even, east, west)
        b_out[v] = jnp.where(even, west, east)

    def blocks():
        for f in range(STATE):
            for i in range(PAIRS):
                yield block(f * PAIRS + i, own(f, top + i), own(f, top + i + PAIRS))
        for i in range(0, PAIRS, 2):
            v, _, _ = sh.block(i, COEF)
            yield block(v, rows_of(COEF, top + i), rows_of(COEF, top + min(i + 1, PAIRS - 1)))

    slots = {}
    for k in range(HALO, sh.mid):
        for f in range(FIELDS):
            v, at, upper = sh.strip(k, f)
            if not upper:
                slots.setdefault(v, []).append((k, f, at))

    def strips(v):
        parts = []
        for k, f, at in slots[v]:
            ahead = sh.strip_pairs
            r = sh.ext - 1 - k - HALO
            a, b = strip_rows_of(f, k - HALO, k - HALO + ahead), strip_rows_of(f, r, r - ahead)
            end = at - (LANES - HALO)
            a_east, a_west = roll(a, end), roll(a, at)
            near = sh.ext - 1 - k < sh.fold_first
            near_other = sh.ext - 1 - k - ahead < sh.fold_first
            b_east, b_west = roll(b, HALF + end), roll(b, HALF + at)
            if not near:
                b_east, b_west = roll(b, end), roll(b, at)
                if f == COEF and near_other:
                    lower_half = sub < SUBLANES // 2
                    b_east = jnp.where(lower_half, b_east, roll(b, HALF + end))
                    b_west = jnp.where(lower_half, b_west, roll(b, HALF + at))
            parts.append((at, a_east, b_east, a_west, b_west))
        yield
        east = west = jnp.zeros((SUBLANES, LANES), F32)
        for at, ea, eb, wa, wb in parts:
            here = (lane >= at) & (lane < at + HALO)
            there = (lane >= HALF + at) & (lane < HALF + at + HALO)
            east = jnp.where(here, ea, jnp.where(there, eb, east))
            west = jnp.where(here, wa, jnp.where(there, wb, west))
        a_out[v] = jnp.where(even, east, west)
        b_out[v] = jnp.where(even, west, east)

    run_staged(blocks(), 10)
    run_staged([strips(v) for v in sorted(slots)], 2)
    lat_rows(sh, own_ref, lat_outs)


def bands_kernel(sh, sizes, own_ref, ra_ref, rb_ref, place_ref, order_ref, fold_out, *lat_outs):
    lat_size, _ = sizes
    even = even_lon()
    lane, sub = lane_ids(), sublane_ids()
    low = lane < HALF
    own = functools.partial(row, own_ref)
    top = sh.height - HALO

    def got(v, upper):
        a, b = ra_ref[v], rb_ref[v]
        w, e = jnp.where(even, b, a), jnp.where(even, a, b)
        if upper:
            w, e = roll(w, SUBLANES // 2, 0), roll(e, SUBLANES // 2, 0)
        return w, e

    def corners(out, is_top):
        def register(v, items):
            parts = []
            for i, f, at in items:
                if is_top:
                    src, h, upper = sh.block(i, f)
                    w_at, e_at = HALF * h + HALF - HALO, HALF * h
                else:
                    src, w_at, upper = sh.strip(HALO + i, f)
                    e_at = w_at
                w, e = got(src, upper)
                parts.append((at, roll(w, at - w_at), roll(e, at + HALO - e_at)))
            yield
            total = jnp.zeros((SUBLANES, LANES), F32)
            for at, w, e in parts:
                total = jnp.where((lane >= at) & (lane < at + HALO), w, total)
                total = jnp.where((lane >= at + HALO) & (lane < at + 2 * HALO), e, total)
            out[v - sh.main] = total

        groups = by_register([(i, f) for f in range(FIELDS) for i in range(HALO)], sh.corner)
        run_staged([register(v, items) for v, items in groups.items()], 3)

    lat_even = lax.rem(lax.axis_index("lat"), 2) == 0

    @pl.when(lat_even)
    def _():
        corners(lat_outs[0], True)
        if len(lat_outs) > 1:
            corners(lat_outs[1], False)

    @pl.when(jnp.logical_not(lat_even))
    def _():
        corners(lat_outs[0], False)
        if len(lat_outs) > 1:
            corners(lat_outs[1], True)

    @pl.when(lax.axis_index("lat") == lat_size - 1)
    def _():
        where_to = place_ref[...]
        rest = where_to & (LANES - 1)
        eastern = where_to >= LANES
        backwards = (where_to - lane) & (LANES - 1)
        main_own = (eastern & (lane >= rest + 1)) | (jnp.logical_not(eastern) & (lane <= rest))
        upper = (lane >= rest + 1) & (lane <= rest + HALO)
        lower = (lane >= rest + 1 - HALO) & (lane <= rest)
        side_own = (eastern & lower) | (jnp.logical_not(eastern) & upper)
        side_far = (eastern & upper & (lane >= HALF)) | (
            jnp.logical_not(eastern) & lower & (lane < HALF)
        )
        coef_signs = jnp.where((sub == 1) | (sub == 2), -1.0, 1.0).astype(F32)

        def reversed_row(f, i):
            v, h, upper = sh.block(i, f)
            w, e = got(v, upper)
            if h == 0:
                w = roll(w, HALF)
            else:
                e = roll(e, HALF)
            v, at, upper = sh.strip(sh.ext - 1 - sh.fold_first - i, f)
            far_w, far_e = got(v, upper)
            far_w, far_e = roll(far_w, -HALO - at), roll(far_e, -at)
            yield
            both = jnp.where(low, e, w)
            mine = own(f, top + i)
            main = jnp.where(main_own, mine, both)
            side = jnp.where(
                side_own, mine, jnp.where(side_far, jnp.where(low, far_w, far_e), both)
            )
            if f == COEF:
                main, side = main * coef_signs, side * coef_signs
            elif f > 0:
                main, side = -main, -side
            main = jnp.take_along_axis(main, backwards, axis=1)
            side = jnp.take_along_axis(side, backwards, axis=1)
            yield
            j = HALO - 1 - i
            v, at = sh.corner(j, f)
            side = roll(side, at - (LANES - HALO))
            if f < STATE:
                fold_out[f * HALO + j] = main
            elif j < PAIRS:
                v2 = STATE * HALO + j
                fold_out[v2] = jnp.where(sub < SUBLANES // 2, main, fold_out[v2])
            else:
                fold_out[STATE * HALO + j - PAIRS] = roll(main, SUBLANES // 2, 0)
            yield
            here = (lane >= at) & (lane < at + 2 * HALO)
            fold_out[v] = jnp.where(here, side, fold_out[v])

        for v in range(STATE * HALO, sh.band):
            fold_out[v] = jnp.zeros((SUBLANES, LANES), F32)
        run_staged([reversed_row(f, i) for f in range(FIELDS) for i in range(HALO)], 8)


EAST0 = HALF // 2
LAG = 4
WET, NORTH_THICK = 4, 5


def north_sign():
    return jnp.where(lane_ids() < HALF, 1.0, -1.0).astype(F32)


class Sweep:
    def __init__(self, elev, vel, old, coef, put, known=None, mirror=None, down=False):
        self.elev_rows, self.vel_rows = elev, vel
        self.old, self.coef, self.put, self.known, self.mirror = old, coef, put, known, mirror
        self.flux_n, self.rolled, self.new, self.slopes = {}, {}, {}, {}
        self.sign = HALF_STEP * north_sign() if mirror is not None else HALF_STEP
        self.low, self.high = min(elev[0] - 1, vel[0]), max(elev[1], vel[1] - 1)
        self.down = down
        self.length = self.high - self.low + 1 + 2 * LAG

    def flux(self, r):
        lo, hi = self.elev_rows
        if not lo - 1 <= r <= hi or r == self.mirror:
            return
        eta, merid = self.old(0, r), self.old(2, r)
        thick = self.coef(r, 0)
        thick_n = thick if self.mirror is None else self.coef(r, NORTH_THICK)
        self.flux_n[r] = thick_n * merid + self.coef(r, 2) * eta
        if lo <= r < hi:
            east = thick * self.old(1, r) + self.coef(r, 1) * eta
            self.rolled[r] = (roll(east, -1), roll(east, 1))
        if self.mirror is not None and r == self.mirror - 1:
            self.flux_n[r + 1] = -roll(self.flux_n[r], HALF)

    def elevation(self, r):
        lo, hi = self.elev_rows
        if not lo <= r < hi:
            return
        plus, minus = self.rolled.pop(r)
        change = (plus - minus) + (self.flux_n[r + 1] - self.flux_n[r - 1])
        eta = self.coef(r, WET) * (self.old(0, r) - change)
        self.new[r] = eta
        self.put(0, r, eta)
        if self.mirror is not None and r == self.mirror - 1:
            self.new[r + 1] = roll(eta, HALF)

    def get_new(self, r):
        if r not in self.new:
            self.new[r] = self.known(r)
            if self.vel_rows[0] <= r < self.vel_rows[1]:
                self.put(0, r, self.new[r])
        return self.new[r]

    def slope(self, r):
        if self.vel_rows[0] <= r < self.vel_rows[1]:
            eta = self.get_new(r)
            self.slopes[r] = (roll(eta, -1), roll(eta, 1))

    def velocity(self, r):
        if not self.vel_rows[0] <= r < self.vel_rows[1]:
            return
        plus, minus = self.slopes.pop(r)
        wet, turn = self.coef(r, WET), self.coef(r, 3)
        zonal, merid = self.old(1, r), self.old(2, r)
        zonal = wet * (zonal - HALF_STEP * (plus - minus)) + turn * merid
        slope = self.sign * (self.get_new(r + 1) - self.get_new(r - 1))
        merid = wet * (merid - slope) - turn * zonal
        self.put(1, r, zonal)
        self.put(2, r, merid)

    def row_at(self, n):
        return self.high - n if self.down else self.low + n

    def offset_from(self, before):
        ahead = before.high - self.high if self.down else self.low - before.low
        return max(2 * LAG + ahead, 0)

    def advance(self, n):
        self.flux(self.row_at(n))
        self.elevation(self.row_at(n - LAG))
        self.slope(self.row_at(n - LAG))
        self.velocity(self.row_at(n - 2 * LAG))


def run_chains(chains):
    waiting = []
    for chain in chains:
        at = 0
        for n, sweep in enumerate(chain):
            at += sweep.offset_from(chain[n - 1]) if n else 0
            waiting.append((n, at, sweep))
    waiting.sort(key=lambda entry: entry[0])
    for t in range(max(at + sweep.length for _, at, sweep in waiting)):
        for _, at, sweep in waiting:
            if at <= t < at + sweep.length:
                sweep.advance(t - at)


def middle_kernel(sh, sizes, own_ref, p_hbm, hist_ref, place_out, first_out, q_out, p_ref, sem):
    copy = pltpu.make_async_copy(p_hbm, p_ref, sem)
    copy.start()
    chain = []
    for step in range(1, SUBCYCLES + 1):
        source = own_ref if step == 1 else hist_ref.at[step - 2]
        chain.append(
            Sweep(
                (2 * step - 1, sh.height - 2 * step + 1),
                (2 * step, sh.height - 2 * step),
                functools.partial(row, source),
                functools.partial(coef, own_ref.at[COEF]),
                functools.partial(put_row, hist_ref.at[step - 1]),
            )
        )
    run_chains([chain])
    copy.wait()
    first, place = fold_place(p_ref, sizes[1])
    q_out[0] = first
    place_out[...] = jnp.full((SUBLANES, LANES), place, jnp.int32)
    first_out[...] = jnp.full((SUBLANES, LANES), first, jnp.int32)


def edges_kernel(sh, own_ref, ra_ref, rb_ref, start_ref, coef_ref, hist_ref):
    even = even_lon()
    lane = lane_ids()
    low = lane < HALF
    half_lane = lane & (HALF - 1)
    west_halo = half_lane < HALO
    east_own = (half_lane >= EAST0) & (half_lane < EAST0 + 2 * HALO)
    east_halo = (half_lane >= EAST0 + 2 * HALO) & (half_lane < EAST0 + 3 * HALO)
    sign = north_sign()

    def got(v, upper):
        a, b = ra_ref[v], rb_ref[v]
        w, e = jnp.where(even, b, a), jnp.where(even, a, b)
        if upper:
            w, e = roll(w, SUBLANES // 2, 0), roll(e, SUBLANES // 2, 0)
        return w, e

    def edge_row(f, k):
        own = own_columns(row(own_ref, f, k - HALO), row(own_ref, f, sh.ext - 1 - k - HALO))
        v, at, upper = sh.strip(k, f)
        w, e = got(v, upper)
        w, e = roll(w, -at), roll(e, EAST0 + 2 * HALO - at)
        i = sh.ext - 1 - k - sh.fold_first
        if i >= 0:
            v, h, upper = sh.block(i, f)
            w2, e2 = got(v, upper)
            w2 = roll(w2, HALF - (HALF * h + HALF - HALO))
            e2 = roll(e2, HALF + EAST0 + 2 * HALO - HALF * h)
        yield
        value = merge_own(own, low, east_own)
        if i >= 0:
            w, e = jnp.where(low, w, w2), jnp.where(low, e, e2)
        value = jnp.where(west_halo, w, jnp.where(east_halo, e, value))
        if f == COEF:
            put_edge_coefs(coef_ref, k - HALO, value, sign)
        else:
            put_row(start_ref, f, k - HALO, value)

    run_staged([edge_row(f, k) for k in range(HALO, sh.mid) for f in range(FIELDS)], 4)

    rows = sh.mid - HALO
    chain = []
    for step in range(1, SUBCYCLES + 1):
        source = start_ref if step == 1 else hist_ref.at[step - 2]
        chain.append(
            Sweep(
                (2 * step - 1, rows),
                (2 * step, rows),
                functools.partial(row, source),
                functools.partial(coef, coef_ref),
                functools.partial(put_row, hist_ref.at[step - 1]),
                mirror=rows,
                down=True,
            )
        )
    run_chains([chain])


def own_columns(a, b):
    east = EAST0 - (LANES - 2 * HALO)
    return roll(a, HALO), roll(a, east), roll(b, HALF + HALO), roll(b, HALF + east)


def merge_own(parts, low, east_own):
    aw, ae, bw, be = parts
    return jnp.where(east_own, jnp.where(low, ae, be), jnp.where(low, aw, bw))


def put_edge_coefs(ref, k, value, sign):
    at = SUBLANES * k
    thick = value[0:1]
    ref[at : at + 2, :] = value[0:2]
    ref[at + 2 : at + 3, :] = value[2:3] * sign[0:1]
    ref[at + 3 : at + 4, :] = value[3:4]
    ref[at + WET : at + WET + 1, :] = jnp.where(thick > 0, 1.0, 0.0).astype(F32)
    ref[at + NORTH_THICK : at + NORTH_THICK + 1, :] = thick * sign[0:1]


class Wedges:
    def __init__(self, sh, own=None, hist=None, edges=(None,) * 3, main=None, edge=None):
        self.sh, self.own, self.hist = sh, own, hist
        self.start, self.ecoef, self.ehist = edges
        self.main, self.begin, self.main_c = main
        self.edge, self.edge_c = edge or (None, None)
        lane = lane_ids()
        self.low = lane < HALF
        self.half_lane = half = lane & (HALF - 1)
        self.east_own = (half >= EAST0) & (half < EAST0 + 2 * HALO)
        halo = (half < HALO) | ((half >= EAST0 + 2 * HALO) & (half < EAST0 + 3 * HALO))
        self.halo_south, self.halo_north = halo & self.low, halo & (lane >= HALF)
        self.sign = north_sign()

    SHAPES = (
        (STATE, 4 * HALO * SUBLANES, LANES),
        (4 * HALO * SUBLANES, LANES),
        (FIELDS, 2 * HALO * SUBLANES, LANES),
        (HALO * SUBLANES, LANES),
    )

    def at(self, r):
        span = 2 * HALO
        return r if r < span else r - (self.sh.ext - span) + span

    def main_row(self, f, r):
        if f == COEF:
            at = SUBLANES * self.at(r)
            return self.main_c[at : at + SUBLANES, :]
        return row(self.main, f, self.at(r))

    def first_row(self, f, r):
        return self.main_row(f, r) if f == COEF else row(self.begin, f, self.at(r))

    def put_main(self, f, r, value):
        if f < STATE:
            put_row(self.main, f, self.at(r), value)
            return
        at = SUBLANES * self.at(r)
        self.main_c[at : at + SUBLANES, :] = value
        self.main_c[at + WET : at + WET + 1, :] = jnp.where(value[0:1] > 0, 1.0, 0.0).astype(F32)

    def put_halo(self, f, r, value):
        north = r >= self.sh.mid
        k, mask = (self.sh.ext - 1 - r, self.halo_north) if north else (r, self.halo_south)
        put_row(self.edge, f, k, jnp.where(mask, value, row(self.edge, f, k)))

    def band(self, north):
        return [self.sh.ext - HALO + i if north else i for i in range(HALO)]

    def take_rows(self, ref, north):
        for f in range(FIELDS):
            for i, r in enumerate(self.band(north)):
                if ref is None:
                    value = jnp.zeros((SUBLANES, LANES), F32)
                elif f < STATE:
                    value = ref[f * HALO + i]
                else:
                    value = ref[STATE * HALO + i % PAIRS]
                    value = value if i < PAIRS else roll(value, SUBLANES // 2, 0)
                self.put_main(f, r, value)
                if f < STATE and self.begin is not self.main:
                    put_row(self.begin, f, self.at(r), value)

    def take_halos(self, ref, first, north):
        base = HALF if north else 0
        if ref is None:
            for f in range(FIELDS):
                for r in self.band(north):
                    self.put_halo(f, r, jnp.zeros((SUBLANES, LANES), F32))
            return

        def band_row(f, i, r):
            v, at = self.sh.corner(i, f)
            v = ref[v - self.sh.main + first]
            w, e = roll(v, base - at), roll(v, base + EAST0 + HALO - at)
            yield
            self.put_halo(f, r, jnp.where(self.half_lane < HALO, w, e))

        rows = list(enumerate(self.band(north)))
        run_staged([band_row(f, i, r) for f in range(FIELDS) for i, r in rows], 16)

    def edge_own(self, out, north_only=False):
        def edge_row(f, k):
            b = self.first_row(f, self.sh.ext - 1 - k)
            parts = own_columns(b if north_only else self.first_row(f, k), b)
            yield
            put_row(out, f, k, merge_own(parts, self.low, self.east_own))

        run_staged([edge_row(f, k) for k in range(HALO) for f in range(FIELDS)], 8)

    def edge_coefs(self):
        for k in range(HALO):
            put_edge_coefs(self.edge_c, k, row(self.edge, COEF, k), self.sign)

    def steps(self, sides):
        ext = self.sh.ext

        def put_edge(f, k, value):
            put_row(self.edge, f, k, value)

        def edge_coef(k, c):
            return coef(self.edge_c, k, c) if k < HALO else coef(self.ecoef, k - HALO, c)

        def main_coef(r, c):
            if HALO <= r < ext - HALO:
                return coef(self.own.at[COEF], r - HALO, c)
            return coef(self.main_c, self.at(r), c)

        edges, south, north = [], [], []
        for step in range(1, SUBCYCLES + 1):
            first, ready = 2 * step - 2, 2 * step + HALO - 2

            def old_main(f, r, step=step, ready=ready):
                if ready <= r < ext - ready:
                    return row(self.own if step == 1 else self.hist.at[step - 2], f, r - HALO)
                return self.main_row(f, r)

            def old_edge(f, k, step=step, ready=ready):
                if k >= ready:
                    return row(self.start if step == 1 else self.ehist.at[step - 2], f, k - HALO)
                return row(self.edge, f, k)

            def known_main(r, step=step):
                return row(self.hist.at[step - 1], 0, r - HALO)

            def known_edge(k, step=step):
                return row(self.ehist.at[step - 1], 0, k - HALO)

            elev, vel = (first + 1, ready + 1), (first + 2, ready + 2)
            edges.append(
                Sweep(
                    elev,
                    vel,
                    old_edge,
                    edge_coef,
                    put_edge,
                    known_edge,
                    mirror=self.sh.mid,
                    down=True,
                )
            )
            south.append(
                Sweep(elev, vel, old_main, main_coef, self.put_main, known_main, down=True)
            )
            elev, vel = [(ext - rows[1], ext - rows[0]) for rows in (elev, vel)]
            north.append(Sweep(elev, vel, old_main, main_coef, self.put_main, known_main))
        chains = {"edges": edges, "south": south, "north": north}
        run_chains([chains[name] for name in sides])

    def output(self, first, last, put):
        ext, mid, ready = self.sh.ext, self.sh.mid, 2 * HALO
        final, e_final = self.hist.at[SUBCYCLES - 1], self.ehist.at[SUBCYCLES - 1]
        lane = lane_ids()

        def output_row(f, r):
            k, h = (r, 0) if r < mid else (ext - 1 - r, HALF)
            v = row(self.edge, f, k) if k < ready else row(e_final, f, k - HALO)
            w, e = roll(v, -(h + HALO)), roll(v, LANES - HALO - (h + EAST0 + HALO))
            yield
            inner = ready <= r < ext - ready
            v = row(final, f, r - HALO) if inner else self.main_row(f, r)
            v = jnp.where(lane < HALO, w, jnp.where(lane >= LANES - HALO, e, v))
            put(f, r - HALO, v)

        run_staged([output_row(f, r) for f in range(STATE) for r in range(first, last)], 10)


def for_bands(sizes, n_lat, take):
    lat_size, _ = sizes
    lat = lax.axis_index("lat")
    lat_even = lax.rem(lat, 2) == 0
    lat_odd = jnp.logical_not(lat_even)
    at_top = lat == lat_size - 1
    pl.when(at_top)(lambda: take(None, True))
    pl.when(lat == 0)(lambda: take(None, False))
    pl.when(lat_even)(lambda: take(0, True))
    pl.when(lat_odd)(lambda: take(0, False))
    if n_lat == 2:
        pl.when(lat_odd & jnp.logical_not(at_top))(lambda: take(1, True))
        pl.when(lat_even & (lat > 0))(lambda: take(1, False))


def wedge_rows_kernel(sh, sizes, n_lat, *refs):
    bands, (own_ref, hist_ref, main, edge_out, order_out, begin, main_c) = (
        refs[:n_lat],
        refs[n_lat:],
    )
    wedges = Wedges(sh, own_ref, hist_ref, main=(main, begin, main_c))
    order_out[...] = jnp.zeros((SUBLANES, LANES), F32)

    def take(n, north):
        wedges.take_rows(None if n is None else bands[n], north)

    for_bands(sizes, n_lat, take)
    wedges.edge_own(edge_out)
    wedges.steps(("south", "north"))


def wedge_edges_kernel(sh, sizes, n_lat, *refs):
    corners, refs = refs[:n_lat], refs[n_lat:]
    hist_ref, main, edge_own, edges = refs[0], refs[1], refs[2], refs[3:6]
    (out_ref, order_out), kept, edge = refs[6:8], refs[8:11], refs[11:]
    wedges = Wedges(sh, None, hist_ref, edges, (main, None, None), edge)
    order_out[...] = jnp.zeros((SUBLANES, LANES), F32)
    for f in range(FIELDS):
        for k in range(HALO):
            put_row(edge[0], f, k, row(edge_own, f, k))

    for k in range(HALO + 1):
        at = slice(SUBLANES * k, SUBLANES * (k + 1))
        kept[1][at, :] = edges[1][at, :]
    for f in range(STATE):
        for k in range(2):
            put_row(kept[0], f, k, row(edges[0], f, k))
        for n in range(SUBCYCLES):
            for k in range(2 * n + 1, 2 * n + 4):
                put_row(kept[2].at[n], f, k, row(edges[2].at[n], f, k))

    def take(n, north):
        wedges.take_halos(None if n is None else corners[n], 0, north)

    for_bands(sizes, n_lat, take)
    wedges.edge_coefs()
    wedges.steps(("edges",))
    out_flat = flat_rows(out_ref)

    def put(f, r, value):
        out_flat[f, pl.ds(r, SUBLANES, stride=sh.height), :] = value

    wedges.output(HALO, sh.ext - HALO, put)


def north_kernel(sh, sizes, got_ref, sent_ref, first_ref, order_ref, *outs):
    main, main_c, edge, edge_c = outs[:4]
    fold_ref = outs[4]
    lat_size, lon_size = sizes

    @pl.when(lax.axis_index("lat") == lat_size - 1)
    def _():
        facing = lax.rem(first_ref[...] - lax.axis_index("lon") + lon_size, lon_size)
        itself = facing == lax.axis_index("lon")
        for v in range(sh.band):
            fold_ref[v] = jnp.where(itself, sent_ref[v], got_ref[v])
        wedges = Wedges(sh, main=(main, main, main_c), edge=(edge, edge_c))
        wedges.take_rows(fold_ref, True)
        wedges.edge_own(edge, north_only=True)
        wedges.take_halos(fold_ref, sh.main, True)
        wedges.edge_coefs()


def last_kernel(sh, sizes, *refs):
    lat_size, _ = sizes
    done_ref, state, begin = refs[0], refs[1:6], refs[6:10]
    out_hbm, late_ref, sems, main, edge = refs[10:]
    height, ext = sh.height, sh.ext
    split = (height - HALO) // SUBLANES * SUBLANES
    at_top = lax.axis_index("lat") == lat_size - 1
    lines = (pl.ds(0, split), pl.ds(split, height - split))

    def copies(source, part):
        return [
            pltpu.make_async_copy(
                source.at[f, :, lines[part]], out_hbm.at[f, :, lines[part]], sems.at[part, f]
            )
            for f in range(STATE)
        ]

    early = copies(done_ref, 0)
    for copy in early:
        copy.start()

    @pl.when(jnp.logical_not(at_top))
    def _():
        rest = copies(done_ref, 1)
        for copy in rest:
            copy.start()
        for copy in rest:
            copy.wait()

    @pl.when(at_top)
    def _():
        wedges = Wedges(
            sh, *state[:2], state[2:], (main, main, begin[1]), (edge, begin[3])
        )
        for f in range(STATE):
            for k in range(HALO):
                put_row(edge, f, k, row(begin[2], f, k))
                at = wedges.at(ext - 1 - k)
                put_row(main, f, at, row(begin[0], f, at))
        wedges.steps(("edges", "north"))

        late_flat, done_flat = flat_rows(late_ref), flat_rows(done_ref)

        def put(f, r, value):
            late_flat[f, pl.ds(r, SUBLANES, stride=height), :] = value

        for f in range(STATE):
            for r in range(split, height - HALO):
                put(f, r, done_flat[f, pl.ds(r, SUBLANES, stride=height), :])
        wedges.output(ext - 2 * HALO, ext - HALO, put)
        rest = copies(late_ref, 1)
        for copy in rest:
            copy.start()
        for copy in rest:
            copy.wait()

    for copy in early:
        copy.wait()


def pair_swaps(size, wrap):
    first = [(i, i ^ 1) for i in range(size)]
    second = []
    for i in range(size):
        j = i + 1 if i % 2 else i - 1
        if wrap or 0 <= j < size:
            second.append((i, j % size))
    return first, second


def vmem(n):
    return [pl.BlockSpec(memory_space=pltpu.VMEM)] * n


def in_hbm(x):
    return pltpu.with_memory_space_constraint(x, pltpu.HBM)


def smem():
    return pl.BlockSpec(memory_space=pltpu.SMEM)


def on_device(mesh_sizes, perturb, background, land_mask, levels, fold_partner):
    lat_size, lon_size, dir_size = mesh_sizes
    height = perturb.shape[2]
    sh = Shapes(height)
    sizes = (lat_size, lon_size)
    flat = perturb.reshape(STATE, SUBLANES * height, LANES)
    tile = (SUBLANES, LANES)

    def shape(n):
        return pltpu.VMEM((n,) + tile, F32)

    params = pltpu.CompilerParams(vmem_limit_bytes=16 * 1024 * 1024)
    rows = SUBLANES * height
    n_lat = 1 if lat_size == 2 else 2
    side_a, side_b, own, *lat_out = pl.pallas_call(
        functools.partial(sides_kernel, sh, sizes),
        out_shape=(
            shape(sh.side),
            shape(sh.side),
            pltpu.VMEM((FIELDS, rows, LANES), F32),
        )
        + (shape(sh.main),) * n_lat,
        in_specs=[pl.BlockSpec(memory_space=pltpu.HBM)] * 4,
        out_specs=tuple(vmem(3 + n_lat)),
        scratch_shapes=[
            pltpu.VMEM(flat.shape, F32),
            pltpu.VMEM(background.shape, F32),
            pltpu.VMEM(land_mask.shape, jnp.int32),
            pltpu.VMEM(levels.shape, jnp.int32),
            pltpu.SemaphoreType.DMA((3 + STATE,)),
        ],
        compiler_params=params,
        name="sides",
    )(*[in_hbm(v) for v in (flat, background, land_mask, levels)])

    lon_swaps = pair_swaps(lon_size, True)
    got_a, got_b = [lax.ppermute(x, "lon", swap) for x, swap in zip((side_a, side_b), lon_swaps)]

    hist, place, first, branch = pl.pallas_call(
        functools.partial(middle_kernel, sh, sizes),
        out_shape=(
            pltpu.VMEM((SUBCYCLES, STATE, rows, LANES), F32),
            pltpu.VMEM(tile, jnp.int32),
            pltpu.VMEM(tile, jnp.int32),
            jax.ShapeDtypeStruct((1,), jnp.int32),
        ),
        in_specs=vmem(1) + [pl.BlockSpec(memory_space=pltpu.HBM)],
        out_specs=tuple(vmem(3)) + (smem(),),
        scratch_shapes=[
            pltpu.SMEM(fold_partner.shape, jnp.int32),
            pltpu.SemaphoreType.DMA,
        ],
        compiler_params=params,
        name="middle",
    )(own, in_hbm(fold_partner))
    lat_swaps = pair_swaps(lat_size, False)[:n_lat]
    got_lat = [lax.ppermute(x, "lat", swap) for x, swap in zip(lat_out, lat_swaps)]
    wedge_main, edge_own, order = pl.pallas_call(
        functools.partial(wedge_rows_kernel, sh, sizes, n_lat),
        out_shape=(
            pltpu.VMEM(Wedges.SHAPES[0], F32),
            pltpu.VMEM(Wedges.SHAPES[2], F32),
            pltpu.VMEM(tile, F32),
        ),
        in_specs=vmem(n_lat + 2),
        out_specs=tuple(vmem(3)),
        scratch_shapes=[pltpu.VMEM(x, F32) for x in Wedges.SHAPES[:2]],
        compiler_params=params,
        name="wedge_rows",
    )(*got_lat, own, hist)
    fold_band, *lat_corners = pl.pallas_call(
        functools.partial(bands_kernel, sh, sizes),
        out_shape=(shape(sh.band),) + (shape(sh.corners),) * n_lat,
        in_specs=vmem(5),
        out_specs=tuple(vmem(1 + n_lat)),
        compiler_params=params,
        name="bands",
    )(own, got_a, got_b, place, order)

    edge_rows = SUBLANES * (sh.mid - HALO)
    edge_shapes = (
        pltpu.VMEM((STATE, edge_rows, LANES), F32),
        pltpu.VMEM((edge_rows, LANES), F32),
        pltpu.VMEM((SUBCYCLES, STATE, edge_rows, LANES), F32),
    )
    step_edges = jax.jit(
        pl.pallas_call(
            functools.partial(edges_kernel, sh),
            out_shape=edge_shapes,
            in_specs=vmem(3),
            out_specs=tuple(vmem(3)),
            compiler_params=params,
            name="edges",
        )
    )
    step_wedge_edges = jax.jit(
        pl.pallas_call(
            functools.partial(wedge_edges_kernel, sh, sizes, n_lat),
            out_shape=(pltpu.VMEM(perturb.shape, F32), pltpu.VMEM(tile, F32)) + edge_shapes,
            in_specs=vmem(n_lat + 6),
            out_specs=tuple(vmem(5)),
            scratch_shapes=[pltpu.VMEM(x, F32) for x in Wedges.SHAPES[2:]],
            compiler_params=params,
            name="wedge_edges",
        )
    )
    take_north = jax.jit(
        pl.pallas_call(
            functools.partial(north_kernel, sh, sizes),
            out_shape=tuple(pltpu.VMEM(x, F32) for x in Wedges.SHAPES),
            in_specs=vmem(4),
            out_specs=tuple(vmem(4)),
            scratch_shapes=[pltpu.VMEM((sh.band,) + tile, F32)],
            compiler_params=params,
            name="north",
        )
    )
    def rest(q, fold_band, lat_corners, wedge_main, edge_own, own, hist, got_a, got_b, first):
        across = []
        for m in range(lon_size):
            j = (q - m) % lon_size
            for a in range(lat_size):
                for d in range(dir_size):
                    source, target = (m, a, d), (j, a, d if j != m else d ^ 1)
                    across.append(
                        tuple((x * lat_size + y) * dir_size + z for x, y, z in (source, target))
                    )
        got_fold = lax.ppermute(fold_band, ("lon", "lat", "dir"), across)
        got_corners = [lax.ppermute(x, "lat", swap) for x, swap in zip(lat_corners, lat_swaps)]
        edges = step_edges(own, got_a, got_b)
        done, order, *kept = step_wedge_edges(*got_corners, hist, wedge_main, edge_own, *edges)
        return kept, done, take_north(got_fold, fold_band, first, order)

    edges, done, beyond = lax.switch(
        branch[0],
        [functools.partial(rest, q) for q in range(lon_size)],
        fold_band,
        lat_corners,
        wedge_main,
        edge_own,
        own,
        hist,
        got_a,
        got_b,
        first,
    )
    return pl.pallas_call(
        functools.partial(last_kernel, sh, sizes),
        out_shape=jax.ShapeDtypeStruct(perturb.shape, F32),
        in_specs=vmem(10),
        out_specs=pl.BlockSpec(memory_space=pltpu.HBM),
        scratch_shapes=[
            pltpu.VMEM(perturb.shape, F32),
            pltpu.SemaphoreType.DMA((2, STATE)),
            pltpu.VMEM(Wedges.SHAPES[0], F32),
            pltpu.VMEM(Wedges.SHAPES[2], F32),
        ],
        compiler_params=params,
        name="last",
    )(done, own, hist, *edges, *beyond)


def solution(mesh):
    placed = (
        P("grp", "dir", "lat", "lon"),
        P("grp", "lat", "lon"),
        P("lat", "lon"),
        P("lat", "lon"),
        P(),
    )
    sizes = tuple(mesh.shape[axis] for axis in ("lat", "lon", "dir"))
    return jax.shard_map(
        functools.partial(on_device, sizes),
        mesh=mesh,
        in_specs=placed,
        out_specs=P("grp", "dir", "lat", "lon"),
        check_vma=False,
    )
```

```python
import functools
from collections import deque

import jax
import jax.numpy as jnp
from jax import lax
from jax.experimental import pallas as pl
from jax.experimental.pallas import tpu as pltpu
from jax.sharding import PartitionSpec as P

SUBCYCLES = 5
NLEV = 90
TIME_STEP = 0.35
HALF_STEP = 0.5 * TIME_STEP

LANES = 128
SUBLANES = 8
HALF = LANES // 2
HALO = 2 * SUBCYCLES
PAIRS = HALO // 2
FIELDS = 4
STATE = 3
COEF = 3
STRIP_SLOTS = HALF // HALO
CORNER_SLOTS = LANES // (2 * HALO)
F32 = jnp.float32


def ceil_div(a, b):
    return -(-a // b)


class Shapes:
    def __init__(self, height):
        self.height = height
        self.ext = height + 2 * HALO
        self.mid = self.ext // 2
        self.fold_first = height
        self.blocks = STATE * PAIRS + ceil_div(PAIRS, 2)
        self.strip_rows = self.mid - HALO
        self.strip_pairs = self.strip_rows // 2
        slots = self.strip_rows * STATE + self.strip_pairs
        self.side = self.blocks + ceil_div(slots, STRIP_SLOTS)
        self.main = STATE * HALO + PAIRS
        self.corners = ceil_div(FIELDS * PAIRS, CORNER_SLOTS)
        self.band = self.main + self.corners

    def block(self, i, f):
        upper = i // PAIRS
        if f < STATE:
            return f * PAIRS + i % PAIRS, upper, False
        return STATE * PAIRS + i % PAIRS // 2, i % PAIRS % 2, upper == 1

    def strip(self, k, f):
        slot, upper = (k - HALO) * STATE + f, False
        if f == COEF:
            upper = k - HALO >= self.strip_pairs
            slot = self.strip_rows * STATE + (k - HALO) % self.strip_pairs
        return self.blocks + slot // STRIP_SLOTS, HALO * (slot % STRIP_SLOTS), upper

    def corner(self, i, f):
        slot = f * PAIRS + min(i, HALO - 1 - i)
        return self.main + slot // CORNER_SLOTS, 2 * HALO * (slot % CORNER_SLOTS)

    @staticmethod
    def away(d):
        return d if d > PAIRS else 0

    @staticmethod
    def corner_lanes(d):
        west, east = (d, HALO - 1), (HALO, 2 * HALO - 1 - d)
        if d > PAIRS:
            west, east = (0, HALO - 1 - d), (HALO + d, 2 * HALO - 1)
        return west, east


def by_register(items, where):
    groups = {}
    for i, f in items:
        v, at = where(i, f)
        groups.setdefault(v, []).append((i, f, at))
    return groups


def roll(x, shift, axis=1):
    shift = shift % x.shape[axis]
    return x if shift == 0 else pltpu.roll(x, shift, axis)


def lane_ids():
    return lax.broadcasted_iota(jnp.int32, (SUBLANES, LANES), 1)


def sublane_ids():
    return lax.broadcasted_iota(jnp.int32, (SUBLANES, LANES), 0)


def run_staged(tasks, window):
    waiting = deque()

    def advance(task):
        try:
            next(task)
        except StopIteration:
            return
        waiting.append(task)

    for task in tasks:
        advance(task)
        while len(waiting) >= window:
            advance(waiting.popleft())
    while waiting:
        advance(waiting.popleft())


def row(ref, f, r):
    return ref[f, SUBLANES * r : SUBLANES * (r + 1), :]


def put_row(ref, f, r, value):
    ref[f, SUBLANES * r : SUBLANES * (r + 1), :] = value


def flat_rows(ref):
    return ref.reshape(ref.shape[0], ref.shape[1] * ref.shape[2], ref.shape[3])


def coef(ref, r, c):
    return jnp.broadcast_to(ref[SUBLANES * r + c : SUBLANES * r + c + 1, :], (SUBLANES, LANES))


def even_lon():
    return jnp.full((SUBLANES, LANES), lax.rem(lax.axis_index("lon"), 2), jnp.int32) == 0


def fold_place(fold_ref, lon_size):
    pivot = fold_ref[0]
    block = pivot // LANES
    rest = pivot - block * LANES
    low = rest < HALF
    place = jnp.where(low, rest + LANES, rest)
    branch = jnp.where(low, block - 1 + lon_size, block)
    return lax.rem(branch, lon_size), place


def pair_coefs(a, b):
    return jnp.where(sublane_ids() < SUBLANES // 2, a, roll(b, SUBLANES // 2, 0))


def lat_rows(sh, own_ref, outs):
    own = functools.partial(row, own_ref)

    def raw_rows(out, first):
        for f in range(STATE):
            for i in range(HALO):
                out[f * HALO + i] = own(f, first + i)
        for i in range(PAIRS):
            out[STATE * HALO + i] = pair_coefs(
                own(COEF, first + i), own(COEF, first + i + PAIRS)
            )

    top = sh.height - HALO
    lat_even = lax.rem(lax.axis_index("lat"), 2) == 0

    @pl.when(lat_even)
    def _():
        raw_rows(outs[0], top)
        if len(outs) > 1:
            raw_rows(outs[1], 0)

    @pl.when(jnp.logical_not(lat_even))
    def _():
        raw_rows(outs[0], 0)
        if len(outs) > 1:
            raw_rows(outs[1], top)


def sides_kernel(sh, sizes, x_hbm, b_hbm, m_hbm, l_hbm, *rest):
    a_out, b_out, own_ref = rest[:3]
    lat_outs, (x_ref, b_ref, m_ref, l_ref, sems) = rest[3:-5], rest[-5:]
    lat_size, _ = sizes
    height = sh.height
    copies = [
        pltpu.make_async_copy(src, dst, sems.at[n])
        for n, (src, dst) in enumerate(
            [(b_hbm, b_ref), (m_hbm, m_ref), (l_hbm, l_ref)]
            + [(x_hbm.at[f], x_ref.at[f]) for f in range(STATE)]
        )
    ]
    for copy in copies:
        copy.start()
    for copy in copies[:3]:
        copy.wait()

    wet = m_ref[...].astype(F32)
    depth = 0.5 + 1.5 * ((l_ref[...] - 1).astype(F32) / (NLEV - 1)) ** 2
    row0 = lax.axis_index("lat") * height
    rows = (row0 + lax.broadcasted_iota(jnp.int32, (height, LANES), 0)).astype(F32)
    coriolis = 0.3 + 0.2 * rows / (height * lat_size)
    planes = [
        HALF_STEP * (wet * (depth + b_ref[0])),
        HALF_STEP * b_ref[1],
        HALF_STEP * b_ref[2],
        wet * (TIME_STEP * coriolis),
        wet,
    ]
    planes += [jnp.zeros_like(wet)] * (SUBLANES - len(planes))
    for c, plane in enumerate(planes):
        for r in range(0, height, SUBLANES):
            own_ref[COEF, pl.ds(SUBLANES * r + c, SUBLANES, stride=SUBLANES), :] = plane[
                r : r + SUBLANES
            ]
    for copy in copies[3:]:
        copy.wait()
    for f in range(STATE):
        for r in range(height):
            put_row(own_ref, f, r, x_ref[f, pl.ds(r, SUBLANES, stride=height), :])

    even = even_lon()
    lane, sub = lane_ids(), sublane_ids()
    low = lane < HALF
    own = functools.partial(row, own_ref)
    top = height - HALO

    def rows_of(f, r):
        return pair_coefs(own(f, r), own(f, r + PAIRS)) if f == COEF else own(f, r)

    def strip_rows_of(f, r, other):
        return pair_coefs(own(f, r), own(f, other)) if f == COEF else own(f, r)

    def block(v, a, b):
        a_up, b_up = roll(a, HALF), roll(b, HALF)
        yield
        east = jnp.where(low, a_up, b)
        west = jnp.where(low, a, b_up)
        a_out[v] = jnp.where(even, east, west)
        b_out[v] = jnp.where(even, west, east)

    def blocks():
        for f in range(STATE):
            for i in range(PAIRS):
                yield block(f * PAIRS + i, own(f, top + i), own(f, top + i + PAIRS))
        for i in range(0, PAIRS, 2):
            v, _, _ = sh.block(i, COEF)
            yield block(v, rows_of(COEF, top + i), rows_of(COEF, top + min(i + 1, PAIRS - 1)))

    slots = {}
    for k in range(HALO, sh.mid):
        for f in range(FIELDS):
            v, at, upper = sh.strip(k, f)
            if not upper:
                slots.setdefault(v, []).append((k, f, at))

    def strips(v):
        parts = []
        for k, f, at in slots[v]:
            ahead = sh.strip_pairs
            r = sh.ext - 1 - k - HALO
            a, b = strip_rows_of(f, k - HALO, k - HALO + ahead), strip_rows_of(f, r, r - ahead)
            end = at - (LANES - HALO)
            a_east, a_west = roll(a, end), roll(a, at)
            near = sh.ext - 1 - k < sh.fold_first
            near_other = sh.ext - 1 - k - ahead < sh.fold_first
            b_east, b_west = roll(b, HALF + end), roll(b, HALF + at)
            if not near:
                b_east, b_west = roll(b, end), roll(b, at)
                if f == COEF and near_other:
                    lower_half = sub < SUBLANES // 2
                    b_east = jnp.where(lower_half, b_east, roll(b, HALF + end))
                    b_west = jnp.where(lower_half, b_west, roll(b, HALF + at))
            parts.append((at, a_east, b_east, a_west, b_west))
        yield
        east = west = jnp.zeros((SUBLANES, LANES), F32)
        for at, ea, eb, wa, wb in parts:
            here = (lane >= at) & (lane < at + HALO)
            there = (lane >= HALF + at) & (lane < HALF + at + HALO)
            east = jnp.where(here, ea, jnp.where(there, eb, east))
            west = jnp.where(here, wa, jnp.where(there, wb, west))
        a_out[v] = jnp.where(even, east, west)
        b_out[v] = jnp.where(even, west, east)

    run_staged(blocks(), 10)
    run_staged([strips(v) for v in sorted(slots)], 2)
    lat_rows(sh, own_ref, lat_outs)


def bands_kernel(sh, sizes, own_ref, ra_ref, rb_ref, place_ref, order_ref, fold_out, *lat_outs):
    lat_size, _ = sizes
    even = even_lon()
    lane, sub = lane_ids(), sublane_ids()
    low = lane < HALF
    own = functools.partial(row, own_ref)
    top = sh.height - HALO

    def got(v, upper):
        a, b = ra_ref[v], rb_ref[v]
        w, e = jnp.where(even, b, a), jnp.where(even, a, b)
        if upper:
            w, e = roll(w, SUBLANES // 2, 0), roll(e, SUBLANES // 2, 0)
        return w, e

    def corners(out, is_top):
        def register(v, items):
            parts = []
            for i, f, at in items:
                if is_top:
                    src, h, upper = sh.block(i, f)
                    w_at, e_at = HALF * h + HALF - HALO, HALF * h
                else:
                    src, w_at, upper = sh.strip(HALO + i, f)
                    e_at = w_at
                w, e = got(src, upper)
                d = HALO - i if is_top else i + 1
                out_by = sh.away(d)
                w, e = roll(w, at - w_at - out_by), roll(e, at + HALO - e_at + out_by)
                parts.append((at, d, w, e))
            yield
            total = jnp.zeros((SUBLANES, LANES), F32)
            for at, d, w, e in parts:
                for (start, end), value in zip(sh.corner_lanes(d), (w, e)):
                    if start <= end:
                        total = jnp.where((lane >= at + start) & (lane <= at + end), value, total)
            out[v - sh.main] = total

        groups = by_register([(i, f) for f in range(FIELDS) for i in range(HALO)], sh.corner)
        run_staged([register(v, items) for v, items in groups.items()], 3)

    lat_even = lax.rem(lax.axis_index("lat"), 2) == 0

    @pl.when(lat_even)
    def _():
        corners(lat_outs[0], True)
        if len(lat_outs) > 1:
            corners(lat_outs[1], False)

    @pl.when(jnp.logical_not(lat_even))
    def _():
        corners(lat_outs[0], False)
        if len(lat_outs) > 1:
            corners(lat_outs[1], True)

    @pl.when(lax.axis_index("lat") == lat_size - 1)
    def _():
        where_to = place_ref[...]
        rest = where_to & (LANES - 1)
        eastern = where_to >= LANES
        backwards = (where_to - lane) & (LANES - 1)
        main_own = (eastern & (lane >= rest + 1)) | (jnp.logical_not(eastern) & (lane <= rest))
        upper = (lane >= rest + 1) & (lane <= rest + HALO)
        lower = (lane >= rest + 1 - HALO) & (lane <= rest)
        side_own = (eastern & lower) | (jnp.logical_not(eastern) & upper)
        side_far = (eastern & upper & (lane >= HALF)) | (
            jnp.logical_not(eastern) & lower & (lane < HALF)
        )
        coef_signs = jnp.where((sub == 1) | (sub == 2), -1.0, 1.0).astype(F32)

        def reversed_row(f, i):
            v, h, upper = sh.block(i, f)
            w, e = got(v, upper)
            if h == 0:
                w = roll(w, HALF)
            else:
                e = roll(e, HALF)
            v, at, upper = sh.strip(sh.ext - 1 - sh.fold_first - i, f)
            far_w, far_e = got(v, upper)
            far_w, far_e = roll(far_w, -HALO - at), roll(far_e, -at)
            yield
            both = jnp.where(low, e, w)
            mine = own(f, top + i)
            main = jnp.where(main_own, mine, both)
            side = jnp.where(
                side_own, mine, jnp.where(side_far, jnp.where(low, far_w, far_e), both)
            )
            if f == COEF:
                main, side = main * coef_signs, side * coef_signs
            elif f > 0:
                main, side = -main, -side
            main = jnp.take_along_axis(main, backwards, axis=1)
            side = jnp.take_along_axis(side, backwards, axis=1)
            yield
            j = HALO - 1 - i
            v, at = sh.corner(j, f)
            d = j + 1
            out_by = sh.away(d)
            moves = (-out_by, out_by) if out_by else (0,)
            moved = [roll(side, at - (LANES - HALO) + by) for by in moves]
            if f < STATE:
                fold_out[f * HALO + j] = main
            elif j < PAIRS:
                v2 = STATE * HALO + j
                fold_out[v2] = jnp.where(sub < SUBLANES // 2, main, fold_out[v2])
            else:
                fold_out[STATE * HALO + j - PAIRS] = roll(main, SUBLANES // 2, 0)
            yield
            total = fold_out[v]
            for (start, end), value in zip(sh.corner_lanes(d), (moved[0], moved[-1])):
                if start <= end:
                    total = jnp.where((lane >= at + start) & (lane <= at + end), value, total)
            fold_out[v] = total

        for v in range(STATE * HALO, sh.band):
            fold_out[v] = jnp.zeros((SUBLANES, LANES), F32)
        run_staged([reversed_row(f, i) for f in range(FIELDS) for i in range(HALO)], 14)


EAST0 = HALF // 2
LAG = 4
WET, NORTH_THICK = 4, 5


def north_sign():
    return jnp.where(lane_ids() < HALF, 1.0, -1.0).astype(F32)


class Sweep:
    def __init__(self, elev, vel, old, coef, put, known=None, mirror=None, down=False):
        self.elev_rows, self.vel_rows = elev, vel
        self.old, self.coef, self.put, self.known, self.mirror = old, coef, put, known, mirror
        self.flux_n, self.rolled, self.new, self.slopes = {}, {}, {}, {}
        self.sign = HALF_STEP * north_sign() if mirror is not None else HALF_STEP
        self.low, self.high = min(elev[0] - 1, vel[0]), max(elev[1], vel[1] - 1)
        self.down = down
        self.length = self.high - self.low + 1 + 2 * LAG

    def flux(self, r):
        lo, hi = self.elev_rows
        if not lo - 1 <= r <= hi or r == self.mirror:
            return
        eta, merid = self.old(0, r), self.old(2, r)
        thick = self.coef(r, 0)
        thick_n = thick if self.mirror is None else self.coef(r, NORTH_THICK)
        self.flux_n[r] = thick_n * merid + self.coef(r, 2) * eta
        if lo <= r < hi:
            east = thick * self.old(1, r) + self.coef(r, 1) * eta
            self.rolled[r] = (roll(east, -1), roll(east, 1))
        if self.mirror is not None and r == self.mirror - 1:
            self.flux_n[r + 1] = -roll(self.flux_n[r], HALF)

    def elevation(self, r):
        lo, hi = self.elev_rows
        if not lo <= r < hi:
            return
        plus, minus = self.rolled.pop(r)
        change = (plus - minus) + (self.flux_n[r + 1] - self.flux_n[r - 1])
        eta = self.coef(r, WET) * (self.old(0, r) - change)
        self.new[r] = eta
        self.put(0, r, eta)
        if self.mirror is not None and r == self.mirror - 1:
            self.new[r + 1] = roll(eta, HALF)

    def get_new(self, r):
        if r not in self.new:
            self.new[r] = self.known(r)
            if self.vel_rows[0] <= r < self.vel_rows[1]:
                self.put(0, r, self.new[r])
        return self.new[r]

    def slope(self, r):
        if self.vel_rows[0] <= r < self.vel_rows[1]:
            eta = self.get_new(r)
            self.slopes[r] = (roll(eta, -1), roll(eta, 1))

    def velocity(self, r):
        if not self.vel_rows[0] <= r < self.vel_rows[1]:
            return
        plus, minus = self.slopes.pop(r)
        wet, turn = self.coef(r, WET), self.coef(r, 3)
        zonal, merid = self.old(1, r), self.old(2, r)
        zonal = wet * (zonal - HALF_STEP * (plus - minus)) + turn * merid
        slope = self.sign * (self.get_new(r + 1) - self.get_new(r - 1))
        merid = wet * (merid - slope) - turn * zonal
        self.put(1, r, zonal)
        self.put(2, r, merid)

    def row_at(self, n):
        return self.high - n if self.down else self.low + n

    def offset_from(self, before):
        ahead = before.high - self.high if self.down else self.low - before.low
        return max(2 * LAG + ahead, 0)

    def advance(self, n):
        self.flux(self.row_at(n))
        self.elevation(self.row_at(n - LAG))
        self.slope(self.row_at(n - LAG))
        self.velocity(self.row_at(n - 2 * LAG))


def run_chains(chains):
    waiting = []
    for chain in chains:
        at = 0
        for n, sweep in enumerate(chain):
            at += sweep.offset_from(chain[n - 1]) if n else 0
            waiting.append((n, at, sweep))
    waiting.sort(key=lambda entry: entry[0])
    for t in range(max(at + sweep.length for _, at, sweep in waiting)):
        for _, at, sweep in waiting:
            if at <= t < at + sweep.length:
                sweep.advance(t - at)


def middle_kernel(sh, sizes, own_ref, p_hbm, hist_ref, place_out, first_out, q_out, p_ref, sem):
    copy = pltpu.make_async_copy(p_hbm, p_ref, sem)
    copy.start()
    chain = []
    for step in range(1, SUBCYCLES + 1):
        source = own_ref if step == 1 else hist_ref.at[step - 2]
        chain.append(
            Sweep(
                (2 * step - 1, sh.height - 2 * step + 1),
                (2 * step, sh.height - 2 * step),
                functools.partial(row, source),
                functools.partial(coef, own_ref.at[COEF]),
                functools.partial(put_row, hist_ref.at[step - 1]),
            )
        )
    run_chains([chain])
    copy.wait()
    first, place = fold_place(p_ref, sizes[1])
    q_out[0] = first
    place_out[...] = jnp.full((SUBLANES, LANES), place, jnp.int32)
    first_out[...] = jnp.full((SUBLANES, LANES), first, jnp.int32)


def edges_kernel(sh, own_ref, ra_ref, rb_ref, start_ref, coef_ref, hist_ref):
    even = even_lon()
    lane = lane_ids()
    low = lane < HALF
    half_lane = lane & (HALF - 1)
    west_halo = half_lane < HALO
    east_own = (half_lane >= EAST0) & (half_lane < EAST0 + 2 * HALO)
    east_halo = (half_lane >= EAST0 + 2 * HALO) & (half_lane < EAST0 + 3 * HALO)
    sign = north_sign()

    def got(v, upper):
        a, b = ra_ref[v], rb_ref[v]
        w, e = jnp.where(even, b, a), jnp.where(even, a, b)
        if upper:
            w, e = roll(w, SUBLANES // 2, 0), roll(e, SUBLANES // 2, 0)
        return w, e

    def edge_row(f, k):
        own = own_columns(row(own_ref, f, k - HALO), row(own_ref, f, sh.ext - 1 - k - HALO))
        v, at, upper = sh.strip(k, f)
        w, e = got(v, upper)
        w, e = roll(w, -at), roll(e, EAST0 + 2 * HALO - at)
        i = sh.ext - 1 - k - sh.fold_first
        if i >= 0:
            v, h, upper = sh.block(i, f)
            w2, e2 = got(v, upper)
            w2 = roll(w2, HALF - (HALF * h + HALF - HALO))
            e2 = roll(e2, HALF + EAST0 + 2 * HALO - HALF * h)
        yield
        value = merge_own(own, low, east_own)
        if i >= 0:
            w, e = jnp.where(low, w, w2), jnp.where(low, e, e2)
        value = jnp.where(west_halo, w, jnp.where(east_halo, e, value))
        if f == COEF:
            put_edge_coefs(coef_ref, k - HALO, value, sign)
        else:
            put_row(start_ref, f, k - HALO, value)

    run_staged([edge_row(f, k) for k in range(HALO, sh.mid) for f in range(FIELDS)], 8)

    rows = sh.mid - HALO
    chain = []
    for step in range(1, SUBCYCLES + 1):
        source = start_ref if step == 1 else hist_ref.at[step - 2]
        chain.append(
            Sweep(
                (2 * step - 1, rows),
                (2 * step, rows),
                functools.partial(row, source),
                functools.partial(coef, coef_ref),
                functools.partial(put_row, hist_ref.at[step - 1]),
                mirror=rows,
                down=True,
            )
        )
    run_chains([chain])


def own_columns(a, b):
    east = EAST0 - (LANES - 2 * HALO)
    return roll(a, HALO), roll(a, east), roll(b, HALF + HALO), roll(b, HALF + east)


def merge_own(parts, low, east_own):
    aw, ae, bw, be = parts
    return jnp.where(east_own, jnp.where(low, ae, be), jnp.where(low, aw, bw))


def put_edge_coefs(ref, k, value, sign):
    at = SUBLANES * k
    thick = value[0:1]
    ref[at : at + 2, :] = value[0:2]
    ref[at + 2 : at + 3, :] = value[2:3] * sign[0:1]
    ref[at + 3 : at + 4, :] = value[3:4]
    ref[at + WET : at + WET + 1, :] = jnp.where(thick > 0, 1.0, 0.0).astype(F32)
    ref[at + NORTH_THICK : at + NORTH_THICK + 1, :] = thick * sign[0:1]


class Wedges:
    def __init__(self, sh, own=None, hist=None, edges=(None,) * 3, main=None, edge=None):
        self.sh, self.own, self.hist = sh, own, hist
        self.start, self.ecoef, self.ehist = edges
        self.main, self.begin, self.main_c = main
        self.edge, self.edge_c = edge or (None, None)
        lane = lane_ids()
        self.low = lane < HALF
        self.half_lane = half = lane & (HALF - 1)
        self.east_own = (half >= EAST0) & (half < EAST0 + 2 * HALO)
        halo = (half < HALO) | ((half >= EAST0 + 2 * HALO) & (half < EAST0 + 3 * HALO))
        self.halo_south, self.halo_north = halo & self.low, halo & (lane >= HALF)
        self.sign = north_sign()

    SHAPES = (
        (STATE, 4 * HALO * SUBLANES, LANES),
        (4 * HALO * SUBLANES, LANES),
        (FIELDS, 2 * HALO * SUBLANES, LANES),
        (HALO * SUBLANES, LANES),
    )

    def at(self, r):
        span = 2 * HALO
        return r if r < span else r - (self.sh.ext - span) + span

    def main_row(self, f, r):
        if f == COEF:
            at = SUBLANES * self.at(r)
            return self.main_c[at : at + SUBLANES, :]
        return row(self.main, f, self.at(r))

    def first_row(self, f, r):
        return self.main_row(f, r) if f == COEF else row(self.begin, f, self.at(r))

    def put_main(self, f, r, value):
        if f < STATE:
            put_row(self.main, f, self.at(r), value)
            return
        at = SUBLANES * self.at(r)
        self.main_c[at : at + SUBLANES, :] = value
        self.main_c[at + WET : at + WET + 1, :] = jnp.where(value[0:1] > 0, 1.0, 0.0).astype(F32)

    def put_halo(self, f, r, value):
        north = r >= self.sh.mid
        k, mask = (self.sh.ext - 1 - r, self.halo_north) if north else (r, self.halo_south)
        put_row(self.edge, f, k, jnp.where(mask, value, row(self.edge, f, k)))

    def band(self, north):
        return [self.sh.ext - HALO + i if north else i for i in range(HALO)]

    def take_rows(self, ref, north):
        for f in range(FIELDS):
            for i, r in enumerate(self.band(north)):
                if ref is None:
                    value = jnp.zeros((SUBLANES, LANES), F32)
                elif f < STATE:
                    value = ref[f * HALO + i]
                else:
                    value = ref[STATE * HALO + i % PAIRS]
                    value = value if i < PAIRS else roll(value, SUBLANES // 2, 0)
                self.put_main(f, r, value)
                if f < STATE and self.begin is not self.main:
                    put_row(self.begin, f, self.at(r), value)

    def take_halos(self, ref, first, north):
        base = HALF if north else 0
        if ref is None:
            for f in range(FIELDS):
                for r in self.band(north):
                    self.put_halo(f, r, jnp.zeros((SUBLANES, LANES), F32))
            return

        def band_row(f, i, r):
            v, at = self.sh.corner(i, f)
            v = ref[v - self.sh.main + first]
            out_by = self.sh.away(i + 1 if north else HALO - i)
            w = roll(v, base - at + out_by)
            e = roll(v, base + EAST0 + HALO - at - out_by)
            yield
            self.put_halo(f, r, jnp.where(self.half_lane < HALO, w, e))

        rows = list(enumerate(self.band(north)))
        run_staged([band_row(f, i, r) for f in range(FIELDS) for i, r in rows], 16)

    def edge_own(self, out, north_only=False):
        def edge_row(f, k):
            b = self.first_row(f, self.sh.ext - 1 - k)
            parts = own_columns(b if north_only else self.first_row(f, k), b)
            yield
            put_row(out, f, k, merge_own(parts, self.low, self.east_own))

        run_staged([edge_row(f, k) for k in range(HALO) for f in range(FIELDS)], 8)

    def edge_coefs(self):
        for k in range(HALO):
            put_edge_coefs(self.edge_c, k, row(self.edge, COEF, k), self.sign)

    def steps(self, sides):
        ext = self.sh.ext

        def put_edge(f, k, value):
            put_row(self.edge, f, k, value)

        def edge_coef(k, c):
            return coef(self.edge_c, k, c) if k < HALO else coef(self.ecoef, k - HALO, c)

        def main_coef(r, c):
            if HALO <= r < ext - HALO:
                return coef(self.own.at[COEF], r - HALO, c)
            return coef(self.main_c, self.at(r), c)

        edges, south, north = [], [], []
        for step in range(1, SUBCYCLES + 1):
            first, ready = 2 * step - 2, 2 * step + HALO - 2

            def old_main(f, r, step=step, ready=ready):
                if ready <= r < ext - ready:
                    return row(self.own if step == 1 else self.hist.at[step - 2], f, r - HALO)
                return self.main_row(f, r)

            def old_edge(f, k, step=step, ready=ready):
                if k >= ready:
                    return row(self.start if step == 1 else self.ehist.at[step - 2], f, k - HALO)
                return row(self.edge, f, k)

            def known_main(r, step=step):
                return row(self.hist.at[step - 1], 0, r - HALO)

            def known_edge(k, step=step):
                return row(self.ehist.at[step - 1], 0, k - HALO)

            elev, vel = (first + 1, ready + 1), (first + 2, ready + 2)
            edges.append(
                Sweep(
                    elev,
                    vel,
                    old_edge,
                    edge_coef,
                    put_edge,
                    known_edge,
                    mirror=self.sh.mid,
                    down=True,
                )
            )
            south.append(
                Sweep(elev, vel, old_main, main_coef, self.put_main, known_main, down=True)
            )
            elev, vel = [(ext - rows[1], ext - rows[0]) for rows in (elev, vel)]
            north.append(Sweep(elev, vel, old_main, main_coef, self.put_main, known_main))
        chains = {"edges": edges, "south": south, "north": north}
        run_chains([chains[name] for name in sides])

    def output(self, first, last, put):
        ext, mid, ready = self.sh.ext, self.sh.mid, 2 * HALO
        final, e_final = self.hist.at[SUBCYCLES - 1], self.ehist.at[SUBCYCLES - 1]
        lane = lane_ids()

        def output_row(f, r):
            k, h = (r, 0) if r < mid else (ext - 1 - r, HALF)
            v = row(self.edge, f, k) if k < ready else row(e_final, f, k - HALO)
            w, e = roll(v, -(h + HALO)), roll(v, LANES - HALO - (h + EAST0 + HALO))
            yield
            inner = ready <= r < ext - ready
            v = row(final, f, r - HALO) if inner else self.main_row(f, r)
            v = jnp.where(lane < HALO, w, jnp.where(lane >= LANES - HALO, e, v))
            put(f, r - HALO, v)

        run_staged([output_row(f, r) for f in range(STATE) for r in range(first, last)], 16)


def for_bands(sizes, n_lat, take):
    lat_size, _ = sizes
    lat = lax.axis_index("lat")
    lat_even = lax.rem(lat, 2) == 0
    lat_odd = jnp.logical_not(lat_even)
    at_top = lat == lat_size - 1
    pl.when(at_top)(lambda: take(None, True))
    pl.when(lat == 0)(lambda: take(None, False))
    pl.when(lat_even)(lambda: take(0, True))
    pl.when(lat_odd)(lambda: take(0, False))
    if n_lat == 2:
        pl.when(lat_odd & jnp.logical_not(at_top))(lambda: take(1, True))
        pl.when(lat_even & (lat > 0))(lambda: take(1, False))


def wedge_rows_kernel(sh, sizes, n_lat, *refs):
    bands, (own_ref, hist_ref, main, edge_out, order_out, begin, main_c) = (
        refs[:n_lat],
        refs[n_lat:],
    )
    wedges = Wedges(sh, own_ref, hist_ref, main=(main, begin, main_c))
    order_out[...] = jnp.zeros((SUBLANES, LANES), F32)

    def take(n, north):
        wedges.take_rows(None if n is None else bands[n], north)

    for_bands(sizes, n_lat, take)
    wedges.edge_own(edge_out)
    wedges.steps(("south", "north"))


def wedge_edges_kernel(sh, sizes, n_lat, *refs):
    corners, refs = refs[:n_lat], refs[n_lat:]
    hist_ref, main, edge_own, edges = refs[0], refs[1], refs[2], refs[3:6]
    (out_ref, order_out), kept, edge = refs[6:8], refs[8:11], refs[11:]
    wedges = Wedges(sh, None, hist_ref, edges, (main, None, None), edge)
    order_out[...] = jnp.zeros((SUBLANES, LANES), F32)
    for f in range(FIELDS):
        for k in range(HALO):
            put_row(edge[0], f, k, row(edge_own, f, k))

    for k in range(HALO + 1):
        at = slice(SUBLANES * k, SUBLANES * (k + 1))
        kept[1][at, :] = edges[1][at, :]
    for f in range(STATE):
        for k in range(2):
            put_row(kept[0], f, k, row(edges[0], f, k))
        for n in range(SUBCYCLES):
            for k in range(2 * n + 1, 2 * n + 4):
                put_row(kept[2].at[n], f, k, row(edges[2].at[n], f, k))

    def take(n, north):
        wedges.take_halos(None if n is None else corners[n], 0, north)

    for_bands(sizes, n_lat, take)
    wedges.edge_coefs()
    wedges.steps(("edges",))
    out_flat = flat_rows(out_ref)

    def put(f, r, value):
        out_flat[f, pl.ds(r, SUBLANES, stride=sh.height), :] = value

    wedges.output(HALO, sh.ext - HALO, put)


def north_kernel(sh, sizes, got_ref, sent_ref, first_ref, order_ref, *outs):
    main, main_c, edge, edge_c = outs[:4]
    fold_ref = outs[4]
    lat_size, lon_size = sizes

    @pl.when(lax.axis_index("lat") == lat_size - 1)
    def _():
        facing = lax.rem(first_ref[...] - lax.axis_index("lon") + lon_size, lon_size)
        itself = facing == lax.axis_index("lon")
        for v in range(sh.band):
            fold_ref[v] = jnp.where(itself, sent_ref[v], got_ref[v])
        wedges = Wedges(sh, main=(main, main, main_c), edge=(edge, edge_c))
        wedges.take_rows(fold_ref, True)
        wedges.edge_own(edge, north_only=True)
        wedges.take_halos(fold_ref, sh.main, True)
        wedges.edge_coefs()


def last_kernel(sh, sizes, *refs):
    lat_size, _ = sizes
    done_ref, state, begin = refs[0], refs[1:6], refs[6:10]
    out_hbm, late_ref, sems, main, edge = refs[10:]
    height, ext = sh.height, sh.ext
    split = (height - HALO) // SUBLANES * SUBLANES
    at_top = lax.axis_index("lat") == lat_size - 1
    lines = (pl.ds(0, split), pl.ds(split, height - split))

    def copies(source, part):
        return [
            pltpu.make_async_copy(
                source.at[f, :, lines[part]], out_hbm.at[f, :, lines[part]], sems.at[part, f]
            )
            for f in range(STATE)
        ]

    early = copies(done_ref, 0)
    for copy in early:
        copy.start()

    @pl.when(jnp.logical_not(at_top))
    def _():
        rest = copies(done_ref, 1)
        for copy in rest:
            copy.start()
        for copy in rest:
            copy.wait()

    @pl.when(at_top)
    def _():
        wedges = Wedges(
            sh, *state[:2], state[2:], (main, main, begin[1]), (edge, begin[3])
        )
        for f in range(STATE):
            for k in range(HALO):
                put_row(edge, f, k, row(begin[2], f, k))
                at = wedges.at(ext - 1 - k)
                put_row(main, f, at, row(begin[0], f, at))
        wedges.steps(("edges", "north"))

        late_flat, done_flat = flat_rows(late_ref), flat_rows(done_ref)

        def put(f, r, value):
            late_flat[f, pl.ds(r, SUBLANES, stride=height), :] = value

        for f in range(STATE):
            for r in range(split, height - HALO):
                put(f, r, done_flat[f, pl.ds(r, SUBLANES, stride=height), :])
        wedges.output(ext - 2 * HALO, ext - HALO, put)
        rest = copies(late_ref, 1)
        for copy in rest:
            copy.start()
        for copy in rest:
            copy.wait()

    for copy in early:
        copy.wait()


def pair_swaps(size, wrap):
    first = [(i, i ^ 1) for i in range(size)]
    second = []
    for i in range(size):
        j = i + 1 if i % 2 else i - 1
        if wrap or 0 <= j < size:
            second.append((i, j % size))
    return first, second


def vmem(n):
    return [pl.BlockSpec(memory_space=pltpu.VMEM)] * n


def in_hbm(x):
    return pltpu.with_memory_space_constraint(x, pltpu.HBM)


def smem():
    return pl.BlockSpec(memory_space=pltpu.SMEM)


def on_device(mesh_sizes, perturb, background, land_mask, levels, fold_partner):
    lat_size, lon_size, dir_size = mesh_sizes
    height = perturb.shape[2]
    sh = Shapes(height)
    sizes = (lat_size, lon_size)
    flat = perturb.reshape(STATE, SUBLANES * height, LANES)
    tile = (SUBLANES, LANES)

    def shape(n):
        return pltpu.VMEM((n,) + tile, F32)

    params = pltpu.CompilerParams(vmem_limit_bytes=16 * 1024 * 1024)
    rows = SUBLANES * height
    n_lat = 1 if lat_size == 2 else 2
    side_a, side_b, own, *lat_out = pl.pallas_call(
        functools.partial(sides_kernel, sh, sizes),
        out_shape=(
            shape(sh.side),
            shape(sh.side),
            pltpu.VMEM((FIELDS, rows, LANES), F32),
        )
        + (shape(sh.main),) * n_lat,
        in_specs=[pl.BlockSpec(memory_space=pltpu.HBM)] * 4,
        out_specs=tuple(vmem(3 + n_lat)),
        scratch_shapes=[
            pltpu.VMEM(flat.shape, F32),
            pltpu.VMEM(background.shape, F32),
            pltpu.VMEM(land_mask.shape, jnp.int32),
            pltpu.VMEM(levels.shape, jnp.int32),
            pltpu.SemaphoreType.DMA((3 + STATE,)),
        ],
        compiler_params=params,
        name="sides",
    )(*[in_hbm(v) for v in (flat, background, land_mask, levels)])

    lon_swaps = pair_swaps(lon_size, True)
    got_a, got_b = [lax.ppermute(x, "lon", swap) for x, swap in zip((side_a, side_b), lon_swaps)]

    hist, place, first, branch = pl.pallas_call(
        functools.partial(middle_kernel, sh, sizes),
        out_shape=(
            pltpu.VMEM((SUBCYCLES, STATE, rows, LANES), F32),
            pltpu.VMEM(tile, jnp.int32),
            pltpu.VMEM(tile, jnp.int32),
            jax.ShapeDtypeStruct((1,), jnp.int32),
        ),
        in_specs=vmem(1) + [pl.BlockSpec(memory_space=pltpu.HBM)],
        out_specs=tuple(vmem(3)) + (smem(),),
        scratch_shapes=[
            pltpu.SMEM(fold_partner.shape, jnp.int32),
            pltpu.SemaphoreType.DMA,
        ],
        compiler_params=params,
        name="middle",
    )(own, in_hbm(fold_partner))
    lat_swaps = pair_swaps(lat_size, False)[:n_lat]
    got_lat = [lax.ppermute(x, "lat", swap) for x, swap in zip(lat_out, lat_swaps)]
    wedge_main, edge_own, order = pl.pallas_call(
        functools.partial(wedge_rows_kernel, sh, sizes, n_lat),
        out_shape=(
            pltpu.VMEM(Wedges.SHAPES[0], F32),
            pltpu.VMEM(Wedges.SHAPES[2], F32),
            pltpu.VMEM(tile, F32),
        ),
        in_specs=vmem(n_lat + 2),
        out_specs=tuple(vmem(3)),
        scratch_shapes=[pltpu.VMEM(x, F32) for x in Wedges.SHAPES[:2]],
        compiler_params=params,
        name="wedge_rows",
    )(*got_lat, own, hist)
    fold_band, *lat_corners = pl.pallas_call(
        functools.partial(bands_kernel, sh, sizes),
        out_shape=(shape(sh.band),) + (shape(sh.corners),) * n_lat,
        in_specs=vmem(5),
        out_specs=tuple(vmem(1 + n_lat)),
        compiler_params=params,
        name="bands",
    )(own, got_a, got_b, place, order)

    edge_rows = SUBLANES * (sh.mid - HALO)
    edge_shapes = (
        pltpu.VMEM((STATE, edge_rows, LANES), F32),
        pltpu.VMEM((edge_rows, LANES), F32),
        pltpu.VMEM((SUBCYCLES, STATE, edge_rows, LANES), F32),
    )
    step_edges = jax.jit(
        pl.pallas_call(
            functools.partial(edges_kernel, sh),
            out_shape=edge_shapes,
            in_specs=vmem(3),
            out_specs=tuple(vmem(3)),
            compiler_params=params,
            name="edges",
        )
    )
    step_wedge_edges = jax.jit(
        pl.pallas_call(
            functools.partial(wedge_edges_kernel, sh, sizes, n_lat),
            out_shape=(pltpu.VMEM(perturb.shape, F32), pltpu.VMEM(tile, F32)) + edge_shapes,
            in_specs=vmem(n_lat + 6),
            out_specs=tuple(vmem(5)),
            scratch_shapes=[pltpu.VMEM(x, F32) for x in Wedges.SHAPES[2:]],
            compiler_params=params,
            name="wedge_edges",
        )
    )
    take_north = jax.jit(
        pl.pallas_call(
            functools.partial(north_kernel, sh, sizes),
            out_shape=tuple(pltpu.VMEM(x, F32) for x in Wedges.SHAPES),
            in_specs=vmem(4),
            out_specs=tuple(vmem(4)),
            scratch_shapes=[pltpu.VMEM((sh.band,) + tile, F32)],
            compiler_params=params,
            name="north",
        )
    )
    def rest(q, fold_band, lat_corners, wedge_main, edge_own, own, hist, got_a, got_b, first):
        across = []
        for m in range(lon_size):
            j = (q - m) % lon_size
            for a in range(lat_size):
                for d in range(dir_size):
                    source, target = (m, a, d), (j, a, d if j != m else d ^ 1)
                    across.append(
                        tuple((x * lat_size + y) * dir_size + z for x, y, z in (source, target))
                    )
        got_fold = lax.ppermute(fold_band, ("lon", "lat", "dir"), across)
        got_corners = [lax.ppermute(x, "lat", swap) for x, swap in zip(lat_corners, lat_swaps)]
        edges = step_edges(own, got_a, got_b)
        done, order, *kept = step_wedge_edges(*got_corners, hist, wedge_main, edge_own, *edges)
        return kept, done, take_north(got_fold, fold_band, first, order)

    edges, done, beyond = lax.switch(
        branch[0],
        [functools.partial(rest, q) for q in range(lon_size)],
        fold_band,
        lat_corners,
        wedge_main,
        edge_own,
        own,
        hist,
        got_a,
        got_b,
        first,
    )
    return pl.pallas_call(
        functools.partial(last_kernel, sh, sizes),
        out_shape=jax.ShapeDtypeStruct(perturb.shape, F32),
        in_specs=vmem(10),
        out_specs=pl.BlockSpec(memory_space=pltpu.HBM),
        scratch_shapes=[
            pltpu.VMEM(perturb.shape, F32),
            pltpu.SemaphoreType.DMA((2, STATE)),
            pltpu.VMEM(Wedges.SHAPES[0], F32),
            pltpu.VMEM(Wedges.SHAPES[2], F32),
        ],
        compiler_params=params,
        name="last",
    )(done, own, hist, *edges, *beyond)


def solution(mesh):
    placed = (
        P("grp", "dir", "lat", "lon"),
        P("grp", "lat", "lon"),
        P("lat", "lon"),
        P("lat", "lon"),
        P(),
    )
    sizes = tuple(mesh.shape[axis] for axis in ("lat", "lon", "dir"))
    return jax.shard_map(
        functools.partial(on_device, sizes),
        mesh=mesh,
        in_specs=placed,
        out_specs=P("grp", "dir", "lat", "lon"),
        check_vma=False,
    )
```

```python
import functools
from collections import deque

import jax
import jax.numpy as jnp
from jax import lax
from jax.experimental import pallas as pl
from jax.experimental.pallas import tpu as pltpu
from jax.sharding import PartitionSpec as P

SUBCYCLES = 5
NLEV = 90
TIME_STEP = 0.35
HALF_STEP = 0.5 * TIME_STEP

LANES = 128
SUBLANES = 8
HALF = LANES // 2
HALO = 2 * SUBCYCLES
PAIRS = HALO // 2
FIELDS = 4
STATE = 3
COEF = 3
STRIP_SLOTS = HALF // HALO
CORNER_SLOTS = LANES // (2 * HALO)
F32 = jnp.float32


def ceil_div(a, b):
    return -(-a // b)


class Shapes:
    def __init__(self, height):
        self.height = height
        self.ext = height + 2 * HALO
        self.mid = self.ext // 2
        self.fold_first = height
        self.blocks = STATE * PAIRS + ceil_div(PAIRS, 2)
        self.strip_rows = self.mid - HALO
        self.strip_pairs = self.strip_rows // 2
        slots = self.strip_rows * STATE + self.strip_pairs
        self.side = self.blocks + ceil_div(slots, STRIP_SLOTS)
        self.main = STATE * HALO + PAIRS
        self.corners = ceil_div(FIELDS * PAIRS, CORNER_SLOTS)
        self.band = self.main + self.corners

    def block(self, i, f):
        upper = i // PAIRS
        if f < STATE:
            return f * PAIRS + i % PAIRS, upper, False
        return STATE * PAIRS + i % PAIRS // 2, i % PAIRS % 2, upper == 1

    def strip(self, k, f):
        slot, upper = (k - HALO) * STATE + f, False
        if f == COEF:
            upper = k - HALO >= self.strip_pairs
            slot = self.strip_rows * STATE + (k - HALO) % self.strip_pairs
        return self.blocks + slot // STRIP_SLOTS, HALO * (slot % STRIP_SLOTS), upper

    def corner(self, i, f):
        slot = f * PAIRS + min(i, HALO - 1 - i)
        return self.main + slot // CORNER_SLOTS, 2 * HALO * (slot % CORNER_SLOTS)

    @staticmethod
    def away(d):
        return d if d > PAIRS else 0

    @staticmethod
    def corner_lanes(d):
        west, east = (d, HALO - 1), (HALO, 2 * HALO - 1 - d)
        if d > PAIRS:
            west, east = (0, HALO - 1 - d), (HALO + d, 2 * HALO - 1)
        return west, east


def by_register(items, where):
    groups = {}
    for i, f in items:
        v, at = where(i, f)
        groups.setdefault(v, []).append((i, f, at))
    return groups


def roll(x, shift, axis=1):
    shift = shift % x.shape[axis]
    return x if shift == 0 else pltpu.roll(x, shift, axis)


def lane_ids():
    return lax.broadcasted_iota(jnp.int32, (SUBLANES, LANES), 1)


def sublane_ids():
    return lax.broadcasted_iota(jnp.int32, (SUBLANES, LANES), 0)


def run_staged(tasks, window):
    waiting = deque()

    def advance(task):
        try:
            next(task)
        except StopIteration:
            return
        waiting.append(task)

    for task in tasks:
        advance(task)
        while len(waiting) >= window:
            advance(waiting.popleft())
    while waiting:
        advance(waiting.popleft())


def row(ref, f, r):
    return ref[f, SUBLANES * r : SUBLANES * (r + 1), :]


def put_row(ref, f, r, value):
    ref[f, SUBLANES * r : SUBLANES * (r + 1), :] = value


def flat_rows(ref):
    return ref.reshape(ref.shape[0], ref.shape[1] * ref.shape[2], ref.shape[3])


def coef(ref, r, c):
    return jnp.broadcast_to(ref[SUBLANES * r + c : SUBLANES * r + c + 1, :], (SUBLANES, LANES))


def even_lon():
    return jnp.full((SUBLANES, LANES), lax.rem(lax.axis_index("lon"), 2), jnp.int32) == 0


def fold_place(fold_ref, lon_size):
    pivot = fold_ref[0]
    block = pivot // LANES
    rest = pivot - block * LANES
    low = rest < HALF
    place = jnp.where(low, rest + LANES, rest)
    branch = jnp.where(low, block - 1 + lon_size, block)
    return lax.rem(branch, lon_size), place


def pair_coefs(a, b):
    return jnp.where(sublane_ids() < SUBLANES // 2, a, roll(b, SUBLANES // 2, 0))


def lat_rows(sh, own_ref, outs):
    own = functools.partial(row, own_ref)

    def raw_rows(out, first):
        for f in range(STATE):
            for i in range(HALO):
                out[f * HALO + i] = own(f, first + i)
        for i in range(PAIRS):
            out[STATE * HALO + i] = pair_coefs(
                own(COEF, first + i), own(COEF, first + i + PAIRS)
            )

    top = sh.height - HALO
    lat_even = lax.rem(lax.axis_index("lat"), 2) == 0

    @pl.when(lat_even)
    def _():
        raw_rows(outs[0], top)
        if len(outs) > 1:
            raw_rows(outs[1], 0)

    @pl.when(jnp.logical_not(lat_even))
    def _():
        raw_rows(outs[0], 0)
        if len(outs) > 1:
            raw_rows(outs[1], top)


def sides_kernel(sh, sizes, x_hbm, b_hbm, m_hbm, l_hbm, *rest):
    a_out, b_out, own_ref = rest[:3]
    lat_outs, (x_ref, b_ref, m_ref, l_ref, sems) = rest[3:-5], rest[-5:]
    lat_size, _ = sizes
    height = sh.height
    copies = [
        pltpu.make_async_copy(src, dst, sems.at[n])
        for n, (src, dst) in enumerate(
            [(b_hbm, b_ref), (m_hbm, m_ref), (l_hbm, l_ref)]
            + [(x_hbm.at[f], x_ref.at[f]) for f in range(STATE)]
        )
    ]
    for copy in copies:
        copy.start()
    for copy in copies[:3]:
        copy.wait()

    wet = m_ref[...].astype(F32)
    depth = 0.5 + 1.5 * ((l_ref[...] - 1).astype(F32) / (NLEV - 1)) ** 2
    row0 = lax.axis_index("lat") * height
    rows = (row0 + lax.broadcasted_iota(jnp.int32, (height, LANES), 0)).astype(F32)
    coriolis = 0.3 + 0.2 * rows / (height * lat_size)
    planes = [
        HALF_STEP * (wet * (depth + b_ref[0])),
        HALF_STEP * b_ref[1],
        HALF_STEP * b_ref[2],
        wet * (TIME_STEP * coriolis),
        wet,
    ]
    planes += [jnp.zeros_like(wet)] * (SUBLANES - len(planes))
    for c, plane in enumerate(planes):
        for r in range(0, height, SUBLANES):
            own_ref[COEF, pl.ds(SUBLANES * r + c, SUBLANES, stride=SUBLANES), :] = plane[
                r : r + SUBLANES
            ]
    for copy in copies[3:]:
        copy.wait()
    for f in range(STATE):
        for r in range(height):
            put_row(own_ref, f, r, x_ref[f, pl.ds(r, SUBLANES, stride=height), :])

    even = even_lon()
    lane, sub = lane_ids(), sublane_ids()
    low = lane < HALF
    own = functools.partial(row, own_ref)
    top = height - HALO

    def rows_of(f, r):
        return pair_coefs(own(f, r), own(f, r + PAIRS)) if f == COEF else own(f, r)

    def strip_rows_of(f, r, other):
        return pair_coefs(own(f, r), own(f, other)) if f == COEF else own(f, r)

    def block(v, a, b):
        a_up, b_up = roll(a, HALF), roll(b, HALF)
        yield
        east = jnp.where(low, a_up, b)
        west = jnp.where(low, a, b_up)
        a_out[v] = jnp.where(even, east, west)
        b_out[v] = jnp.where(even, west, east)

    def blocks():
        for f in range(STATE):
            for i in range(PAIRS):
                yield block(f * PAIRS + i, own(f, top + i), own(f, top + i + PAIRS))
        for i in range(0, PAIRS, 2):
            v, _, _ = sh.block(i, COEF)
            yield block(v, rows_of(COEF, top + i), rows_of(COEF, top + min(i + 1, PAIRS - 1)))

    slots = {}
    for k in range(HALO, sh.mid):
        for f in range(FIELDS):
            v, at, upper = sh.strip(k, f)
            if not upper:
                slots.setdefault(v, []).append((k, f, at))

    def strips(v):
        parts = []
        for k, f, at in slots[v]:
            ahead = sh.strip_pairs
            r = sh.ext - 1 - k - HALO
            a, b = strip_rows_of(f, k - HALO, k - HALO + ahead), strip_rows_of(f, r, r - ahead)
            end = at - (LANES - HALO)
            a_east, a_west = roll(a, end), roll(a, at)
            near = sh.ext - 1 - k < sh.fold_first
            near_other = sh.ext - 1 - k - ahead < sh.fold_first
            b_east, b_west = roll(b, HALF + end), roll(b, HALF + at)
            if not near:
                b_east, b_west = roll(b, end), roll(b, at)
                if f == COEF and near_other:
                    lower_half = sub < SUBLANES // 2
                    b_east = jnp.where(lower_half, b_east, roll(b, HALF + end))
                    b_west = jnp.where(lower_half, b_west, roll(b, HALF + at))
            parts.append((at, a_east, b_east, a_west, b_west))
        yield
        east = west = jnp.zeros((SUBLANES, LANES), F32)
        for at, ea, eb, wa, wb in parts:
            here = (lane >= at) & (lane < at + HALO)
            there = (lane >= HALF + at) & (lane < HALF + at + HALO)
            east = jnp.where(here, ea, jnp.where(there, eb, east))
            west = jnp.where(here, wa, jnp.where(there, wb, west))
        a_out[v] = jnp.where(even, east, west)
        b_out[v] = jnp.where(even, west, east)

    run_staged(blocks(), 10)
    run_staged([strips(v) for v in sorted(slots)], 2)
    lat_rows(sh, own_ref, lat_outs)


def bands_kernel(sh, sizes, own_ref, ra_ref, rb_ref, place_ref, order_ref, fold_out, *lat_outs):
    lat_size, _ = sizes
    even = even_lon()
    lane, sub = lane_ids(), sublane_ids()
    low = lane < HALF
    own = functools.partial(row, own_ref)
    top = sh.height - HALO

    def got(v, upper):
        a, b = ra_ref[v], rb_ref[v]
        w, e = jnp.where(even, b, a), jnp.where(even, a, b)
        if upper:
            w, e = roll(w, SUBLANES // 2, 0), roll(e, SUBLANES // 2, 0)
        return w, e

    def corners(out, is_top):
        def register(v, items):
            parts = []
            for i, f, at in items:
                if is_top:
                    src, h, upper = sh.block(i, f)
                    w_at, e_at = HALF * h + HALF - HALO, HALF * h
                else:
                    src, w_at, upper = sh.strip(HALO + i, f)
                    e_at = w_at
                w, e = got(src, upper)
                d = HALO - i if is_top else i + 1
                out_by = sh.away(d)
                w, e = roll(w, at - w_at - out_by), roll(e, at + HALO - e_at + out_by)
                parts.append((at, d, w, e))
            yield
            total = jnp.zeros((SUBLANES, LANES), F32)
            for at, d, w, e in parts:
                for (start, end), value in zip(sh.corner_lanes(d), (w, e)):
                    if start <= end:
                        total = jnp.where((lane >= at + start) & (lane <= at + end), value, total)
            out[v - sh.main] = total

        groups = by_register([(i, f) for f in range(FIELDS) for i in range(HALO)], sh.corner)
        run_staged([register(v, items) for v, items in groups.items()], 3)

    lat_even = lax.rem(lax.axis_index("lat"), 2) == 0

    @pl.when(lat_even)
    def _():
        corners(lat_outs[0], True)
        if len(lat_outs) > 1:
            corners(lat_outs[1], False)

    @pl.when(jnp.logical_not(lat_even))
    def _():
        corners(lat_outs[0], False)
        if len(lat_outs) > 1:
            corners(lat_outs[1], True)

    @pl.when(lax.axis_index("lat") == lat_size - 1)
    def _():
        where_to = place_ref[...]
        rest = where_to & (LANES - 1)
        eastern = where_to >= LANES
        backwards = (where_to - lane) & (LANES - 1)
        main_own = (eastern & (lane >= rest + 1)) | (jnp.logical_not(eastern) & (lane <= rest))
        upper = (lane >= rest + 1) & (lane <= rest + HALO)
        lower = (lane >= rest + 1 - HALO) & (lane <= rest)
        side_own = (eastern & lower) | (jnp.logical_not(eastern) & upper)
        side_far = (eastern & upper & (lane >= HALF)) | (
            jnp.logical_not(eastern) & lower & (lane < HALF)
        )
        coef_signs = jnp.where((sub == 1) | (sub == 2), -1.0, 1.0).astype(F32)

        def reversed_row(f, i):
            v, h, upper = sh.block(i, f)
            w, e = got(v, upper)
            if h == 0:
                w = roll(w, HALF)
            else:
                e = roll(e, HALF)
            v, at, upper = sh.strip(sh.ext - 1 - sh.fold_first - i, f)
            far_w, far_e = got(v, upper)
            far_w, far_e = roll(far_w, -HALO - at), roll(far_e, -at)
            yield
            both = jnp.where(low, e, w)
            mine = own(f, top + i)
            main = jnp.where(main_own, mine, both)
            side = jnp.where(
                side_own, mine, jnp.where(side_far, jnp.where(low, far_w, far_e), both)
            )
            if f == COEF:
                main, side = main * coef_signs, side * coef_signs
            elif f > 0:
                main, side = -main, -side
            main = jnp.take_along_axis(main, backwards, axis=1)
            side = jnp.take_along_axis(side, backwards, axis=1)
            yield
            j = HALO - 1 - i
            v, at = sh.corner(j, f)
            d = j + 1
            out_by = sh.away(d)
            moves = (-out_by, out_by) if out_by else (0,)
            moved = [roll(side, at - (LANES - HALO) + by) for by in moves]
            if f < STATE:
                fold_out[f * HALO + j] = main
            elif j < PAIRS:
                v2 = STATE * HALO + j
                fold_out[v2] = jnp.where(sub < SUBLANES // 2, main, fold_out[v2])
            else:
                fold_out[STATE * HALO + j - PAIRS] = roll(main, SUBLANES // 2, 0)
            yield
            total = fold_out[v]
            for (start, end), value in zip(sh.corner_lanes(d), (moved[0], moved[-1])):
                if start <= end:
                    total = jnp.where((lane >= at + start) & (lane <= at + end), value, total)
            fold_out[v] = total

        for v in range(STATE * HALO, sh.band):
            fold_out[v] = jnp.zeros((SUBLANES, LANES), F32)
        run_staged([reversed_row(f, i) for f in range(FIELDS) for i in range(HALO)], 14)


EAST0 = HALF // 2
LAG = 4
WET, NORTH_THICK = 4, 5


def north_sign():
    return jnp.where(lane_ids() < HALF, 1.0, -1.0).astype(F32)


class Sweep:
    def __init__(self, elev, vel, old, coef, put, known=None, mirror=None, down=False):
        self.elev_rows, self.vel_rows = elev, vel
        self.old, self.coef, self.put, self.known, self.mirror = old, coef, put, known, mirror
        self.flux_n, self.rolled, self.new, self.slopes = {}, {}, {}, {}
        self.sign = HALF_STEP * north_sign() if mirror is not None else HALF_STEP
        self.low, self.high = min(elev[0] - 1, vel[0]), max(elev[1], vel[1] - 1)
        self.down = down
        self.length = self.high - self.low + 1 + 2 * LAG

    def flux(self, r):
        lo, hi = self.elev_rows
        if not lo - 1 <= r <= hi or r == self.mirror:
            return
        eta, merid = self.old(0, r), self.old(2, r)
        thick = self.coef(r, 0)
        thick_n = thick if self.mirror is None else self.coef(r, NORTH_THICK)
        self.flux_n[r] = thick_n * merid + self.coef(r, 2) * eta
        if lo <= r < hi:
            east = thick * self.old(1, r) + self.coef(r, 1) * eta
            self.rolled[r] = (roll(east, -1), roll(east, 1))
        if self.mirror is not None and r == self.mirror - 1:
            self.flux_n[r + 1] = -roll(self.flux_n[r], HALF)

    def elevation(self, r):
        lo, hi = self.elev_rows
        if not lo <= r < hi:
            return
        plus, minus = self.rolled.pop(r)
        change = (plus - minus) + (self.flux_n[r + 1] - self.flux_n[r - 1])
        eta = self.coef(r, WET) * (self.old(0, r) - change)
        self.new[r] = eta
        self.put(0, r, eta)
        if self.mirror is not None and r == self.mirror - 1:
            self.new[r + 1] = roll(eta, HALF)

    def get_new(self, r):
        if r not in self.new:
            self.new[r] = self.known(r)
            if self.vel_rows[0] <= r < self.vel_rows[1]:
                self.put(0, r, self.new[r])
        return self.new[r]

    def slope(self, r):
        if self.vel_rows[0] <= r < self.vel_rows[1]:
            eta = self.get_new(r)
            self.slopes[r] = (roll(eta, -1), roll(eta, 1))

    def velocity(self, r):
        if not self.vel_rows[0] <= r < self.vel_rows[1]:
            return
        plus, minus = self.slopes.pop(r)
        wet, turn = self.coef(r, WET), self.coef(r, 3)
        zonal, merid = self.old(1, r), self.old(2, r)
        zonal = wet * (zonal - HALF_STEP * (plus - minus)) + turn * merid
        slope = self.sign * (self.get_new(r + 1) - self.get_new(r - 1))
        merid = wet * (merid - slope) - turn * zonal
        self.put(1, r, zonal)
        self.put(2, r, merid)

    def row_at(self, n):
        return self.high - n if self.down else self.low + n

    def offset_from(self, before):
        ahead = before.high - self.high if self.down else self.low - before.low
        return max(2 * LAG + ahead, 0)

    def advance(self, n):
        self.flux(self.row_at(n))
        self.elevation(self.row_at(n - LAG))
        self.slope(self.row_at(n - LAG))
        self.velocity(self.row_at(n - 2 * LAG))


def run_chains(chains):
    waiting = []
    for chain in chains:
        at = 0
        for n, sweep in enumerate(chain):
            at += sweep.offset_from(chain[n - 1]) if n else 0
            waiting.append((n, at, sweep))
    waiting.sort(key=lambda entry: entry[0])
    for t in range(max(at + sweep.length for _, at, sweep in waiting)):
        for _, at, sweep in waiting:
            if at <= t < at + sweep.length:
                sweep.advance(t - at)


def middle_kernel(sh, sizes, own_ref, p_hbm, hist_ref, place_out, first_out, q_out, p_ref, sem):
    copy = pltpu.make_async_copy(p_hbm, p_ref, sem)
    copy.start()
    chain = []
    for step in range(1, SUBCYCLES + 1):
        source = own_ref if step == 1 else hist_ref.at[step - 2]
        chain.append(
            Sweep(
                (2 * step - 1, sh.height - 2 * step + 1),
                (2 * step, sh.height - 2 * step),
                functools.partial(row, source),
                functools.partial(coef, own_ref.at[COEF]),
                functools.partial(put_row, hist_ref.at[step - 1]),
            )
        )
    run_chains([chain])
    copy.wait()
    first, place = fold_place(p_ref, sizes[1])
    q_out[0] = first
    place_out[...] = jnp.full((SUBLANES, LANES), place, jnp.int32)
    first_out[...] = jnp.full((SUBLANES, LANES), first, jnp.int32)


def edges_kernel(sh, own_ref, ra_ref, rb_ref, start_ref, coef_ref, hist_ref):
    even = even_lon()
    lane = lane_ids()
    low = lane < HALF
    half_lane = lane & (HALF - 1)
    west_halo = half_lane < HALO
    east_own = (half_lane >= EAST0) & (half_lane < EAST0 + 2 * HALO)
    east_halo = (half_lane >= EAST0 + 2 * HALO) & (half_lane < EAST0 + 3 * HALO)
    sign = north_sign()

    def got(v, upper):
        a, b = ra_ref[v], rb_ref[v]
        w, e = jnp.where(even, b, a), jnp.where(even, a, b)
        if upper:
            w, e = roll(w, SUBLANES // 2, 0), roll(e, SUBLANES // 2, 0)
        return w, e

    def edge_row(f, k):
        own = own_columns(row(own_ref, f, k - HALO), row(own_ref, f, sh.ext - 1 - k - HALO))
        v, at, upper = sh.strip(k, f)
        w, e = got(v, upper)
        w, e = roll(w, -at), roll(e, EAST0 + 2 * HALO - at)
        i = sh.ext - 1 - k - sh.fold_first
        if i >= 0:
            v, h, upper = sh.block(i, f)
            w2, e2 = got(v, upper)
            w2 = roll(w2, HALF - (HALF * h + HALF - HALO))
            e2 = roll(e2, HALF + EAST0 + 2 * HALO - HALF * h)
        yield
        value = merge_own(own, low, east_own)
        if i >= 0:
            w, e = jnp.where(low, w, w2), jnp.where(low, e, e2)
        value = jnp.where(west_halo, w, jnp.where(east_halo, e, value))
        if f == COEF:
            put_edge_coefs(coef_ref, k - HALO, value, sign)
        else:
            put_row(start_ref, f, k - HALO, value)

    run_staged([edge_row(f, k) for k in range(HALO, sh.mid) for f in range(FIELDS)], 8)

    rows = sh.mid - HALO
    chain = []
    for step in range(1, SUBCYCLES + 1):
        source = start_ref if step == 1 else hist_ref.at[step - 2]
        chain.append(
            Sweep(
                (2 * step - 1, rows),
                (2 * step, rows),
                functools.partial(row, source),
                functools.partial(coef, coef_ref),
                functools.partial(put_row, hist_ref.at[step - 1]),
                mirror=rows,
                down=True,
            )
        )
    run_chains([chain])


def own_columns(a, b):
    east = EAST0 - (LANES - 2 * HALO)
    return roll(a, HALO), roll(a, east), roll(b, HALF + HALO), roll(b, HALF + east)


def merge_own(parts, low, east_own):
    aw, ae, bw, be = parts
    return jnp.where(east_own, jnp.where(low, ae, be), jnp.where(low, aw, bw))


def put_edge_coefs(ref, k, value, sign):
    at = SUBLANES * k
    thick = value[0:1]
    ref[at : at + 2, :] = value[0:2]
    ref[at + 2 : at + 3, :] = value[2:3] * sign[0:1]
    ref[at + 3 : at + 4, :] = value[3:4]
    ref[at + WET : at + WET + 1, :] = jnp.where(thick > 0, 1.0, 0.0).astype(F32)
    ref[at + NORTH_THICK : at + NORTH_THICK + 1, :] = thick * sign[0:1]


class Wedges:
    def __init__(self, sh, own=None, hist=None, edges=(None,) * 3, main=None, edge=None):
        self.sh, self.own, self.hist = sh, own, hist
        self.start, self.ecoef, self.ehist = edges
        self.main, self.begin, self.main_c = main
        self.edge, self.edge_c = edge or (None, None)
        lane = lane_ids()
        self.low = lane < HALF
        self.half_lane = half = lane & (HALF - 1)
        self.east_own = (half >= EAST0) & (half < EAST0 + 2 * HALO)
        halo = (half < HALO) | ((half >= EAST0 + 2 * HALO) & (half < EAST0 + 3 * HALO))
        self.halo_south, self.halo_north = halo & self.low, halo & (lane >= HALF)
        self.sign = north_sign()

    SHAPES = (
        (STATE, 4 * HALO * SUBLANES, LANES),
        (4 * HALO * SUBLANES, LANES),
        (FIELDS, 2 * HALO * SUBLANES, LANES),
        (HALO * SUBLANES, LANES),
    )

    def at(self, r):
        span = 2 * HALO
        return r if r < span else r - (self.sh.ext - span) + span

    def main_row(self, f, r):
        if f == COEF:
            at = SUBLANES * self.at(r)
            return self.main_c[at : at + SUBLANES, :]
        return row(self.main, f, self.at(r))

    def first_row(self, f, r):
        return self.main_row(f, r) if f == COEF else row(self.begin, f, self.at(r))

    def put_main(self, f, r, value):
        if f < STATE:
            put_row(self.main, f, self.at(r), value)
            return
        at = SUBLANES * self.at(r)
        self.main_c[at : at + SUBLANES, :] = value
        self.main_c[at + WET : at + WET + 1, :] = jnp.where(value[0:1] > 0, 1.0, 0.0).astype(F32)

    def put_halo(self, f, r, value):
        north = r >= self.sh.mid
        k, mask = (self.sh.ext - 1 - r, self.halo_north) if north else (r, self.halo_south)
        put_row(self.edge, f, k, jnp.where(mask, value, row(self.edge, f, k)))

    def band(self, north):
        return [self.sh.ext - HALO + i if north else i for i in range(HALO)]

    def take_rows(self, ref, north):
        for f in range(FIELDS):
            for i, r in enumerate(self.band(north)):
                if ref is None:
                    value = jnp.zeros((SUBLANES, LANES), F32)
                elif f < STATE:
                    value = ref[f * HALO + i]
                else:
                    value = ref[STATE * HALO + i % PAIRS]
                    value = value if i < PAIRS else roll(value, SUBLANES // 2, 0)
                self.put_main(f, r, value)
                if f < STATE and self.begin is not self.main:
                    put_row(self.begin, f, self.at(r), value)

    def take_halos(self, ref, first, north):
        base = HALF if north else 0
        if ref is None:
            for f in range(FIELDS):
                for r in self.band(north):
                    self.put_halo(f, r, jnp.zeros((SUBLANES, LANES), F32))
            return

        def band_row(f, i, r):
            v, at = self.sh.corner(i, f)
            v = ref[v - self.sh.main + first]
            out_by = self.sh.away(i + 1 if north else HALO - i)
            w = roll(v, base - at + out_by)
            e = roll(v, base + EAST0 + HALO - at - out_by)
            yield
            self.put_halo(f, r, jnp.where(self.half_lane < HALO, w, e))

        rows = list(enumerate(self.band(north)))
        run_staged([band_row(f, i, r) for f in range(FIELDS) for i, r in rows], 16)

    def edge_own(self, out, north_only=False):
        def edge_row(f, k):
            b = self.first_row(f, self.sh.ext - 1 - k)
            parts = own_columns(b if north_only else self.first_row(f, k), b)
            yield
            put_row(out, f, k, merge_own(parts, self.low, self.east_own))

        run_staged([edge_row(f, k) for k in range(HALO) for f in range(FIELDS)], 8)

    def edge_coefs(self):
        for k in range(HALO):
            put_edge_coefs(self.edge_c, k, row(self.edge, COEF, k), self.sign)

    def steps(self, sides):
        ext = self.sh.ext

        def put_edge(f, k, value):
            put_row(self.edge, f, k, value)

        def edge_coef(k, c):
            return coef(self.edge_c, k, c) if k < HALO else coef(self.ecoef, k - HALO, c)

        def main_coef(r, c):
            if HALO <= r < ext - HALO:
                return coef(self.own.at[COEF], r - HALO, c)
            return coef(self.main_c, self.at(r), c)

        edges, south, north = [], [], []
        for step in range(1, SUBCYCLES + 1):
            first, ready = 2 * step - 2, 2 * step + HALO - 2

            def old_main(f, r, step=step, ready=ready):
                if ready <= r < ext - ready:
                    return row(self.own if step == 1 else self.hist.at[step - 2], f, r - HALO)
                return self.main_row(f, r)

            def old_edge(f, k, step=step, ready=ready):
                if k >= ready:
                    return row(self.start if step == 1 else self.ehist.at[step - 2], f, k - HALO)
                return row(self.edge, f, k)

            def known_main(r, step=step):
                return row(self.hist.at[step - 1], 0, r - HALO)

            def known_edge(k, step=step):
                return row(self.ehist.at[step - 1], 0, k - HALO)

            elev, vel = (first + 1, ready + 1), (first + 2, ready + 2)
            edges.append(
                Sweep(
                    elev,
                    vel,
                    old_edge,
                    edge_coef,
                    put_edge,
                    known_edge,
                    mirror=self.sh.mid,
                    down=True,
                )
            )
            south.append(
                Sweep(elev, vel, old_main, main_coef, self.put_main, known_main, down=True)
            )
            elev, vel = [(ext - rows[1], ext - rows[0]) for rows in (elev, vel)]
            north.append(Sweep(elev, vel, old_main, main_coef, self.put_main, known_main))
        chains = {"edges": edges, "south": south, "north": north}
        run_chains([chains[name] for name in sides])

    def output(self, first, last, put, fields=range(STATE)):
        ext, mid, ready = self.sh.ext, self.sh.mid, 2 * HALO
        final, e_final = self.hist.at[SUBCYCLES - 1], self.ehist.at[SUBCYCLES - 1]
        lane = lane_ids()

        def output_row(f, r):
            k, h = (r, 0) if r < mid else (ext - 1 - r, HALF)
            v = row(self.edge, f, k) if k < ready else row(e_final, f, k - HALO)
            w, e = roll(v, -(h + HALO)), roll(v, LANES - HALO - (h + EAST0 + HALO))
            yield
            inner = ready <= r < ext - ready
            v = row(final, f, r - HALO) if inner else self.main_row(f, r)
            v = jnp.where(lane < HALO, w, jnp.where(lane >= LANES - HALO, e, v))
            put(f, r - HALO, v)

        run_staged([output_row(f, r) for f in fields for r in range(first, last)], 16)


def for_bands(sizes, n_lat, take):
    lat_size, _ = sizes
    lat = lax.axis_index("lat")
    lat_even = lax.rem(lat, 2) == 0
    lat_odd = jnp.logical_not(lat_even)
    at_top = lat == lat_size - 1
    pl.when(at_top)(lambda: take(None, True))
    pl.when(lat == 0)(lambda: take(None, False))
    pl.when(lat_even)(lambda: take(0, True))
    pl.when(lat_odd)(lambda: take(0, False))
    if n_lat == 2:
        pl.when(lat_odd & jnp.logical_not(at_top))(lambda: take(1, True))
        pl.when(lat_even & (lat > 0))(lambda: take(1, False))


def wedge_rows_kernel(sh, sizes, n_lat, *refs):
    bands, (own_ref, hist_ref, main, edge_out, order_out, begin, main_c) = (
        refs[:n_lat],
        refs[n_lat:],
    )
    wedges = Wedges(sh, own_ref, hist_ref, main=(main, begin, main_c))
    order_out[...] = jnp.zeros((SUBLANES, LANES), F32)

    def take(n, north):
        wedges.take_rows(None if n is None else bands[n], north)

    for_bands(sizes, n_lat, take)
    wedges.edge_own(edge_out)
    wedges.steps(("south", "north"))


def wedge_edges_kernel(sh, sizes, n_lat, *refs):
    corners, refs = refs[:n_lat], refs[n_lat:]
    hist_ref, main, edge_own, edges = refs[0], refs[1], refs[2], refs[3:6]
    (out_ref, order_out), kept, edge = refs[6:8], refs[8:11], refs[11:]
    wedges = Wedges(sh, None, hist_ref, edges, (main, None, None), edge)
    order_out[...] = jnp.zeros((SUBLANES, LANES), F32)
    for f in range(FIELDS):
        for k in range(HALO):
            put_row(edge[0], f, k, row(edge_own, f, k))

    for k in range(HALO + 1):
        at = slice(SUBLANES * k, SUBLANES * (k + 1))
        kept[1][at, :] = edges[1][at, :]
    for f in range(STATE):
        for k in range(2):
            put_row(kept[0], f, k, row(edges[0], f, k))
        for n in range(SUBCYCLES):
            for k in range(2 * n + 1, 2 * n + 4):
                put_row(kept[2].at[n], f, k, row(edges[2].at[n], f, k))

    def take(n, north):
        wedges.take_halos(None if n is None else corners[n], 0, north)

    for_bands(sizes, n_lat, take)
    wedges.edge_coefs()
    wedges.steps(("edges",))
    out_flat = flat_rows(out_ref)

    def put(f, r, value):
        out_flat[f, pl.ds(r, SUBLANES, stride=sh.height), :] = value

    wedges.output(HALO, sh.ext - HALO, put)


def north_kernel(sh, sizes, got_ref, sent_ref, first_ref, order_ref, *outs):
    main, main_c, edge, edge_c = outs[:4]
    fold_ref = outs[4]
    lat_size, lon_size = sizes

    @pl.when(lax.axis_index("lat") == lat_size - 1)
    def _():
        facing = lax.rem(first_ref[...] - lax.axis_index("lon") + lon_size, lon_size)
        itself = facing == lax.axis_index("lon")
        for v in range(sh.band):
            fold_ref[v] = jnp.where(itself, sent_ref[v], got_ref[v])
        wedges = Wedges(sh, main=(main, main, main_c), edge=(edge, edge_c))
        wedges.take_rows(fold_ref, True)
        wedges.edge_own(edge, north_only=True)
        wedges.take_halos(fold_ref, sh.main, True)
        wedges.edge_coefs()


def last_kernel(sh, sizes, *refs):
    lat_size, _ = sizes
    done_ref, state, begin = refs[0], refs[1:6], refs[6:10]
    out_hbm, late_ref, sems, main, edge = refs[10:]
    height, ext = sh.height, sh.ext
    split = (height - HALO) // SUBLANES * SUBLANES
    at_top = lax.axis_index("lat") == lat_size - 1
    lines = (pl.ds(0, split), pl.ds(split, height - split))

    def copies(source, part):
        return [
            pltpu.make_async_copy(
                source.at[f, :, lines[part]], out_hbm.at[f, :, lines[part]], sems.at[part, f]
            )
            for f in range(STATE)
        ]

    early = copies(done_ref, 0)
    for copy in early:
        copy.start()

    @pl.when(jnp.logical_not(at_top))
    def _():
        rest = copies(done_ref, 1)
        for copy in rest:
            copy.start()
        for copy in rest:
            copy.wait()

    @pl.when(at_top)
    def _():
        wedges = Wedges(
            sh, *state[:2], state[2:], (main, main, begin[1]), (edge, begin[3])
        )
        for f in range(STATE):
            for k in range(HALO):
                put_row(edge, f, k, row(begin[2], f, k))
                at = wedges.at(ext - 1 - k)
                put_row(main, f, at, row(begin[0], f, at))
        late_flat, done_flat = flat_rows(late_ref), flat_rows(done_ref)

        def put(f, r, value):
            late_flat[f, pl.ds(r, SUBLANES, stride=height), :] = value

        for f in range(STATE):
            for r in range(split, height - HALO):
                put(f, r, done_flat[f, pl.ds(r, SUBLANES, stride=height), :])
        wedges.steps(("edges", "north"))
        rest = copies(late_ref, 1)
        for f, copy in enumerate(rest):
            wedges.output(ext - 2 * HALO, ext - HALO, put, (f,))
            copy.start()
        for copy in rest:
            copy.wait()

    for copy in early:
        copy.wait()


def pair_swaps(size, wrap):
    first = [(i, i ^ 1) for i in range(size)]
    second = []
    for i in range(size):
        j = i + 1 if i % 2 else i - 1
        if wrap or 0 <= j < size:
            second.append((i, j % size))
    return first, second


def vmem(n):
    return [pl.BlockSpec(memory_space=pltpu.VMEM)] * n


def in_hbm(x):
    return pltpu.with_memory_space_constraint(x, pltpu.HBM)


def smem():
    return pl.BlockSpec(memory_space=pltpu.SMEM)


def on_device(mesh_sizes, perturb, background, land_mask, levels, fold_partner):
    lat_size, lon_size, dir_size = mesh_sizes
    height = perturb.shape[2]
    sh = Shapes(height)
    sizes = (lat_size, lon_size)
    flat = perturb.reshape(STATE, SUBLANES * height, LANES)
    tile = (SUBLANES, LANES)

    def shape(n):
        return pltpu.VMEM((n,) + tile, F32)

    params = pltpu.CompilerParams(vmem_limit_bytes=16 * 1024 * 1024)
    rows = SUBLANES * height
    n_lat = 1 if lat_size == 2 else 2
    side_a, side_b, own, *lat_out = pl.pallas_call(
        functools.partial(sides_kernel, sh, sizes),
        out_shape=(
            shape(sh.side),
            shape(sh.side),
            pltpu.VMEM((FIELDS, rows, LANES), F32),
        )
        + (shape(sh.main),) * n_lat,
        in_specs=[pl.BlockSpec(memory_space=pltpu.HBM)] * 4,
        out_specs=tuple(vmem(3 + n_lat)),
        scratch_shapes=[
            pltpu.VMEM(flat.shape, F32),
            pltpu.VMEM(background.shape, F32),
            pltpu.VMEM(land_mask.shape, jnp.int32),
            pltpu.VMEM(levels.shape, jnp.int32),
            pltpu.SemaphoreType.DMA((3 + STATE,)),
        ],
        compiler_params=params,
        name="sides",
    )(*[in_hbm(v) for v in (flat, background, land_mask, levels)])

    lon_swaps = pair_swaps(lon_size, True)
    got_a, got_b = [lax.ppermute(x, "lon", swap) for x, swap in zip((side_a, side_b), lon_swaps)]

    hist, place, first, branch = pl.pallas_call(
        functools.partial(middle_kernel, sh, sizes),
        out_shape=(
            pltpu.VMEM((SUBCYCLES, STATE, rows, LANES), F32),
            pltpu.VMEM(tile, jnp.int32),
            pltpu.VMEM(tile, jnp.int32),
            jax.ShapeDtypeStruct((1,), jnp.int32),
        ),
        in_specs=vmem(1) + [pl.BlockSpec(memory_space=pltpu.HBM)],
        out_specs=tuple(vmem(3)) + (smem(),),
        scratch_shapes=[
            pltpu.SMEM(fold_partner.shape, jnp.int32),
            pltpu.SemaphoreType.DMA,
        ],
        compiler_params=params,
        name="middle",
    )(own, in_hbm(fold_partner))
    lat_swaps = pair_swaps(lat_size, False)[:n_lat]
    got_lat = [lax.ppermute(x, "lat", swap) for x, swap in zip(lat_out, lat_swaps)]
    wedge_main, edge_own, order = pl.pallas_call(
        functools.partial(wedge_rows_kernel, sh, sizes, n_lat),
        out_shape=(
            pltpu.VMEM(Wedges.SHAPES[0], F32),
            pltpu.VMEM(Wedges.SHAPES[2], F32),
            pltpu.VMEM(tile, F32),
        ),
        in_specs=vmem(n_lat + 2),
        out_specs=tuple(vmem(3)),
        scratch_shapes=[pltpu.VMEM(x, F32) for x in Wedges.SHAPES[:2]],
        compiler_params=params,
        name="wedge_rows",
    )(*got_lat, own, hist)
    fold_band, *lat_corners = pl.pallas_call(
        functools.partial(bands_kernel, sh, sizes),
        out_shape=(shape(sh.band),) + (shape(sh.corners),) * n_lat,
        in_specs=vmem(5),
        out_specs=tuple(vmem(1 + n_lat)),
        compiler_params=params,
        name="bands",
    )(own, got_a, got_b, place, order)

    edge_rows = SUBLANES * (sh.mid - HALO)
    edge_shapes = (
        pltpu.VMEM((STATE, edge_rows, LANES), F32),
        pltpu.VMEM((edge_rows, LANES), F32),
        pltpu.VMEM((SUBCYCLES, STATE, edge_rows, LANES), F32),
    )
    step_edges = jax.jit(
        pl.pallas_call(
            functools.partial(edges_kernel, sh),
            out_shape=edge_shapes,
            in_specs=vmem(3),
            out_specs=tuple(vmem(3)),
            compiler_params=params,
            name="edges",
        )
    )
    step_wedge_edges = jax.jit(
        pl.pallas_call(
            functools.partial(wedge_edges_kernel, sh, sizes, n_lat),
            out_shape=(pltpu.VMEM(perturb.shape, F32), pltpu.VMEM(tile, F32)) + edge_shapes,
            in_specs=vmem(n_lat + 6),
            out_specs=tuple(vmem(5)),
            scratch_shapes=[pltpu.VMEM(x, F32) for x in Wedges.SHAPES[2:]],
            compiler_params=params,
            name="wedge_edges",
        )
    )
    take_north = jax.jit(
        pl.pallas_call(
            functools.partial(north_kernel, sh, sizes),
            out_shape=tuple(pltpu.VMEM(x, F32) for x in Wedges.SHAPES),
            in_specs=vmem(4),
            out_specs=tuple(vmem(4)),
            scratch_shapes=[pltpu.VMEM((sh.band,) + tile, F32)],
            compiler_params=params,
            name="north",
        )
    )
    def rest(q, fold_band, lat_corners, wedge_main, edge_own, own, hist, got_a, got_b, first):
        across = []
        for m in range(lon_size):
            j = (q - m) % lon_size
            for a in range(lat_size):
                for d in range(dir_size):
                    source, target = (m, a, d), (j, a, d if j != m else d ^ 1)
                    across.append(
                        tuple((x * lat_size + y) * dir_size + z for x, y, z in (source, target))
                    )
        got_fold = lax.ppermute(fold_band, ("lon", "lat", "dir"), across)
        got_corners = [lax.ppermute(x, "lat", swap) for x, swap in zip(lat_corners, lat_swaps)]
        edges = step_edges(own, got_a, got_b)
        done, order, *kept = step_wedge_edges(*got_corners, hist, wedge_main, edge_own, *edges)
        return kept, done, take_north(got_fold, fold_band, first, order)

    edges, done, beyond = lax.switch(
        branch[0],
        [functools.partial(rest, q) for q in range(lon_size)],
        fold_band,
        lat_corners,
        wedge_main,
        edge_own,
        own,
        hist,
        got_a,
        got_b,
        first,
    )
    return pl.pallas_call(
        functools.partial(last_kernel, sh, sizes),
        out_shape=jax.ShapeDtypeStruct(perturb.shape, F32),
        in_specs=vmem(10),
        out_specs=pl.BlockSpec(memory_space=pltpu.HBM),
        scratch_shapes=[
            pltpu.VMEM(perturb.shape, F32),
            pltpu.SemaphoreType.DMA((2, STATE)),
            pltpu.VMEM(Wedges.SHAPES[0], F32),
            pltpu.VMEM(Wedges.SHAPES[2], F32),
        ],
        compiler_params=params,
        name="last",
    )(done, own, hist, *edges, *beyond)


def solution(mesh):
    placed = (
        P("grp", "dir", "lat", "lon"),
        P("grp", "lat", "lon"),
        P("lat", "lon"),
        P("lat", "lon"),
        P(),
    )
    sizes = tuple(mesh.shape[axis] for axis in ("lat", "lon", "dir"))
    return jax.shard_map(
        functools.partial(on_device, sizes),
        mesh=mesh,
        in_specs=placed,
        out_specs=P("grp", "dir", "lat", "lon"),
        check_vma=False,
    )
```

```python
import functools
from collections import deque

import jax
import jax.numpy as jnp
from jax import lax
from jax.experimental import pallas as pl
from jax.experimental.pallas import tpu as pltpu
from jax.sharding import PartitionSpec as P

SUBCYCLES = 5
NLEV = 90
TIME_STEP = 0.35
HALF_STEP = 0.5 * TIME_STEP

LANES = 128
SUBLANES = 8
HALF = LANES // 2
HALO = 2 * SUBCYCLES
PAIRS = HALO // 2
FIELDS = 4
STATE = 3
COEF = 3
STRIP_SLOTS = HALF // HALO
CORNER_SLOTS = LANES // (2 * HALO)
F32 = jnp.float32


def ceil_div(a, b):
    return -(-a // b)


class Shapes:
    def __init__(self, height):
        self.height = height
        self.ext = height + 2 * HALO
        self.mid = self.ext // 2
        self.fold_first = height
        self.blocks = STATE * PAIRS + ceil_div(PAIRS, 2)
        self.strip_rows = self.mid - HALO
        self.strip_pairs = self.strip_rows // 2
        slots = self.strip_rows * STATE + self.strip_pairs
        self.side = self.blocks + ceil_div(slots, STRIP_SLOTS)
        self.main = STATE * HALO + PAIRS
        self.corners = ceil_div(FIELDS * PAIRS, CORNER_SLOTS)
        self.band = self.main + self.corners

    def block(self, i, f):
        upper = i // PAIRS
        if f < STATE:
            return f * PAIRS + i % PAIRS, upper, False
        return STATE * PAIRS + i % PAIRS // 2, i % PAIRS % 2, upper == 1

    def strip(self, k, f):
        slot, upper = (k - HALO) * STATE + f, False
        if f == COEF:
            upper = k - HALO >= self.strip_pairs
            slot = self.strip_rows * STATE + (k - HALO) % self.strip_pairs
        return self.blocks + slot // STRIP_SLOTS, HALO * (slot % STRIP_SLOTS), upper

    def corner(self, i, f):
        slot = f * PAIRS + min(i, HALO - 1 - i)
        return self.main + slot // CORNER_SLOTS, 2 * HALO * (slot % CORNER_SLOTS)

    @staticmethod
    def away(d):
        return d if d > PAIRS else 0

    @staticmethod
    def corner_lanes(d):
        west, east = (d, HALO - 1), (HALO, 2 * HALO - 1 - d)
        if d > PAIRS:
            west, east = (0, HALO - 1 - d), (HALO + d, 2 * HALO - 1)
        return west, east


def by_register(items, where):
    groups = {}
    for i, f in items:
        v, at = where(i, f)
        groups.setdefault(v, []).append((i, f, at))
    return groups


def roll(x, shift, axis=1):
    shift = shift % x.shape[axis]
    return x if shift == 0 else pltpu.roll(x, shift, axis)


def lane_ids():
    return lax.broadcasted_iota(jnp.int32, (SUBLANES, LANES), 1)


def sublane_ids():
    return lax.broadcasted_iota(jnp.int32, (SUBLANES, LANES), 0)


def run_staged(tasks, window):
    waiting = deque()

    def advance(task):
        try:
            next(task)
        except StopIteration:
            return
        waiting.append(task)

    for task in tasks:
        advance(task)
        while len(waiting) >= window:
            advance(waiting.popleft())
    while waiting:
        advance(waiting.popleft())


def row(ref, f, r):
    return ref[f, SUBLANES * r : SUBLANES * (r + 1), :]


def put_row(ref, f, r, value):
    ref[f, SUBLANES * r : SUBLANES * (r + 1), :] = value


def flat_rows(ref):
    return ref.reshape(ref.shape[0], ref.shape[1] * ref.shape[2], ref.shape[3])


def coef(ref, r, c):
    return jnp.broadcast_to(ref[SUBLANES * r + c : SUBLANES * r + c + 1, :], (SUBLANES, LANES))


def even_lon():
    return jnp.full((SUBLANES, LANES), lax.rem(lax.axis_index("lon"), 2), jnp.int32) == 0


def fold_place(fold_ref, lon_size):
    pivot = fold_ref[0]
    block = pivot // LANES
    rest = pivot - block * LANES
    low = rest < HALF
    place = jnp.where(low, rest + LANES, rest)
    branch = jnp.where(low, block - 1 + lon_size, block)
    return lax.rem(branch, lon_size), place


def pair_coefs(a, b):
    return jnp.where(sublane_ids() < SUBLANES // 2, a, roll(b, SUBLANES // 2, 0))


def lat_rows(sh, own_ref, outs):
    own = functools.partial(row, own_ref)

    def raw_rows(out, first):
        for f in range(STATE):
            for i in range(HALO):
                out[f * HALO + i] = own(f, first + i)
        for i in range(PAIRS):
            out[STATE * HALO + i] = pair_coefs(
                own(COEF, first + i), own(COEF, first + i + PAIRS)
            )

    top = sh.height - HALO
    lat_even = lax.rem(lax.axis_index("lat"), 2) == 0

    @pl.when(lat_even)
    def _():
        raw_rows(outs[0], top)
        if len(outs) > 1:
            raw_rows(outs[1], 0)

    @pl.when(jnp.logical_not(lat_even))
    def _():
        raw_rows(outs[0], 0)
        if len(outs) > 1:
            raw_rows(outs[1], top)


def sides_kernel(sh, sizes, x_hbm, b_hbm, m_hbm, l_hbm, *rest):
    a_out, b_out, own_ref = rest[:3]
    lat_outs, (x_ref, b_ref, m_ref, l_ref, sems) = rest[3:-5], rest[-5:]
    lat_size, _ = sizes
    height = sh.height
    copies = [
        pltpu.make_async_copy(src, dst, sems.at[n])
        for n, (src, dst) in enumerate(
            [(b_hbm, b_ref), (m_hbm, m_ref), (l_hbm, l_ref)]
            + [(x_hbm.at[f], x_ref.at[f]) for f in range(STATE)]
        )
    ]
    for copy in copies:
        copy.start()
    for copy in copies[:3]:
        copy.wait()

    wet = m_ref[...].astype(F32)
    depth = 0.5 + 1.5 * ((l_ref[...] - 1).astype(F32) / (NLEV - 1)) ** 2
    row0 = lax.axis_index("lat") * height
    rows = (row0 + lax.broadcasted_iota(jnp.int32, (height, LANES), 0)).astype(F32)
    coriolis = 0.3 + 0.2 * rows / (height * lat_size)
    planes = [
        HALF_STEP * (wet * (depth + b_ref[0])),
        HALF_STEP * b_ref[1],
        HALF_STEP * b_ref[2],
        wet * (TIME_STEP * coriolis),
        wet,
    ]
    planes += [jnp.zeros_like(wet)] * (SUBLANES - len(planes))
    for c, plane in enumerate(planes):
        for r in range(0, height, SUBLANES):
            own_ref[COEF, pl.ds(SUBLANES * r + c, SUBLANES, stride=SUBLANES), :] = plane[
                r : r + SUBLANES
            ]
    for copy in copies[3:]:
        copy.wait()
    for f in range(STATE):
        for r in range(height):
            put_row(own_ref, f, r, x_ref[f, pl.ds(r, SUBLANES, stride=height), :])

    even = even_lon()
    lane, sub = lane_ids(), sublane_ids()
    low = lane < HALF
    own = functools.partial(row, own_ref)
    top = height - HALO

    def rows_of(f, r):
        return pair_coefs(own(f, r), own(f, r + PAIRS)) if f == COEF else own(f, r)

    def strip_rows_of(f, r, other):
        return pair_coefs(own(f, r), own(f, other)) if f == COEF else own(f, r)

    def block(v, a, b):
        a_up, b_up = roll(a, HALF), roll(b, HALF)
        yield
        east = jnp.where(low, a_up, b)
        west = jnp.where(low, a, b_up)
        a_out[v] = jnp.where(even, east, west)
        b_out[v] = jnp.where(even, west, east)

    def blocks():
        for f in range(STATE):
            for i in range(PAIRS):
                yield block(f * PAIRS + i, own(f, top + i), own(f, top + i + PAIRS))
        for i in range(0, PAIRS, 2):
            v, _, _ = sh.block(i, COEF)
            yield block(v, rows_of(COEF, top + i), rows_of(COEF, top + min(i + 1, PAIRS - 1)))

    slots = {}
    for k in range(HALO, sh.mid):
        for f in range(FIELDS):
            v, at, upper = sh.strip(k, f)
            if not upper:
                slots.setdefault(v, []).append((k, f, at))

    def strips(v):
        parts = []
        for k, f, at in slots[v]:
            ahead = sh.strip_pairs
            r = sh.ext - 1 - k - HALO
            a, b = strip_rows_of(f, k - HALO, k - HALO + ahead), strip_rows_of(f, r, r - ahead)
            end = at - (LANES - HALO)
            a_east, a_west = roll(a, end), roll(a, at)
            near = sh.ext - 1 - k < sh.fold_first
            near_other = sh.ext - 1 - k - ahead < sh.fold_first
            b_east, b_west = roll(b, HALF + end), roll(b, HALF + at)
            if not near:
                b_east, b_west = roll(b, end), roll(b, at)
                if f == COEF and near_other:
                    lower_half = sub < SUBLANES // 2
                    b_east = jnp.where(lower_half, b_east, roll(b, HALF + end))
                    b_west = jnp.where(lower_half, b_west, roll(b, HALF + at))
            parts.append((at, a_east, b_east, a_west, b_west))
        yield
        east = west = jnp.zeros((SUBLANES, LANES), F32)
        for at, ea, eb, wa, wb in parts:
            here = (lane >= at) & (lane < at + HALO)
            there = (lane >= HALF + at) & (lane < HALF + at + HALO)
            east = jnp.where(here, ea, jnp.where(there, eb, east))
            west = jnp.where(here, wa, jnp.where(there, wb, west))
        a_out[v] = jnp.where(even, east, west)
        b_out[v] = jnp.where(even, west, east)

    run_staged(blocks(), 10)
    run_staged([strips(v) for v in sorted(slots)], 2)
    lat_rows(sh, own_ref, lat_outs)


def bands_kernel(sh, sizes, own_ref, ra_ref, rb_ref, place_ref, order_ref, fold_out, *lat_outs):
    lat_size, _ = sizes
    even = even_lon()
    lane, sub = lane_ids(), sublane_ids()
    low = lane < HALF
    own = functools.partial(row, own_ref)
    top = sh.height - HALO

    def got(v, upper):
        a, b = ra_ref[v], rb_ref[v]
        w, e = jnp.where(even, b, a), jnp.where(even, a, b)
        if upper:
            w, e = roll(w, SUBLANES // 2, 0), roll(e, SUBLANES // 2, 0)
        return w, e

    def corners(out, is_top):
        def register(v, items):
            parts = []
            for i, f, at in items:
                if is_top:
                    src, h, upper = sh.block(i, f)
                    w_at, e_at = HALF * h + HALF - HALO, HALF * h
                else:
                    src, w_at, upper = sh.strip(HALO + i, f)
                    e_at = w_at
                w, e = got(src, upper)
                d = HALO - i if is_top else i + 1
                out_by = sh.away(d)
                w, e = roll(w, at - w_at - out_by), roll(e, at + HALO - e_at + out_by)
                parts.append((at, d, w, e))
            yield
            total = jnp.zeros((SUBLANES, LANES), F32)
            for at, d, w, e in parts:
                for (start, end), value in zip(sh.corner_lanes(d), (w, e)):
                    if start <= end:
                        total = jnp.where((lane >= at + start) & (lane <= at + end), value, total)
            out[v - sh.main] = total

        groups = by_register([(i, f) for f in range(FIELDS) for i in range(HALO)], sh.corner)
        run_staged([register(v, items) for v, items in groups.items()], 3)

    lat_even = lax.rem(lax.axis_index("lat"), 2) == 0

    @pl.when(lat_even)
    def _():
        corners(lat_outs[0], True)
        if len(lat_outs) > 1:
            corners(lat_outs[1], False)

    @pl.when(jnp.logical_not(lat_even))
    def _():
        corners(lat_outs[0], False)
        if len(lat_outs) > 1:
            corners(lat_outs[1], True)

    @pl.when(lax.axis_index("lat") == lat_size - 1)
    def _():
        where_to = place_ref[...]
        rest = where_to & (LANES - 1)
        eastern = where_to >= LANES
        backwards = (where_to - lane) & (LANES - 1)
        main_own = (eastern & (lane >= rest + 1)) | (jnp.logical_not(eastern) & (lane <= rest))
        upper = (lane >= rest + 1) & (lane <= rest + HALO)
        lower = (lane >= rest + 1 - HALO) & (lane <= rest)
        side_own = (eastern & lower) | (jnp.logical_not(eastern) & upper)
        side_far = (eastern & upper & (lane >= HALF)) | (
            jnp.logical_not(eastern) & lower & (lane < HALF)
        )
        coef_signs = jnp.where((sub == 1) | (sub == 2), -1.0, 1.0).astype(F32)

        def reversed_row(f, i):
            v, h, upper = sh.block(i, f)
            w, e = got(v, upper)
            if h == 0:
                w = roll(w, HALF)
            else:
                e = roll(e, HALF)
            v, at, upper = sh.strip(sh.ext - 1 - sh.fold_first - i, f)
            far_w, far_e = got(v, upper)
            far_w, far_e = roll(far_w, -HALO - at), roll(far_e, -at)
            yield
            both = jnp.where(low, e, w)
            mine = own(f, top + i)
            main = jnp.where(main_own, mine, both)
            side = jnp.where(
                side_own, mine, jnp.where(side_far, jnp.where(low, far_w, far_e), both)
            )
            if f == COEF:
                main, side = main * coef_signs, side * coef_signs
            elif f > 0:
                main, side = -main, -side
            main = jnp.take_along_axis(main, backwards, axis=1)
            side = jnp.take_along_axis(side, backwards, axis=1)
            yield
            j = HALO - 1 - i
            v, at = sh.corner(j, f)
            d = j + 1
            out_by = sh.away(d)
            moves = (-out_by, out_by) if out_by else (0,)
            moved = [roll(side, at - (LANES - HALO) + by) for by in moves]
            if f < STATE:
                fold_out[f * HALO + j] = main
            elif j < PAIRS:
                v2 = STATE * HALO + j
                fold_out[v2] = jnp.where(sub < SUBLANES // 2, main, fold_out[v2])
            else:
                fold_out[STATE * HALO + j - PAIRS] = roll(main, SUBLANES // 2, 0)
            yield
            total = fold_out[v]
            for (start, end), value in zip(sh.corner_lanes(d), (moved[0], moved[-1])):
                if start <= end:
                    total = jnp.where((lane >= at + start) & (lane <= at + end), value, total)
            fold_out[v] = total

        for v in range(STATE * HALO, sh.band):
            fold_out[v] = jnp.zeros((SUBLANES, LANES), F32)
        run_staged([reversed_row(f, i) for f in range(FIELDS) for i in range(HALO)], 14)


EAST0 = HALF // 2
LAG = 4
WET, NORTH_THICK = 4, 5


def north_sign():
    return jnp.where(lane_ids() < HALF, 1.0, -1.0).astype(F32)


class Sweep:
    def __init__(self, elev, vel, old, coef, put, known=None, mirror=None, down=False):
        self.elev_rows, self.vel_rows = elev, vel
        self.old, self.coef, self.put, self.known, self.mirror = old, coef, put, known, mirror
        self.flux_n, self.rolled, self.new, self.slopes = {}, {}, {}, {}
        self.sign = HALF_STEP * north_sign() if mirror is not None else HALF_STEP
        self.low, self.high = min(elev[0] - 1, vel[0]), max(elev[1], vel[1] - 1)
        self.down = down
        self.length = self.high - self.low + 1 + 2 * LAG

    def flux(self, r):
        lo, hi = self.elev_rows
        if not lo - 1 <= r <= hi or r == self.mirror:
            return
        eta, merid = self.old(0, r), self.old(2, r)
        thick = self.coef(r, 0)
        thick_n = thick if self.mirror is None else self.coef(r, NORTH_THICK)
        self.flux_n[r] = thick_n * merid + self.coef(r, 2) * eta
        if lo <= r < hi:
            east = thick * self.old(1, r) + self.coef(r, 1) * eta
            self.rolled[r] = (roll(east, -1), roll(east, 1))
        if self.mirror is not None and r == self.mirror - 1:
            self.flux_n[r + 1] = -roll(self.flux_n[r], HALF)

    def elevation(self, r):
        lo, hi = self.elev_rows
        if not lo <= r < hi:
            return
        plus, minus = self.rolled.pop(r)
        change = (plus - minus) + (self.flux_n[r + 1] - self.flux_n[r - 1])
        eta = self.coef(r, WET) * (self.old(0, r) - change)
        self.new[r] = eta
        self.put(0, r, eta)
        if self.mirror is not None and r == self.mirror - 1:
            self.new[r + 1] = roll(eta, HALF)

    def get_new(self, r):
        if r not in self.new:
            self.new[r] = self.known(r)
            if self.vel_rows[0] <= r < self.vel_rows[1]:
                self.put(0, r, self.new[r])
        return self.new[r]

    def slope(self, r):
        if self.vel_rows[0] <= r < self.vel_rows[1]:
            eta = self.get_new(r)
            self.slopes[r] = (roll(eta, -1), roll(eta, 1))

    def velocity(self, r):
        if not self.vel_rows[0] <= r < self.vel_rows[1]:
            return
        plus, minus = self.slopes.pop(r)
        wet, turn = self.coef(r, WET), self.coef(r, 3)
        zonal, merid = self.old(1, r), self.old(2, r)
        zonal = wet * (zonal - HALF_STEP * (plus - minus)) + turn * merid
        slope = self.sign * (self.get_new(r + 1) - self.get_new(r - 1))
        merid = wet * (merid - slope) - turn * zonal
        self.put(1, r, zonal)
        self.put(2, r, merid)

    def row_at(self, n):
        return self.high - n if self.down else self.low + n

    def offset_from(self, before):
        ahead = before.high - self.high if self.down else self.low - before.low
        return max(2 * LAG + ahead, 0)

    def advance(self, n):
        self.flux(self.row_at(n))
        self.elevation(self.row_at(n - LAG))
        self.slope(self.row_at(n - LAG))
        self.velocity(self.row_at(n - 2 * LAG))


def run_chains(chains):
    waiting = []
    for chain in chains:
        at = 0
        for n, sweep in enumerate(chain):
            at += sweep.offset_from(chain[n - 1]) if n else 0
            waiting.append((n, at, sweep))
    waiting.sort(key=lambda entry: entry[0])
    for t in range(max(at + sweep.length for _, at, sweep in waiting)):
        for _, at, sweep in waiting:
            if at <= t < at + sweep.length:
                sweep.advance(t - at)


def middle_kernel(sh, sizes, own_ref, p_hbm, hist_ref, place_out, first_out, q_out, p_ref, sem):
    copy = pltpu.make_async_copy(p_hbm, p_ref, sem)
    copy.start()
    chain = []
    for step in range(1, SUBCYCLES + 1):
        source = own_ref if step == 1 else hist_ref.at[step - 2]
        chain.append(
            Sweep(
                (2 * step - 1, sh.height - 2 * step + 1),
                (2 * step, sh.height - 2 * step),
                functools.partial(row, source),
                functools.partial(coef, own_ref.at[COEF]),
                functools.partial(put_row, hist_ref.at[step - 1]),
            )
        )
    run_chains([chain])
    copy.wait()
    first, place = fold_place(p_ref, sizes[1])
    q_out[0] = first
    place_out[...] = jnp.full((SUBLANES, LANES), place, jnp.int32)
    first_out[...] = jnp.full((SUBLANES, LANES), first, jnp.int32)


def edges_kernel(sh, own_ref, ra_ref, rb_ref, start_ref, coef_ref, hist_ref):
    even = even_lon()
    lane = lane_ids()
    low = lane < HALF
    half_lane = lane & (HALF - 1)
    west_halo = half_lane < HALO
    east_own = (half_lane >= EAST0) & (half_lane < EAST0 + 2 * HALO)
    east_halo = (half_lane >= EAST0 + 2 * HALO) & (half_lane < EAST0 + 3 * HALO)
    sign = north_sign()

    def got(v, upper):
        a, b = ra_ref[v], rb_ref[v]
        w, e = jnp.where(even, b, a), jnp.where(even, a, b)
        if upper:
            w, e = roll(w, SUBLANES // 2, 0), roll(e, SUBLANES // 2, 0)
        return w, e

    def edge_row(f, k):
        own = own_columns(row(own_ref, f, k - HALO), row(own_ref, f, sh.ext - 1 - k - HALO))
        v, at, upper = sh.strip(k, f)
        w, e = got(v, upper)
        w, e = roll(w, -at), roll(e, EAST0 + 2 * HALO - at)
        i = sh.ext - 1 - k - sh.fold_first
        if i >= 0:
            v, h, upper = sh.block(i, f)
            w2, e2 = got(v, upper)
            w2 = roll(w2, HALF - (HALF * h + HALF - HALO))
            e2 = roll(e2, HALF + EAST0 + 2 * HALO - HALF * h)
        yield
        value = merge_own(own, low, east_own)
        if i >= 0:
            w, e = jnp.where(low, w, w2), jnp.where(low, e, e2)
        value = jnp.where(west_halo, w, jnp.where(east_halo, e, value))
        if f == COEF:
            put_edge_coefs(coef_ref, k - HALO, value, sign)
        else:
            put_row(start_ref, f, k - HALO, value)

    run_staged([edge_row(f, k) for k in range(HALO, sh.mid) for f in range(FIELDS)], 8)

    rows = sh.mid - HALO
    chain = []
    for step in range(1, SUBCYCLES + 1):
        source = start_ref if step == 1 else hist_ref.at[step - 2]
        chain.append(
            Sweep(
                (2 * step - 1, rows),
                (2 * step, rows),
                functools.partial(row, source),
                functools.partial(coef, coef_ref),
                functools.partial(put_row, hist_ref.at[step - 1]),
                mirror=rows,
                down=True,
            )
        )
    run_chains([chain])


def own_columns(a, b):
    east = EAST0 - (LANES - 2 * HALO)
    return roll(a, HALO), roll(a, east), roll(b, HALF + HALO), roll(b, HALF + east)


def merge_own(parts, low, east_own):
    aw, ae, bw, be = parts
    return jnp.where(east_own, jnp.where(low, ae, be), jnp.where(low, aw, bw))


def put_edge_coefs(ref, k, value, sign):
    at = SUBLANES * k
    thick = value[0:1]
    ref[at : at + 2, :] = value[0:2]
    ref[at + 2 : at + 3, :] = value[2:3] * sign[0:1]
    ref[at + 3 : at + 4, :] = value[3:4]
    ref[at + WET : at + WET + 1, :] = jnp.where(thick > 0, 1.0, 0.0).astype(F32)
    ref[at + NORTH_THICK : at + NORTH_THICK + 1, :] = thick * sign[0:1]


class Wedges:
    def __init__(self, sh, own=None, hist=None, edges=(None,) * 3, main=None, edge=None):
        self.sh, self.own, self.hist = sh, own, hist
        self.start, self.ecoef, self.ehist = edges
        self.main, self.begin, self.main_c = main
        self.edge, self.edge_c = edge or (None, None)
        lane = lane_ids()
        self.low = lane < HALF
        self.half_lane = half = lane & (HALF - 1)
        self.east_own = (half >= EAST0) & (half < EAST0 + 2 * HALO)
        halo = (half < HALO) | ((half >= EAST0 + 2 * HALO) & (half < EAST0 + 3 * HALO))
        self.halo_south, self.halo_north = halo & self.low, halo & (lane >= HALF)
        self.sign = north_sign()

    SHAPES = (
        (STATE, 4 * HALO * SUBLANES, LANES),
        (4 * HALO * SUBLANES, LANES),
        (FIELDS, 2 * HALO * SUBLANES, LANES),
        (HALO * SUBLANES, LANES),
    )

    def at(self, r):
        span = 2 * HALO
        return r if r < span else r - (self.sh.ext - span) + span

    def main_row(self, f, r):
        if f == COEF:
            at = SUBLANES * self.at(r)
            return self.main_c[at : at + SUBLANES, :]
        return row(self.main, f, self.at(r))

    def first_row(self, f, r):
        return self.main_row(f, r) if f == COEF else row(self.begin, f, self.at(r))

    def put_main(self, f, r, value):
        if f < STATE:
            put_row(self.main, f, self.at(r), value)
            return
        at = SUBLANES * self.at(r)
        self.main_c[at : at + SUBLANES, :] = value
        self.main_c[at + WET : at + WET + 1, :] = jnp.where(value[0:1] > 0, 1.0, 0.0).astype(F32)

    def put_halo(self, f, r, value):
        north = r >= self.sh.mid
        k, mask = (self.sh.ext - 1 - r, self.halo_north) if north else (r, self.halo_south)
        put_row(self.edge, f, k, jnp.where(mask, value, row(self.edge, f, k)))

    def band(self, north):
        return [self.sh.ext - HALO + i if north else i for i in range(HALO)]

    def take_rows(self, ref, north):
        for f in range(FIELDS):
            for i, r in enumerate(self.band(north)):
                if ref is None:
                    value = jnp.zeros((SUBLANES, LANES), F32)
                elif f < STATE:
                    value = ref[f * HALO + i]
                else:
                    value = ref[STATE * HALO + i % PAIRS]
                    value = value if i < PAIRS else roll(value, SUBLANES // 2, 0)
                self.put_main(f, r, value)
                if f < STATE and self.begin is not self.main:
                    put_row(self.begin, f, self.at(r), value)

    def take_halos(self, ref, first, north):
        base = HALF if north else 0
        if ref is None:
            for f in range(FIELDS):
                for r in self.band(north):
                    self.put_halo(f, r, jnp.zeros((SUBLANES, LANES), F32))
            return

        def band_row(f, i, r):
            v, at = self.sh.corner(i, f)
            v = ref[v - self.sh.main + first]
            out_by = self.sh.away(i + 1 if north else HALO - i)
            w = roll(v, base - at + out_by)
            e = roll(v, base + EAST0 + HALO - at - out_by)
            yield
            self.put_halo(f, r, jnp.where(self.half_lane < HALO, w, e))

        rows = list(enumerate(self.band(north)))
        run_staged([band_row(f, i, r) for f in range(FIELDS) for i, r in rows], 16)

    def edge_own(self, out, north_only=False):
        def edge_row(f, k):
            b = self.first_row(f, self.sh.ext - 1 - k)
            parts = own_columns(b if north_only else self.first_row(f, k), b)
            yield
            put_row(out, f, k, merge_own(parts, self.low, self.east_own))

        run_staged([edge_row(f, k) for k in range(HALO) for f in range(FIELDS)], 8)

    def edge_coefs(self):
        for k in range(HALO):
            put_edge_coefs(self.edge_c, k, row(self.edge, COEF, k), self.sign)

    def steps(self, sides):
        ext = self.sh.ext

        def put_edge(f, k, value):
            put_row(self.edge, f, k, value)

        def edge_coef(k, c):
            return coef(self.edge_c, k, c) if k < HALO else coef(self.ecoef, k - HALO, c)

        def main_coef(r, c):
            if HALO <= r < ext - HALO:
                return coef(self.own.at[COEF], r - HALO, c)
            return coef(self.main_c, self.at(r), c)

        edges, south, north = [], [], []
        for step in range(1, SUBCYCLES + 1):
            first, ready = 2 * step - 2, 2 * step + HALO - 2

            def old_main(f, r, step=step, ready=ready):
                if ready <= r < ext - ready:
                    return row(self.own if step == 1 else self.hist.at[step - 2], f, r - HALO)
                return self.main_row(f, r)

            def old_edge(f, k, step=step, ready=ready):
                if k >= ready:
                    return row(self.start if step == 1 else self.ehist.at[step - 2], f, k - HALO)
                return row(self.edge, f, k)

            def known_main(r, step=step):
                return row(self.hist.at[step - 1], 0, r - HALO)

            def known_edge(k, step=step):
                return row(self.ehist.at[step - 1], 0, k - HALO)

            elev, vel = (first + 1, ready + 1), (first + 2, ready + 2)
            edges.append(
                Sweep(
                    elev,
                    vel,
                    old_edge,
                    edge_coef,
                    put_edge,
                    known_edge,
                    mirror=self.sh.mid,
                    down=True,
                )
            )
            south.append(
                Sweep(elev, vel, old_main, main_coef, self.put_main, known_main, down=True)
            )
            elev, vel = [(ext - rows[1], ext - rows[0]) for rows in (elev, vel)]
            north.append(Sweep(elev, vel, old_main, main_coef, self.put_main, known_main))
        chains = {"edges": edges, "south": south, "north": north}
        run_chains([chains[name] for name in sides])

    def output(self, first, last, put, fields=range(STATE)):
        ext, mid, ready = self.sh.ext, self.sh.mid, 2 * HALO
        final, e_final = self.hist.at[SUBCYCLES - 1], self.ehist.at[SUBCYCLES - 1]
        lane = lane_ids()

        def output_row(f, r):
            k, h = (r, 0) if r < mid else (ext - 1 - r, HALF)
            v = row(self.edge, f, k) if k < ready else row(e_final, f, k - HALO)
            w, e = roll(v, -(h + HALO)), roll(v, LANES - HALO - (h + EAST0 + HALO))
            yield
            inner = ready <= r < ext - ready
            v = row(final, f, r - HALO) if inner else self.main_row(f, r)
            v = jnp.where(lane < HALO, w, jnp.where(lane >= LANES - HALO, e, v))
            put(f, r - HALO, v)

        run_staged([output_row(f, r) for f in fields for r in range(first, last)], 16)


def for_bands(sizes, n_lat, take):
    lat_size, _ = sizes
    lat = lax.axis_index("lat")
    lat_even = lax.rem(lat, 2) == 0
    lat_odd = jnp.logical_not(lat_even)
    at_top = lat == lat_size - 1
    pl.when(at_top)(lambda: take(None, True))
    pl.when(lat == 0)(lambda: take(None, False))
    pl.when(lat_even)(lambda: take(0, True))
    pl.when(lat_odd)(lambda: take(0, False))
    if n_lat == 2:
        pl.when(lat_odd & jnp.logical_not(at_top))(lambda: take(1, True))
        pl.when(lat_even & (lat > 0))(lambda: take(1, False))


def wedge_rows_kernel(sh, sizes, n_lat, *refs):
    bands, (own_ref, hist_ref, main, edge_out, order_out, begin, main_c) = (
        refs[:n_lat],
        refs[n_lat:],
    )
    wedges = Wedges(sh, own_ref, hist_ref, main=(main, begin, main_c))
    order_out[...] = jnp.zeros((SUBLANES, LANES), F32)

    def take(n, north):
        wedges.take_rows(None if n is None else bands[n], north)

    for_bands(sizes, n_lat, take)
    wedges.edge_own(edge_out)
    wedges.steps(("south", "north"))


def wedge_edges_kernel(sh, sizes, n_lat, *refs):
    corners, refs = refs[:n_lat], refs[n_lat:]
    hist_ref, main, edge_own, edges = refs[0], refs[1], refs[2], refs[3:6]
    (out_ref, order_out), kept, edge = refs[6:8], refs[8:11], refs[11:]
    wedges = Wedges(sh, None, hist_ref, edges, (main, None, None), edge)
    order_out[...] = jnp.zeros((SUBLANES, LANES), F32)
    for f in range(FIELDS):
        for k in range(HALO):
            put_row(edge[0], f, k, row(edge_own, f, k))

    for k in range(HALO + 1):
        at = slice(SUBLANES * k, SUBLANES * (k + 1))
        kept[1][at, :] = edges[1][at, :]
    for f in range(STATE):
        for k in range(2):
            put_row(kept[0], f, k, row(edges[0], f, k))
        for n in range(SUBCYCLES):
            for k in range(2 * n + 1, 2 * n + 4):
                put_row(kept[2].at[n], f, k, row(edges[2].at[n], f, k))

    def take(n, north):
        wedges.take_halos(None if n is None else corners[n], 0, north)

    for_bands(sizes, n_lat, take)
    wedges.edge_coefs()
    wedges.steps(("edges",))
    out_flat = flat_rows(out_ref)

    def put(f, r, value):
        out_flat[f, pl.ds(r, SUBLANES, stride=sh.height), :] = value

    wedges.output(HALO, sh.ext - HALO, put)


class Either:
    def __init__(self, mask, first, second):
        self.mask, self.first, self.second = mask, first, second

    def __getitem__(self, v):
        return jnp.where(self.mask, self.first[v], self.second[v])


def north_kernel(sh, sizes, got_ref, sent_ref, first_ref, order_ref, *outs):
    main, main_c, edge, edge_c = outs[:4]
    lat_size, lon_size = sizes

    @pl.when(lax.axis_index("lat") == lat_size - 1)
    def _():
        facing = lax.rem(first_ref[...] - lax.axis_index("lon") + lon_size, lon_size)
        itself = facing == lax.axis_index("lon")
        fold_ref = Either(itself, sent_ref, got_ref)
        wedges = Wedges(sh, main=(main, main, main_c), edge=(edge, edge_c))
        wedges.take_rows(fold_ref, True)
        wedges.edge_own(edge, north_only=True)
        wedges.take_halos(fold_ref, sh.main, True)
        wedges.edge_coefs()


def last_kernel(sh, sizes, *refs):
    lat_size, _ = sizes
    done_ref, state, begin = refs[0], refs[1:6], refs[6:10]
    out_hbm, late_ref, sems, main, edge = refs[10:]
    height, ext = sh.height, sh.ext
    split = (height - HALO) // SUBLANES * SUBLANES
    at_top = lax.axis_index("lat") == lat_size - 1
    lines = (pl.ds(0, split), pl.ds(split, height - split))

    def copies(source, part):
        return [
            pltpu.make_async_copy(
                source.at[f, :, lines[part]], out_hbm.at[f, :, lines[part]], sems.at[part, f]
            )
            for f in range(STATE)
        ]

    early = copies(done_ref, 0)
    for copy in early:
        copy.start()

    @pl.when(jnp.logical_not(at_top))
    def _():
        rest = copies(done_ref, 1)
        for copy in rest:
            copy.start()
        for copy in rest:
            copy.wait()

    @pl.when(at_top)
    def _():
        wedges = Wedges(
            sh, *state[:2], state[2:], (main, main, begin[1]), (edge, begin[3])
        )
        for f in range(STATE):
            for k in range(HALO):
                put_row(edge, f, k, row(begin[2], f, k))
                at = wedges.at(ext - 1 - k)
                put_row(main, f, at, row(begin[0], f, at))
        late_flat, done_flat = flat_rows(late_ref), flat_rows(done_ref)

        def put(f, r, value):
            late_flat[f, pl.ds(r, SUBLANES, stride=height), :] = value

        for f in range(STATE):
            for r in range(split, height - HALO):
                put(f, r, done_flat[f, pl.ds(r, SUBLANES, stride=height), :])
        wedges.steps(("edges", "north"))
        rest = copies(late_ref, 1)
        for f, copy in enumerate(rest):
            wedges.output(ext - 2 * HALO, ext - HALO, put, (f,))
            copy.start()
        for copy in rest:
            copy.wait()

    for copy in early:
        copy.wait()


def pair_swaps(size, wrap):
    first = [(i, i ^ 1) for i in range(size)]
    second = []
    for i in range(size):
        j = i + 1 if i % 2 else i - 1
        if wrap or 0 <= j < size:
            second.append((i, j % size))
    return first, second


def vmem(n):
    return [pl.BlockSpec(memory_space=pltpu.VMEM)] * n


def in_hbm(x):
    return pltpu.with_memory_space_constraint(x, pltpu.HBM)


def smem():
    return pl.BlockSpec(memory_space=pltpu.SMEM)


def on_device(mesh_sizes, perturb, background, land_mask, levels, fold_partner):
    lat_size, lon_size, dir_size = mesh_sizes
    height = perturb.shape[2]
    sh = Shapes(height)
    sizes = (lat_size, lon_size)
    flat = perturb.reshape(STATE, SUBLANES * height, LANES)
    tile = (SUBLANES, LANES)

    def shape(n):
        return pltpu.VMEM((n,) + tile, F32)

    params = pltpu.CompilerParams(vmem_limit_bytes=16 * 1024 * 1024)
    rows = SUBLANES * height
    n_lat = 1 if lat_size == 2 else 2
    side_a, side_b, own, *lat_out = pl.pallas_call(
        functools.partial(sides_kernel, sh, sizes),
        out_shape=(
            shape(sh.side),
            shape(sh.side),
            pltpu.VMEM((FIELDS, rows, LANES), F32),
        )
        + (shape(sh.main),) * n_lat,
        in_specs=[pl.BlockSpec(memory_space=pltpu.HBM)] * 4,
        out_specs=tuple(vmem(3 + n_lat)),
        scratch_shapes=[
            pltpu.VMEM(flat.shape, F32),
            pltpu.VMEM(background.shape, F32),
            pltpu.VMEM(land_mask.shape, jnp.int32),
            pltpu.VMEM(levels.shape, jnp.int32),
            pltpu.SemaphoreType.DMA((3 + STATE,)),
        ],
        compiler_params=params,
        name="sides",
    )(*[in_hbm(v) for v in (flat, background, land_mask, levels)])

    lon_swaps = pair_swaps(lon_size, True)
    got_a, got_b = [lax.ppermute(x, "lon", swap) for x, swap in zip((side_a, side_b), lon_swaps)]

    hist, place, first, branch = pl.pallas_call(
        functools.partial(middle_kernel, sh, sizes),
        out_shape=(
            pltpu.VMEM((SUBCYCLES, STATE, rows, LANES), F32),
            pltpu.VMEM(tile, jnp.int32),
            pltpu.VMEM(tile, jnp.int32),
            jax.ShapeDtypeStruct((1,), jnp.int32),
        ),
        in_specs=vmem(1) + [pl.BlockSpec(memory_space=pltpu.HBM)],
        out_specs=tuple(vmem(3)) + (smem(),),
        scratch_shapes=[
            pltpu.SMEM(fold_partner.shape, jnp.int32),
            pltpu.SemaphoreType.DMA,
        ],
        compiler_params=params,
        name="middle",
    )(own, in_hbm(fold_partner))
    lat_swaps = pair_swaps(lat_size, False)[:n_lat]
    got_lat = [lax.ppermute(x, "lat", swap) for x, swap in zip(lat_out, lat_swaps)]
    wedge_main, edge_own, order = pl.pallas_call(
        functools.partial(wedge_rows_kernel, sh, sizes, n_lat),
        out_shape=(
            pltpu.VMEM(Wedges.SHAPES[0], F32),
            pltpu.VMEM(Wedges.SHAPES[2], F32),
            pltpu.VMEM(tile, F32),
        ),
        in_specs=vmem(n_lat + 2),
        out_specs=tuple(vmem(3)),
        scratch_shapes=[pltpu.VMEM(x, F32) for x in Wedges.SHAPES[:2]],
        compiler_params=params,
        name="wedge_rows",
    )(*got_lat, own, hist)
    fold_band, *lat_corners = pl.pallas_call(
        functools.partial(bands_kernel, sh, sizes),
        out_shape=(shape(sh.band),) + (shape(sh.corners),) * n_lat,
        in_specs=vmem(5),
        out_specs=tuple(vmem(1 + n_lat)),
        compiler_params=params,
        name="bands",
    )(own, got_a, got_b, place, order)

    edge_rows = SUBLANES * (sh.mid - HALO)
    edge_shapes = (
        pltpu.VMEM((STATE, edge_rows, LANES), F32),
        pltpu.VMEM((edge_rows, LANES), F32),
        pltpu.VMEM((SUBCYCLES, STATE, edge_rows, LANES), F32),
    )
    step_edges = jax.jit(
        pl.pallas_call(
            functools.partial(edges_kernel, sh),
            out_shape=edge_shapes,
            in_specs=vmem(3),
            out_specs=tuple(vmem(3)),
            compiler_params=params,
            name="edges",
        )
    )
    step_wedge_edges = jax.jit(
        pl.pallas_call(
            functools.partial(wedge_edges_kernel, sh, sizes, n_lat),
            out_shape=(pltpu.VMEM(perturb.shape, F32), pltpu.VMEM(tile, F32)) + edge_shapes,
            in_specs=vmem(n_lat + 6),
            out_specs=tuple(vmem(5)),
            scratch_shapes=[pltpu.VMEM(x, F32) for x in Wedges.SHAPES[2:]],
            compiler_params=params,
            name="wedge_edges",
        )
    )
    take_north = jax.jit(
        pl.pallas_call(
            functools.partial(north_kernel, sh, sizes),
            out_shape=tuple(pltpu.VMEM(x, F32) for x in Wedges.SHAPES),
            in_specs=vmem(4),
            out_specs=tuple(vmem(4)),
            compiler_params=params,
            name="north",
        )
    )
    def rest(q, fold_band, lat_corners, wedge_main, edge_own, own, hist, got_a, got_b, first):
        across = []
        for m in range(lon_size):
            j = (q - m) % lon_size
            for a in range(lat_size):
                for d in range(dir_size):
                    source, target = (m, a, d), (j, a, d if j != m else d ^ 1)
                    across.append(
                        tuple((x * lat_size + y) * dir_size + z for x, y, z in (source, target))
                    )
        got_fold = lax.ppermute(fold_band, ("lon", "lat", "dir"), across)
        got_corners = [lax.ppermute(x, "lat", swap) for x, swap in zip(lat_corners, lat_swaps)]
        edges = step_edges(own, got_a, got_b)
        done, order, *kept = step_wedge_edges(*got_corners, hist, wedge_main, edge_own, *edges)
        return kept, done, take_north(got_fold, fold_band, first, order)

    edges, done, beyond = lax.switch(
        branch[0],
        [functools.partial(rest, q) for q in range(lon_size)],
        fold_band,
        lat_corners,
        wedge_main,
        edge_own,
        own,
        hist,
        got_a,
        got_b,
        first,
    )
    return pl.pallas_call(
        functools.partial(last_kernel, sh, sizes),
        out_shape=jax.ShapeDtypeStruct(perturb.shape, F32),
        in_specs=vmem(10),
        out_specs=pl.BlockSpec(memory_space=pltpu.HBM),
        scratch_shapes=[
            pltpu.VMEM(perturb.shape, F32),
            pltpu.SemaphoreType.DMA((2, STATE)),
            pltpu.VMEM(Wedges.SHAPES[0], F32),
            pltpu.VMEM(Wedges.SHAPES[2], F32),
        ],
        compiler_params=params,
        name="last",
    )(done, own, hist, *edges, *beyond)


def solution(mesh):
    placed = (
        P("grp", "dir", "lat", "lon"),
        P("grp", "lat", "lon"),
        P("lat", "lon"),
        P("lat", "lon"),
        P(),
    )
    sizes = tuple(mesh.shape[axis] for axis in ("lat", "lon", "dir"))
    return jax.shard_map(
        functools.partial(on_device, sizes),
        mesh=mesh,
        in_specs=placed,
        out_specs=P("grp", "dir", "lat", "lon"),
        check_vma=False,
    )
```
